256 devices in a mesh: section: 2 (over z_lo), tok: 4 (over z_hi), vocab: 32 (over x, y, core).
Axes of the slice: x: 4, y: 4, z: 8 (z_hi: 4, z_lo: 2; z = z_hi * 2 + z_lo), core: 2. Of those that a mesh axis runs over, the one named last changes fastest.
Arguments:
- hidden: bfloat16 [2, 256, 8192], P('section', 'tok', 'vocab'), may hold values from -40 to 40
- head: bfloat16 [2, 8192, 64128], P('section', None, ('tok', 'vocab')), may hold values from -1.0535376 to 1.0535376
- token_ids: int32 [256], replicated, may hold values from 0 to 64127
- loss_mask: int32 [256], replicated, may hold values 0 or 1
Outputs:
- head_grad: bfloat16 [8192, 64128], P('section', ('tok', 'vocab'))
- hidden_grad: bfloat16 [256, 8192], P('tok', ('section', 'vocab'))
The draws below stay inside these ranges and needn't reach their ends.
All inputs are finite; a program needn't handle non-finite values.
Results may differ from the reference program's by a relative error of at most 0.018.
Values may be sent and summed in bfloat16 or wider, within the bound.
No kernel may reach another device: no remote copies, remote signals or barrier semaphores. Data moves between devices by JAX's collectives and lax.ppermute only.
A program may use at most 128 MiB of HBM per device.

```python
import math
import jax
import jax.numpy as jnp
import numpy as np

D = 8192
V = 64128
TOKENS = 256


def draw_rows(key, lowest, highest):
    noise_key, scale_key = jax.random.split(key)
    noise = jnp.clip(jax.random.normal(noise_key, (2, TOKENS, D), jnp.float32), -4.0, 4.0)
    scales = jnp.exp(jax.random.uniform(scale_key, (2, TOKENS, 1), jnp.float32, math.log(lowest), math.log(highest)))
    return (noise * scales, scales)


def draw_hidden(key, part):
    states, scales = draw_rows(key, 0.5, 5.0)
    return states.astype(jnp.bfloat16)


def aligned_head(key, states, scales, aligned):
    base_key, column_key, row_pick, column_pick = jax.random.split(key, 4)
    normal_part = jnp.clip(jax.random.normal(base_key, (2, D, V), jnp.float32), -4.0, 4.0)
    column_scale = jnp.exp(jax.random.uniform(column_key, (1, 1, V), jnp.float32, math.log(0.5), math.log(5.0)))
    weights = normal_part * column_scale * (3.0 / math.sqrt(D))
    for number in range(aligned):
        row_index = jax.random.randint(jax.random.fold_in(row_pick, number), (), 0, TOKENS)
        column_index = jax.random.randint(jax.random.fold_in(column_pick, number), (), 0, V)
        partner = (column_index + V // 2) % V
        target = 120.0 + 40.0 * number
        for slot in range(2):
            factor = scales[slot, row_index, 0]
            vector = states[slot, row_index] / (D * factor * factor)
            weights = weights.at[slot, :, column_index].set(target * vector)
            weights = weights.at[slot, :, partner].set((target - 2.0) * vector)
    return weights


def draw_head(key, part):
    states, scales = draw_rows(key, 0.5, 5.0)
    weights = aligned_head(jax.random.fold_in(key, 7), states, scales, 0)
    return weights.astype(jnp.bfloat16)


def place_ends(values, own_key, low, largest):
    dims = values.shape
    index_at = [jax.random.randint(jax.random.fold_in(own_key, axis), (), 0, dims[axis]) for axis in range(len(dims))]
    values = values.at[tuple(index_at)].set(low)
    longest = dims.index(max(dims))
    index_at[longest] = (index_at[longest] + 1) % dims[longest]
    return values.at[tuple(index_at)].set(largest)


def rank_bounds(number_of, slope):
    weights = [(1 << 20) // math.isqrt(standing ** slope) + 1 for standing in range(1, number_of + 1)]
    spread = 1 + sum(weights) // (1 << 30)
    return np.cumsum(np.array([max(1, weight // spread) for weight in weights]))


def skewed_ids(rng, shape, number_of, slope):
    listing = rank_bounds(number_of, slope)
    ticket = jax.random.randint(jax.random.fold_in(rng, 1), shape, 0, int(listing[number_of - 1]))
    rank = jnp.searchsorted(jnp.asarray(listing, jnp.int32), ticket, side="right")
    return jax.random.permutation(jax.random.fold_in(rng, 2), number_of)[rank].astype(jnp.int32)


def setup_inputs(seed: int = 0) -> dict:
    key_of = jax.random.split(jax.random.key(seed), 5)
    return {
        "hidden": draw_hidden(jax.random.fold_in(key_of[4], 71), 0),
        "head": draw_head(jax.random.fold_in(key_of[4], 71), 0),
        "token_ids": place_ends(skewed_ids(key_of[2], (TOKENS,), V, 2), jax.random.fold_in(key_of[2], 3), 0, V - 1).astype(jnp.int32),
        "loss_mask": place_ends((jax.random.randint(key_of[3], (TOKENS,), 0, 4) < 3).astype(jnp.int32), jax.random.fold_in(key_of[3], 1), 0, 1),
    }


def softmax_parts(logits):
    peak = jnp.max(logits, axis=1, keepdims=True)
    shifted = logits - peak
    scaled = jnp.exp(shifted)
    total = jnp.sum(scaled, axis=1, keepdims=True)
    moment = jnp.sum(scaled * shifted, axis=1, keepdims=True)
    log_probs = shifted - jnp.log(total)
    entropy = jnp.log(total) - moment / total
    return log_probs, entropy


def reference(hidden, head, token_ids, loss_mask):
    teacher_logits = jnp.dot(hidden[0], head[0], preferred_element_type=jnp.float32)
    student_logits = jnp.dot(hidden[1], head[1], preferred_element_type=jnp.float32)
    teacher_logp, teacher_entropy = softmax_parts(teacher_logits)
    student_logp, unused_entropy = softmax_parts(student_logits)
    columns = jnp.arange(V, dtype=jnp.int32)
    onehot = (token_ids[:, None] == columns[None, :]).astype(jnp.float32)
    weight = loss_mask.astype(jnp.float32)[:, None]
    student_probs = jnp.exp(student_logp)
    grad_logits = weight * (teacher_entropy * (student_probs - jnp.exp(teacher_logp)) + student_probs - onehot)
    grad_logits = grad_logits.astype(jnp.bfloat16)
    head_grad = jnp.dot(hidden[1].T, grad_logits, preferred_element_type=jnp.float32).astype(jnp.bfloat16)
    hidden_grad = jnp.dot(grad_logits, head[1].T, preferred_element_type=jnp.float32).astype(jnp.bfloat16)
    return head_grad, hidden_grad
```

```python
import functools
import jax
import jax.numpy as jnp
from jax import lax
from jax.experimental import pallas as pl
from jax.experimental.pallas import tpu as pltpu
from jax.sharding import PartitionSpec as P

AXES = ("section", "tok", "vocab")
SIZES = {"s": 2, "t": 4, "x": 4, "y": 4, "c": 2}
MIB = 1024 * 1024


def route(only=None, **shift):
    names = list(SIZES)
    pairs = []
    for device in range(256):
        place, rest = {}, device
        for name in reversed(names):
            rest, place[name] = divmod(rest, SIZES[name])
        if only is not None and place["s"] != only:
            continue
        target = 0
        for name in names:
            target = target * SIZES[name] + (place[name] + shift.get(name, 0)) % SIZES[name]
        pairs.append((device, target))
    return pairs


def send(block, only=None, **shift):
    return lax.ppermute(block, AXES, route(only, **shift))


def params(mib):
    return pltpu.CompilerParams(vmem_limit_bytes=mib * MIB)


VMEM = pl.BlockSpec(memory_space=pltpu.VMEM)
SMEM = pl.BlockSpec(memory_space=pltpu.SMEM)


def order_rows_kernel(place_ref, r0, r1, r2, r3, top_ref, low_ref, rows_ref):
    tok = place_ref[1]
    block = r0.shape[0]
    for d, ref in enumerate((r0, r1, r2, r3)):
        rows_ref[pl.ds(pl.multiple_of((tok + 4 - d) % 4 * block, block), block), :] = ref[...]
    top_ref[...] = rows_ref[: 2 * block]
    low_ref[...] = rows_ref[2 * block :]


def order_rows(place, blocks):
    block, wide = blocks[0].shape
    half = jax.ShapeDtypeStruct((2 * block, wide), blocks[0].dtype)
    return pl.pallas_call(
        order_rows_kernel,
        out_shape=[half, half],
        in_specs=[SMEM] + [VMEM] * 4,
        out_specs=[VMEM, VMEM],
        scratch_shapes=[pltpu.VMEM((4 * block, wide), blocks[0].dtype)],
    )(place, *blocks)


def logits_kernel(place_ref, head_ref, *refs):
    own_a, own_b, other_a, other_b = (refs[4 * i : 4 * i + 4] for i in range(4))
    hidden_ref, scaled_ref, short_ref, stats_ref, acc_ref = refs[16:]
    step = pl.program_id(0)
    y, c = place_ref[3], place_ref[4]
    chunk = own_a[0].shape[2]
    half = own_a[0].shape[1]
    for dy in range(4):
        y_at = (y + 4 - dy) % 4
        for core, a, b in ((c, own_a, own_b), (1 - c, other_a, other_b)):
            columns = pl.ds(pl.multiple_of((y_at * 2 + core) * chunk, chunk), chunk)
            hidden_ref[0, :half, columns] = a[dy][step]
            for dx in range(4):
                @pl.when(step == dx)
                def _():
                    hidden_ref[0, half:, columns] = b[dx][dy]
    part = lax.dot_general(
        head_ref[...], hidden_ref[0], (((1,), (1,)), ((), ())), preferred_element_type=jnp.float32
    )

    @pl.when(step == 0)
    def _():
        acc_ref[...] = part

    @pl.when(step > 0)
    def _():
        acc_ref[...] += part

    @pl.when(step == 3)
    def _():
        logits = acc_ref[...]
        peak = jnp.max(logits, axis=0, keepdims=True)
        shifted = logits - peak
        scaled = jnp.exp(shifted)
        scaled_ref[...] = scaled
        short_ref[...] = scaled.astype(jnp.bfloat16)
        stats_ref[0:1] = peak
        stats_ref[1:2] = jnp.sum(scaled, axis=0, keepdims=True)
        stats_ref[2:3] = jnp.sum(scaled * shifted, axis=0, keepdims=True)
        stats_ref[3:8] = jnp.zeros((5, peak.shape[1]), jnp.float32)


def logits_parts(place, head_t, own_a, own_b, other_a, other_b):
    width, features = head_t.shape
    _, half, chunk = own_a[0].shape
    toks = 2 * half
    block = features // 4

    def fixed(step, place):
        return (0, 0)

    piece = pl.BlockSpec((4, half, chunk), lambda step, place: (0, 0, 0))
    return pl.pallas_call(
        logits_kernel,
        grid_spec=pltpu.PrefetchScalarGridSpec(
            num_scalar_prefetch=1,
            grid=(4,),
            in_specs=[pl.BlockSpec((width, block), lambda step, place: (0, (place[2] + 4 - step) % 4))]
            + [piece] * 16,
            out_specs=[
                pl.BlockSpec((1, toks, block), lambda step, place: ((place[2] + 4 - step) % 4, 0, 0)),
                pl.BlockSpec((width, toks), fixed),
                pl.BlockSpec((width, toks), fixed),
                pl.BlockSpec((8, toks), fixed),
            ],
            scratch_shapes=[pltpu.VMEM((width, toks), jnp.float32)],
        ),
        out_shape=[
            jax.ShapeDtypeStruct((4, toks, block), jnp.bfloat16),
            jax.ShapeDtypeStruct((width, toks), jnp.float32),
            jax.ShapeDtypeStruct((width, toks), jnp.bfloat16),
            jax.ShapeDtypeStruct((8, toks), jnp.float32),
        ],
        compiler_params=params(32),
    )(place, head_t, *own_a, *own_b, *other_a, *other_b)


def merge_kernel(*refs):
    *ins, out_ref = refs
    peak = ins[0][0:1]
    for ref in ins[1:]:
        peak = jnp.maximum(peak, ref[0:1])
    total = jnp.zeros_like(peak)
    moment = jnp.zeros_like(peak)
    for ref in ins:
        drop = ref[0:1] - peak
        factor = jnp.exp(drop)
        total += factor * ref[1:2]
        moment += factor * (ref[2:3] + drop * ref[1:2])
    out_ref[0:1] = peak
    out_ref[1:2] = total
    out_ref[2:3] = moment
    out_ref[3:8] = jnp.zeros((5, peak.shape[1]), jnp.float32)


def merge(*stats):
    return pl.pallas_call(
        merge_kernel,
        out_shape=jax.ShapeDtypeStruct(stats[0].shape, jnp.float32),
        in_specs=[VMEM] * len(stats),
        out_specs=VMEM,
    )(*stats)


def scale_kernel(local_ref, *refs):
    *ins, out_ref = refs
    peak = ins[0][0:1]
    for ref in ins[1:]:
        peak = jnp.maximum(peak, ref[0:1])
    total = jnp.zeros_like(peak)
    moment = jnp.zeros_like(peak)
    for ref in ins:
        drop = ref[0:1] - peak
        factor = jnp.exp(drop)
        total += factor * ref[1:2]
        moment += factor * (ref[2:3] + drop * ref[1:2])
    out_ref[0:1] = jnp.exp(local_ref[0:1] - peak) / total
    out_ref[1:2] = jnp.log(total) - moment / total
    out_ref[2:8] = jnp.zeros((6, peak.shape[1]), jnp.float32)


def local_scale(local, *stats):
    return pl.pallas_call(
        scale_kernel,
        out_shape=jax.ShapeDtypeStruct(local.shape, jnp.float32),
        in_specs=[VMEM] * (1 + len(stats)),
        out_specs=VMEM,
    )(local, *stats)


def hidden_grad_kernel(place_ref, own_ref, other_ref, own_stats, other_stats, ids_ref, mask_ref, head_ref, *refs):
    keep_a, keep_b, give_a, give_b = (refs[4 * i : 4 * i + 4] for i in range(4))
    grad_ref, turned_ref, wide_ref = refs[16:]
    step = pl.program_id(0)
    y, c = place_ref[3], place_ref[4]

    @pl.when(step == 0)
    def _():
        teacher = place_ref[0] == 0
        mask = mask_ref[...].astype(jnp.float32)
        entropy = jnp.where(teacher, own_stats[1:2], other_stats[1:2])
        by_own = jnp.where(teacher, -entropy, entropy + 1.0) * own_stats[0:1] * mask
        by_other = jnp.where(teacher, entropy + 1.0, -entropy) * other_stats[0:1] * mask
        width = own_ref.shape[0]
        first = ((place_ref[1] * 4 + place_ref[2]) * 8 + y * 2 + c) * width
        entries = lax.broadcasted_iota(jnp.int32, own_ref.shape, 0) + first
        onehot = jnp.where(entries == ids_ref[...], mask, 0.0)
        grad = by_own * own_ref[...] + by_other * other_ref[...].astype(jnp.float32) - onehot
        grad_ref[...] = grad.astype(jnp.bfloat16)
        turned_ref[...] = grad.T.astype(jnp.bfloat16)

    wide_ref[...] = jnp.dot(
        turned_ref[...], head_ref[...], preferred_element_type=jnp.float32
    ).astype(jnp.bfloat16)
    for dy in range(4):
        y_at = (y + dy) % 4
        for core, a, b in ((c, keep_a, keep_b), (1 - c, give_a, give_b)):
            columns = pl.ds(pl.multiple_of((y_at * 2 + core) * 128, 128), 128)
            for dx in range(4):
                @pl.when(step == dx)
                def _():
                    a[dx][dy] = wide_ref[:, columns]

            @pl.when(step >= 4)
            def _():
                b[dy][step - 4] = wide_ref[:, columns]


def hidden_grad_parts(place, own, other, own_stats, other_stats, ids, mask, head_t):
    width, features = head_t.shape
    toks = own.shape[1]
    block = features // 8

    def fixed(step, place):
        return (0, 0)

    piece = pl.BlockSpec((4, toks, 128), lambda step, place: (0, 0, 0))
    outs = pl.pallas_call(
        hidden_grad_kernel,
        grid_spec=pltpu.PrefetchScalarGridSpec(
            num_scalar_prefetch=1,
            grid=(8,),
            in_specs=[
                pl.BlockSpec((width, toks), fixed),
                pl.BlockSpec((width, toks), fixed),
                pl.BlockSpec((8, toks), fixed),
                pl.BlockSpec((8, toks), fixed),
                pl.BlockSpec((1, toks), fixed),
                pl.BlockSpec((1, toks), fixed),
                pl.BlockSpec(
                    (width, block), lambda step, place: (0, step // 4 * 4 + (place[2] + step % 4) % 4)
                ),
            ],
            out_specs=[piece] * 16 + [pl.BlockSpec((width, toks), fixed)],
            scratch_shapes=[
                pltpu.VMEM((toks, width), jnp.bfloat16),
                pltpu.VMEM((toks, block), jnp.bfloat16),
            ],
        ),
        out_shape=[jax.ShapeDtypeStruct((4, toks, 128), jnp.bfloat16)] * 16
        + [jax.ShapeDtypeStruct((width, toks), jnp.bfloat16)],
        compiler_params=params(32),
    )(place, own, other, own_stats, other_stats, ids, mask, head_t)
    return outs[0:4], outs[4:8], outs[8:12], outs[12:16], outs[16]


def add_kernel(*refs):
    *ins, out_ref = refs
    total = ins[0][...].astype(jnp.float32)
    for ref in ins[1:]:
        total += ref[...].astype(jnp.float32)
    out_ref[...] = total.astype(out_ref.dtype)


def add(*blocks):
    return pl.pallas_call(
        add_kernel,
        out_shape=jax.ShapeDtypeStruct(blocks[0].shape, blocks[0].dtype),
        in_specs=[VMEM] * len(blocks),
        out_specs=VMEM,
    )(*blocks)


def add_split_kernel(*refs):
    ins, outs = refs[:4], refs[4:]
    for d, out_ref in enumerate(outs):
        total = ins[0][d].astype(jnp.float32)
        for ref in ins[1:]:
            total += ref[d].astype(jnp.float32)
        out_ref[...] = total.astype(out_ref.dtype)


def add_split(*blocks):
    return pl.pallas_call(
        add_split_kernel,
        out_shape=[jax.ShapeDtypeStruct(blocks[0].shape[1:], blocks[0].dtype)] * 4,
        in_specs=[VMEM] * 4,
        out_specs=[VMEM] * 4,
    )(*blocks)


def add_rows_kernel(place_ref, *refs):
    ins_a, ins_b, outs, sum_ref = refs[:4], refs[4:8], refs[8:12], refs[12]
    tok = place_ref[1]
    for half, ins in enumerate((ins_a, ins_b)):
        total = ins[0][...].astype(jnp.float32)
        for ref in ins[1:]:
            total += ref[...].astype(jnp.float32)
        sum_ref[:, 128 * half : 128 * half + 128] = total.astype(sum_ref.dtype)
    block = outs[0].shape[0]
    for d, out_ref in enumerate(outs):
        out_ref[...] = sum_ref[pl.ds(pl.multiple_of((tok + d) % 4 * block, block), block), :]


def add_rows(place, blocks_a, blocks_b):
    toks = blocks_a[0].shape[0]
    return pl.pallas_call(
        add_rows_kernel,
        out_shape=[jax.ShapeDtypeStruct((toks // 4, 256), jnp.bfloat16)] * 4,
        in_specs=[SMEM] + [VMEM] * 8,
        out_specs=[VMEM] * 4,
        scratch_shapes=[pltpu.VMEM((toks, 256), jnp.bfloat16)],
    )(place, *blocks_a, *blocks_b)


def head_grad_kernel(place_ref, grad_ref, own_ref, sent_ref, out_ref):
    teacher = place_ref[0] == 0
    for flag, ref in ((teacher, sent_ref), (jnp.logical_not(teacher), own_ref)):
        @pl.when(flag)
        def _():
            out_ref[...] = jnp.dot(
                grad_ref[...], ref[0], preferred_element_type=jnp.float32
            ).astype(jnp.bfloat16)


def head_grad_half(place, grad, hidden, sent):
    width, toks = grad.shape
    block = hidden.shape[2] // 2
    return pl.pallas_call(
        head_grad_kernel,
        grid_spec=pltpu.PrefetchScalarGridSpec(
            num_scalar_prefetch=1,
            grid=(4,),
            in_specs=[
                pl.BlockSpec((width, toks), lambda step, place: (0, 0)),
                pl.BlockSpec((1, toks, block), lambda step, place: (2 + step // 2, 0, step % 2)),
                pl.BlockSpec((1, toks, block), lambda step, place: (step // 2, 0, step % 2)),
            ],
            out_specs=pl.BlockSpec((width, block), lambda step, place: (0, step)),
        ),
        out_shape=jax.ShapeDtypeStruct((width, 4 * block), jnp.bfloat16),
        compiler_params=params(32),
    )(place, grad, hidden, sent)


def on_device(hidden, head, token_ids, loss_mask):
    section, tok, vocab = (lax.axis_index(name) for name in AXES)
    place = jnp.stack([section, tok, vocab // 8, vocab // 2 % 4, vocab % 2]).astype(jnp.int32)
    core = vocab % 2
    head_t = head[0].T
    states = hidden[0]

    with jax.named_scope("gather_tok"):
        top, low = order_rows(place, [states] + [send(states, t=d) for d in (1, 2, 3)])
    with jax.named_scope("gather_first"):
        top = jnp.stack([top] + [send(top, x=d) for d in (1, 2, 3)])
        low = jnp.stack([low] + [send(low, y=d) for d in (1, 2, 3)])
    with jax.named_scope("gather_second"):
        own_a = [top] + [send(top, y=d) for d in (1, 2, 3)]
        own_b = [low] + [send(low, x=d) for d in (1, 2, 3)]
    with jax.named_scope("gather_cores"):
        other_a = [send(block, c=1) for block in own_a]
        other_b = [send(block, c=1) for block in own_b]
    with jax.named_scope("logits"):
        gathered, scaled, short, local = logits_parts(place, head_t, own_a, own_b, other_a, other_b)

    with jax.named_scope("exchange_scaled"):
        other_short = send(short, s=1)
    with jax.named_scope("student_hidden"):
        mine = lax.dynamic_index_in_dim(gathered, core, 0, keepdims=False)
        sent = send(mine, only=1, s=1)
        twin = send(sent, only=0, c=1)
        sent = jnp.where(core == 0, jnp.stack([sent, twin]), jnp.stack([twin, sent]))

    with jax.named_scope("stats"):
        stats = merge(local, send(local, c=1))
        stats = merge(stats, *[send(stats, x=d) for d in (1, 2, 3)])
        stats = merge(stats, *[send(stats, y=d) for d in (1, 2, 3)])
        own_stats = local_scale(local, stats, *[send(stats, t=d) for d in (1, 2, 3)])
        other_stats = send(own_stats, s=1)

    with jax.named_scope("hidden_grad"):
        keep_a, keep_b, give_a, give_b, grad = hidden_grad_parts(
            place, scaled, other_short, own_stats, other_stats, token_ids[None], loss_mask[None], head_t
        )
    with jax.named_scope("reduce_cores"):
        sum_a = [add(k, send(g, c=1)) for k, g in zip(keep_a, give_a)]
        sum_b = [add(k, send(g, c=1)) for k, g in zip(keep_b, give_b)]
    with jax.named_scope("reduce_first"):
        parts_a = add_split(sum_a[0], *[send(sum_a[d], x=d) for d in (1, 2, 3)])
        parts_b = add_split(sum_b[0], *[send(sum_b[d], y=d) for d in (1, 2, 3)])
    with jax.named_scope("reduce_second"):
        rows = add_rows(
            place,
            [parts_a[0]] + [send(parts_a[d], y=d) for d in (1, 2, 3)],
            [parts_b[0]] + [send(parts_b[d], x=d) for d in (1, 2, 3)],
        )
    with jax.named_scope("reduce_tok"):
        reduced = add(rows[0], *[send(rows[d], t=d) for d in (1, 2, 3)])
    with jax.named_scope("hidden_out"):
        sent_hidden = send(reduced[:, :128], only=1, s=1)
        hidden_out = jnp.where(section == 0, sent_hidden, reduced[:, 128:])
    with jax.named_scope("head_grad"):
        head_out = head_grad_half(place, grad, gathered, sent).T
    return head_out, hidden_out


def solution(mesh):
    in_specs = (P("section", "tok", "vocab"), P("section", None, ("tok", "vocab")), P(), P())
    out_specs = (P("section", ("tok", "vocab")), P("tok", ("section", "vocab")))
    return jax.shard_map(
        on_device, mesh=mesh, in_specs=in_specs, out_specs=out_specs, check_vma=False
    )
```

```python
import jax
import jax.numpy as jnp
from jax import lax
from jax.experimental import pallas as pl
from jax.experimental.pallas import tpu as pltpu
from jax.sharding import PartitionSpec as P

AXES = ("section", "tok", "vocab")
SIZES = {"s": 2, "t": 4, "x": 4, "y": 4, "c": 2}
MIB = 1024 * 1024


def route(only, even, odd):
    names = list(SIZES)
    pairs = []
    for device in range(256):
        place, rest = {}, device
        for name in reversed(names):
            rest, place[name] = divmod(rest, SIZES[name])
        if only is not None and place["s"] != only:
            continue
        shift = odd if place["c"] else even
        if shift is None:
            continue
        target = 0
        for name in names:
            target = target * SIZES[name] + (place[name] + shift.get(name, 0)) % SIZES[name]
        pairs.append((device, target))
    return pairs


def send(block, only=None, **shift):
    return lax.ppermute(block, AXES, route(only, shift, shift))


def send_by_core(block, even, odd, only=None):
    return lax.ppermute(block, AXES, route(only, even, odd))


def params(mib):
    return pltpu.CompilerParams(vmem_limit_bytes=mib * MIB)


VMEM = pl.BlockSpec(memory_space=pltpu.VMEM)


def logits_kernel(place_ref, head_ref, *refs):
    own, other = refs[:4], refs[4:8]
    hidden_ref, half_ref, scaled_ref, short_ref, stats_ref, acc_ref = refs[8:]
    step = pl.program_id(0)
    tok, x, y, c = place_ref[1], place_ref[2], place_ref[3], place_ref[4]
    _, _, rows, chunk = own[0].shape

    def lay(columns, piece):
        for dt in range(4):
            at = pl.ds(pl.multiple_of((tok + 4 - dt) % 4 * rows, rows), rows)
            hidden_ref[0, at, columns] = piece(dt)

    for dy in range(4):
        y_at = (y + 4 - dy) % 4
        for core, blocks in ((c, own), (1 - c, other)):
            columns = pl.ds(pl.multiple_of((y_at * 2 + core) * chunk, chunk), chunk)

            @pl.when(core == 0)
            def _():
                lay(columns, lambda dt: blocks[dy][step, dt])

            for dx in range(4):
                @pl.when(jnp.logical_and(core == 1, step == dx))
                def _():
                    lay(columns, lambda dt: blocks[dx][dy, dt])

    @pl.when((x + 4 - step) % 4 == c)
    def _():
        half_ref[...] = hidden_ref[0]

    part = lax.dot_general(
        head_ref[...], hidden_ref[0], (((1,), (1,)), ((), ())), preferred_element_type=jnp.float32
    )

    @pl.when(step == 0)
    def _():
        acc_ref[...] = part

    @pl.when(step > 0)
    def _():
        acc_ref[...] += part

    @pl.when(step == 3)
    def _():
        logits = acc_ref[...]
        peak = jnp.max(logits, axis=0, keepdims=True)
        shifted = logits - peak
        scaled = jnp.exp(shifted)
        scaled_ref[...] = scaled
        short_ref[...] = scaled.astype(jnp.bfloat16)
        stats_ref[0:1] = peak
        stats_ref[1:2] = jnp.sum(scaled, axis=0, keepdims=True)
        stats_ref[2:3] = jnp.sum(scaled * shifted, axis=0, keepdims=True)
        stats_ref[3:8] = jnp.zeros((5, peak.shape[1]), jnp.float32)


def logits_parts(place, head_t, own, other):
    width, features = head_t.shape
    toks = 4 * own[0].shape[2]
    block = features // 4

    def fixed(step, place):
        return (0, 0)

    piece = pl.BlockSpec(own[0].shape, lambda step, place: (0, 0, 0, 0))
    return pl.pallas_call(
        logits_kernel,
        grid_spec=pltpu.PrefetchScalarGridSpec(
            num_scalar_prefetch=1,
            grid=(4,),
            in_specs=[pl.BlockSpec((width, block), lambda step, place: (0, (place[2] + 4 - step) % 4))]
            + [piece] * 8,
            out_specs=[
                pl.BlockSpec((1, toks, block), lambda step, place: ((place[2] + 4 - step) % 4, 0, 0)),
                pl.BlockSpec((toks, block), fixed),
                pl.BlockSpec((width, toks), fixed),
                pl.BlockSpec((width, toks), fixed),
                pl.BlockSpec((8, toks), fixed),
            ],
            scratch_shapes=[pltpu.VMEM((width, toks), jnp.float32)],
        ),
        out_shape=[
            jax.ShapeDtypeStruct((4, toks, block), jnp.bfloat16),
            jax.ShapeDtypeStruct((toks, block), jnp.bfloat16),
            jax.ShapeDtypeStruct((width, toks), jnp.float32),
            jax.ShapeDtypeStruct((width, toks), jnp.bfloat16),
            jax.ShapeDtypeStruct((8, toks), jnp.float32),
        ],
        compiler_params=params(26),
    )(place, head_t, *own, *other)


def merge_kernel(*refs):
    *ins, out_ref = refs
    peak = ins[0][0:1]
    for ref in ins[1:]:
        peak = jnp.maximum(peak, ref[0:1])
    total = jnp.zeros_like(peak)
    moment = jnp.zeros_like(peak)
    for ref in ins:
        drop = ref[0:1] - peak
        factor = jnp.exp(drop)
        total += factor * ref[1:2]
        moment += factor * (ref[2:3] + drop * ref[1:2])
    out_ref[0:1] = peak
    out_ref[1:2] = total
    out_ref[2:3] = moment
    out_ref[3:8] = jnp.zeros((5, peak.shape[1]), jnp.float32)


def merge(*stats):
    return pl.pallas_call(
        merge_kernel,
        out_shape=jax.ShapeDtypeStruct(stats[0].shape, jnp.float32),
        in_specs=[VMEM] * len(stats),
        out_specs=VMEM,
        compiler_params=params(1),
    )(*stats)


def scale_kernel(local_ref, *refs):
    *ins, out_ref = refs
    peak = ins[0][0:1]
    for ref in ins[1:]:
        peak = jnp.maximum(peak, ref[0:1])
    total = jnp.zeros_like(peak)
    moment = jnp.zeros_like(peak)
    for ref in ins:
        drop = ref[0:1] - peak
        factor = jnp.exp(drop)
        total += factor * ref[1:2]
        moment += factor * (ref[2:3] + drop * ref[1:2])
    out_ref[0:1] = jnp.exp(local_ref[0:1] - peak) / total
    out_ref[1:2] = jnp.log(total) - moment / total
    out_ref[2:8] = jnp.zeros((6, peak.shape[1]), jnp.float32)


def local_scale(local, *stats):
    return pl.pallas_call(
        scale_kernel,
        out_shape=jax.ShapeDtypeStruct(local.shape, jnp.float32),
        in_specs=[VMEM] * (1 + len(stats)),
        out_specs=VMEM,
        compiler_params=params(1),
    )(local, *stats)


def piece_products(turned_ref, head_refs, out_refs, add_refs=None):
    step = pl.program_id(0)
    for d in range(4):
        @pl.when(step == d)
        def _():
            for e in range(4):
                part = jnp.dot(turned_ref[...], head_refs[e][...], preferred_element_type=jnp.float32)
                if add_refs is not None:
                    part += add_refs[d][e].astype(jnp.float32)
                out_refs[d][e] = part.astype(jnp.bfloat16)


def piece_specs(width, twin):
    def spec(e):
        def index(d, place):
            x, y, c = place[2], place[3], place[4]
            mixed = c == 0
            at_x = (x + jnp.where(mixed, d, e)) % 4
            at_y = (y + jnp.where(mixed, e, d)) % 4
            return (0, c * 16 + at_x * 4 + at_y)

        def twin_index(d, place):
            x, y, c = place[2], place[3], 1 - place[4]
            mixed = c == 0
            at_x = (x + jnp.where(mixed, d, e)) % 4
            at_y = (y + jnp.where(mixed, e, d)) % 4
            return (0, c * 16 + at_x * 4 + at_y)

        return pl.BlockSpec((width, 256), twin_index if twin else index)

    return [spec(e) for e in range(4)]


def give_kernel(place_ref, own_ref, other_ref, own_stats, other_stats, ids_ref, mask_ref, *refs):
    heads, outs, grad_ref, turned_ref = refs[:4], refs[4:8], refs[8], refs[9]

    @pl.when(pl.program_id(0) == 0)
    def _():
        teacher = place_ref[0] == 0
        mask = mask_ref[...].astype(jnp.float32)
        entropy = jnp.where(teacher, own_stats[1:2], other_stats[1:2])
        by_own = jnp.where(teacher, -entropy, entropy + 1.0) * own_stats[0:1] * mask
        by_other = jnp.where(teacher, entropy + 1.0, -entropy) * other_stats[0:1] * mask
        width = own_ref.shape[0]
        first = ((place_ref[1] * 4 + place_ref[2]) * 8 + place_ref[3] * 2 + place_ref[4]) * width
        entries = lax.broadcasted_iota(jnp.int32, own_ref.shape, 0) + first
        onehot = jnp.where(entries == ids_ref[...], mask, 0.0)
        grad = by_own * own_ref[...] + by_other * other_ref[...].astype(jnp.float32) - onehot
        grad_ref[...] = grad.astype(jnp.bfloat16)
        turned_ref[...] = grad.T.astype(jnp.bfloat16)

    piece_products(turned_ref, heads, outs)


def give_parts(place, own, other, own_stats, other_stats, ids, mask, head_t):
    width, features = head_t.shape
    toks = own.shape[1]

    def fixed(d, place):
        return (0, 0)

    share = (4, toks, 256)
    outs = pl.pallas_call(
        give_kernel,
        grid_spec=pltpu.PrefetchScalarGridSpec(
            num_scalar_prefetch=1,
            grid=(4,),
            in_specs=[
                pl.BlockSpec((width, toks), fixed),
                pl.BlockSpec((width, toks), fixed),
                pl.BlockSpec((8, toks), fixed),
                pl.BlockSpec((8, toks), fixed),
                pl.BlockSpec((1, toks), fixed),
                pl.BlockSpec((1, toks), fixed),
            ]
            + piece_specs(width, True),
            out_specs=[pl.BlockSpec(share, lambda d, place: (0, 0, 0))] * 4
            + [pl.BlockSpec((width, toks), fixed), pl.BlockSpec((toks, width), fixed)],
        ),
        out_shape=[jax.ShapeDtypeStruct(share, jnp.bfloat16)] * 4
        + [
            jax.ShapeDtypeStruct((width, toks), jnp.bfloat16),
            jax.ShapeDtypeStruct((toks, width), jnp.bfloat16),
        ],
        compiler_params=params(12),
    )(place, own, other, own_stats, other_stats, ids, mask, *[head_t] * 4)
    return outs[:4], outs[4], outs[5]


def keep_kernel(place_ref, turned_ref, *refs):
    piece_products(turned_ref, refs[:4], refs[8:12], refs[4:8])


def keep_parts(place, turned, head_t, received):
    width, features = head_t.shape
    share = received[0].shape
    whole = pl.BlockSpec(share, lambda d, place: (0, 0, 0))
    return pl.pallas_call(
        keep_kernel,
        grid_spec=pltpu.PrefetchScalarGridSpec(
            num_scalar_prefetch=1,
            grid=(4,),
            in_specs=[pl.BlockSpec(turned.shape, lambda d, place: (0, 0))]
            + piece_specs(width, False)
            + [whole] * 4,
            out_specs=[whole] * 4,
        ),
        out_shape=[jax.ShapeDtypeStruct(share, jnp.bfloat16)] * 4,
        compiler_params=params(14),
    )(place, turned, *[head_t] * 4, *received)


def add_split_kernel(*refs):
    ins, outs = refs[:4], refs[4:]
    for d, out_ref in enumerate(outs):
        total = ins[0][d].astype(jnp.float32)
        for ref in ins[1:]:
            total += ref[d].astype(jnp.float32)
        out_ref[...] = total.astype(out_ref.dtype)


def add_split(*blocks):
    return pl.pallas_call(
        add_split_kernel,
        out_shape=[jax.ShapeDtypeStruct(blocks[0].shape[1:], blocks[0].dtype)] * 4,
        in_specs=[VMEM] * 4,
        out_specs=[VMEM] * 4,
        compiler_params=params(6),
    )(*blocks)


def add_rows_kernel(place_ref, *refs):
    ins, outs, sum_ref = refs[:4], refs[4:8], refs[8]
    tok = place_ref[1]
    total = ins[0][...].astype(jnp.float32)
    for ref in ins[1:]:
        total += ref[...].astype(jnp.float32)
    sum_ref[...] = total.astype(sum_ref.dtype)
    block = outs[0].shape[0]
    for d, out_ref in enumerate(outs):
        out_ref[...] = sum_ref[pl.ds(pl.multiple_of((tok + d) % 4 * block, block), block), :]


def add_rows(place, blocks):
    toks, wide = blocks[0].shape
    return pl.pallas_call(
        add_rows_kernel,
        out_shape=[jax.ShapeDtypeStruct((toks // 4, wide), jnp.bfloat16)] * 4,
        in_specs=[pl.BlockSpec(memory_space=pltpu.SMEM)] + [VMEM] * 4,
        out_specs=[VMEM] * 4,
        scratch_shapes=[pltpu.VMEM((toks, wide), jnp.bfloat16)],
        compiler_params=params(2),
    )(place, *blocks)


def add_halves_kernel(*refs):
    ins, outs = refs[:4], refs[4:]
    total = ins[0][...].astype(jnp.float32)
    for ref in ins[1:]:
        total += ref[...].astype(jnp.float32)
    for half, out_ref in enumerate(outs):
        out_ref[...] = total[:, 128 * half : 128 * half + 128].astype(out_ref.dtype)


def add_halves(*blocks):
    rows, wide = blocks[0].shape
    return pl.pallas_call(
        add_halves_kernel,
        out_shape=[jax.ShapeDtypeStruct((rows, wide // 2), jnp.bfloat16)] * 2,
        in_specs=[VMEM] * 4,
        out_specs=[VMEM] * 2,
        compiler_params=params(1),
    )(*blocks)


def head_grad_kernel(place_ref, grad_ref, own_ref, sent_ref, twin_ref, out_ref):
    teacher = place_ref[0] == 0
    from_twin = pl.program_id(0) // 2 != place_ref[4]

    def write(block):
        out_ref[...] = jnp.dot(
            grad_ref[...], block, preferred_element_type=jnp.float32
        ).astype(jnp.bfloat16)

    @pl.when(jnp.logical_not(teacher))
    def _():
        write(own_ref[0])

    @pl.when(jnp.logical_and(teacher, from_twin))
    def _():
        write(twin_ref[...])

    @pl.when(jnp.logical_and(teacher, jnp.logical_not(from_twin)))
    def _():
        write(sent_ref[...])


def head_grad_half(place, grad, hidden, sent, twin):
    width, toks = grad.shape
    block = hidden.shape[2] // 2
    return pl.pallas_call(
        head_grad_kernel,
        grid_spec=pltpu.PrefetchScalarGridSpec(
            num_scalar_prefetch=1,
            grid=(4,),
            in_specs=[
                pl.BlockSpec((width, toks), lambda step, place: (0, 0)),
                pl.BlockSpec((1, toks, block), lambda step, place: (2 + step // 2, 0, step % 2)),
                pl.BlockSpec((toks, block), lambda step, place: (0, step % 2)),
                pl.BlockSpec((toks, block), lambda step, place: (0, step % 2)),
            ],
            out_specs=pl.BlockSpec((width, block), lambda step, place: (0, step)),
        ),
        out_shape=jax.ShapeDtypeStruct((width, 4 * block), jnp.bfloat16),
        compiler_params=params(8),
    )(place, grad, hidden, sent, twin)


def spread(stats, name):
    far = send(stats, **{name: 2})
    near = send_by_core(stats, {name: 1}, {name: 3})
    return [stats, far, near, send(near, c=1)]


def on_device(hidden, head, token_ids, loss_mask):
    section, tok, vocab = (lax.axis_index(name) for name in AXES)
    place = jnp.stack([section, tok, vocab // 8, vocab // 2 % 4, vocab % 2]).astype(jnp.int32)
    core = vocab % 2
    head_t = head[0].T
    states = hidden[0]

    with jax.named_scope("gather_tok"):
        block = jnp.stack([states] + [send(states, t=d) for d in (1, 2, 3)])
    with jax.named_scope("gather_first"):
        block = jnp.stack([block] + [send_by_core(block, {"x": d}, {"y": d}) for d in (1, 2, 3)])
    with jax.named_scope("gather_second"):
        own = [block] + [send_by_core(block, {"y": d}, {"x": d}) for d in (1, 2, 3)]
    with jax.named_scope("gather_cores"):
        other = [send(block, c=1) for block in own]
    with jax.named_scope("logits"):
        gathered, half, scaled, short, local = logits_parts(place, head_t, own, other)

    with jax.named_scope("stats"):
        stats = merge(local, send(local, c=1))
        stats, short, half = lax.optimization_barrier((stats, short, half))
    with jax.named_scope("exchange_scaled"):
        other_short = send(short, s=1)
    with jax.named_scope("student_hidden"):
        sent = send(half, only=1, s=1)
        twin = send(sent, only=0, c=1)
    with jax.named_scope("stats"):
        stats = merge(*spread(stats, "x"))
        stats = merge(*spread(stats, "y"))
        own_stats = local_scale(local, *spread(stats, "t"))
        other_stats = send(own_stats, s=1)

    with jax.named_scope("hidden_grad_give"):
        give, grad, turned = give_parts(
            place, scaled, other_short, own_stats, other_stats, token_ids[None], loss_mask[None], head_t
        )
        received = [send(block, only=1, c=1) for block in give]
    with jax.named_scope("hidden_grad_keep"):
        sums = keep_parts(place, turned, head_t, received)
    with jax.named_scope("reduce_first"):
        firsts = [send_by_core(sums[d], {"x": d}, {"y": d}, 1) for d in (1, 2, 3)]
    with jax.named_scope("head_grad"):
        head_out = head_grad_half(place, grad, gathered, sent, twin)
        firsts[0], head_out = lax.optimization_barrier((firsts[0], head_out))
    with jax.named_scope("reduce_second"):
        parts = add_split(sums[0], *firsts)
        seconds = [send_by_core(parts[d], {"y": d}, {"x": d}, 1) for d in (1, 2, 3)]
    with jax.named_scope("reduce_tok"):
        rows = add_rows(place, [parts[0]] + seconds)
        left, right = add_halves(rows[0], *[send(rows[d], only=1, t=d) for d in (1, 2, 3)])
    with jax.named_scope("hidden_out"):
        straight = send_by_core(left, {"s": 1}, {"c": 1}, 1)
        across = send_by_core(right, {"s": 1, "c": 1}, None, 1)
        mine = jnp.where(section == 1, right, across)
        hidden_out = jnp.where(core == 1, mine, straight)
    return head_out.T, hidden_out


def solution(mesh):
    in_specs = (P("section", "tok", "vocab"), P("section", None, ("tok", "vocab")), P(), P())
    out_specs = (P("section", ("tok", "vocab")), P("tok", ("section", "vocab")))
    return jax.shard_map(
        on_device, mesh=mesh, in_specs=in_specs, out_specs=out_specs, check_vma=False
    )
```

```python
import jax
import jax.numpy as jnp
from jax import lax
from jax.experimental import pallas as pl
from jax.experimental.pallas import tpu as pltpu
from jax.sharding import PartitionSpec as P

AXES = ("section", "tok", "vocab")
SIZES = {"s": 2, "t": 4, "x": 4, "y": 4, "c": 2}
MIB = 1024 * 1024


def route(shift_of):
    names = list(SIZES)
    pairs = []
    for device in range(256):
        place, rest = {}, device
        for name in reversed(names):
            rest, place[name] = divmod(rest, SIZES[name])
        shift = shift_of(place)
        target = 0
        for name in names:
            target = target * SIZES[name] + (place[name] + shift.get(name, 0)) % SIZES[name]
        pairs.append((device, target))
    return pairs


def send(block, **shift):
    return lax.ppermute(block, AXES, route(lambda place: shift))


def send_by_core(block, even, odd):
    return lax.ppermute(block, AXES, route(lambda place: odd if place["c"] else even))


def send_both_ways(block):
    def shift_of(place):
        return {"s": 1, "t": (1 if place["s"] else 3) if place["c"] else 0}

    return lax.ppermute(block, AXES, route(shift_of))


def send_left(block):
    return lax.ppermute(block, AXES, route(lambda place: {"c" if place["s"] == place["c"] else "s": 1}))


def params(mib):
    return pltpu.CompilerParams(vmem_limit_bytes=mib * MIB)


VMEM = pl.BlockSpec(memory_space=pltpu.VMEM)


def stage_kernel(in_ref, out_ref):
    out_ref[...] = in_ref[...]


def stage(head_t):
    width, features = head_t.shape
    block = pl.BlockSpec((width, features // 8), lambda step: (0, step))
    return pl.pallas_call(
        stage_kernel,
        grid=(8,),
        out_shape=jax.ShapeDtypeStruct(head_t.shape, head_t.dtype),
        in_specs=[block],
        out_specs=block,
        compiler_params=params(6),
        cost_estimate=pl.CostEstimate(flops=0, bytes_accessed=4 * width * features, transcendentals=0),
    )(head_t)


def first_half_kernel(place_ref, *refs):
    own, out_ref = refs[:4], refs[4]
    tok, x, y, c = place_ref[1], place_ref[2], place_ref[3], place_ref[4]
    _, _, rows, chunk = own[0].shape

    def lay(x_at, y_at, piece):
        columns = pl.ds(pl.multiple_of(y_at * chunk, chunk), chunk)
        for dt in range(4):
            at = pl.ds(pl.multiple_of((tok + 4 - dt) % 4 * rows, rows), rows)
            out_ref[x_at, at, columns] = piece(dt)

    for x_at in range(2):
        dx = (x + 4 - x_at) % 4

        @pl.when(c == 0)
        def _():
            for dy in range(4):
                lay(x_at, (y + 4 - dy) % 4, lambda dt: own[dy][dx, dt])

        for step in range(4):
            @pl.when(jnp.logical_and(c == 1, dx == step))
            def _():
                for dy in range(4):
                    lay(x_at, (y + 4 - dy) % 4, lambda dt: own[step][dy, dt])


def first_half(place, own):
    _, _, rows, chunk = own[0].shape
    return pl.pallas_call(
        first_half_kernel,
        out_shape=jax.ShapeDtypeStruct((2, 4 * rows, 4 * chunk), own[0].dtype),
        in_specs=[pl.BlockSpec(memory_space=pltpu.SMEM)] + [VMEM] * 4,
        out_specs=VMEM,
        compiler_params=params(5),
    )(place, *own)


def logits_kernel(place_ref, head_ref, *refs):
    own, other = refs[:4], refs[4:8]
    hidden_ref, scaled_ref, short_ref, stats_ref, acc_ref = refs[8:]
    step = pl.program_id(0)
    tok, y, c = place_ref[1], place_ref[3], place_ref[4]
    _, _, rows, chunk = own[0].shape

    def lay(columns, piece):
        for dt in range(4):
            at = pl.ds(pl.multiple_of((tok + 4 - dt) % 4 * rows, rows), rows)
            hidden_ref[0, at, columns] = piece(dt)

    for dy in range(4):
        y_at = (y + 4 - dy) % 4
        for core, blocks in ((c, own), (1 - c, other)):
            columns = pl.ds(pl.multiple_of((y_at * 2 + core) * chunk, chunk), chunk)

            @pl.when(core == 0)
            def _():
                lay(columns, lambda dt: blocks[dy][step, dt])

            for dx in range(4):
                @pl.when(jnp.logical_and(core == 1, step == dx))
                def _():
                    lay(columns, lambda dt: blocks[dx][dy, dt])

    part = lax.dot_general(
        head_ref[...], hidden_ref[0], (((1,), (1,)), ((), ())), preferred_element_type=jnp.float32
    )

    @pl.when(step == 0)
    def _():
        acc_ref[...] = part

    @pl.when(step > 0)
    def _():
        acc_ref[...] += part

    @pl.when(step == 3)
    def _():
        logits = acc_ref[...]
        peak = jnp.max(logits, axis=0, keepdims=True)
        shifted = logits - peak
        scaled = jnp.exp(shifted)
        scaled_ref[...] = scaled
        short_ref[...] = scaled.astype(jnp.bfloat16)
        stats_ref[0:1] = peak
        stats_ref[1:2] = jnp.sum(scaled, axis=0, keepdims=True)
        stats_ref[2:3] = jnp.sum(scaled * shifted, axis=0, keepdims=True)
        stats_ref[3:8] = jnp.zeros((5, peak.shape[1]), jnp.float32)


def logits_parts(place, head_t, own, other):
    width, features = head_t.shape
    toks = 4 * own[0].shape[2]
    block = features // 4

    def fixed(step, place):
        return (0, 0)

    piece = pl.BlockSpec(own[0].shape, lambda step, place: (0, 0, 0, 0))
    return pl.pallas_call(
        logits_kernel,
        grid_spec=pltpu.PrefetchScalarGridSpec(
            num_scalar_prefetch=1,
            grid=(4,),
            in_specs=[pl.BlockSpec((width, block), lambda step, place: (0, (place[2] + 4 - step) % 4))]
            + [piece] * 8,
            out_specs=[
                pl.BlockSpec((1, toks, block), lambda step, place: ((place[2] + 4 - step) % 4, 0, 0)),
                pl.BlockSpec((width, toks), fixed),
                pl.BlockSpec((width, toks), fixed),
                pl.BlockSpec((8, toks), fixed),
            ],
            scratch_shapes=[pltpu.VMEM((width, toks), jnp.float32)],
        ),
        out_shape=[
            jax.ShapeDtypeStruct((4, toks, block), jnp.bfloat16),
            jax.ShapeDtypeStruct((width, toks), jnp.float32),
            jax.ShapeDtypeStruct((width, toks), jnp.bfloat16),
            jax.ShapeDtypeStruct((8, toks), jnp.float32),
        ],
        compiler_params=params(26),
    )(place, head_t, *own, *other)


def merge_kernel(*refs):
    *ins, out_ref = refs
    peak = ins[0][0:1]
    for ref in ins[1:]:
        peak = jnp.maximum(peak, ref[0:1])
    total = jnp.zeros_like(peak)
    moment = jnp.zeros_like(peak)
    for ref in ins:
        drop = ref[0:1] - peak
        factor = jnp.exp(drop)
        total += factor * ref[1:2]
        moment += factor * (ref[2:3] + drop * ref[1:2])
    out_ref[0:1] = peak
    out_ref[1:2] = total
    out_ref[2:3] = moment
    out_ref[3:8] = jnp.zeros((5, peak.shape[1]), jnp.float32)


def merge(*stats):
    return pl.pallas_call(
        merge_kernel,
        out_shape=jax.ShapeDtypeStruct(stats[0].shape, jnp.float32),
        in_specs=[VMEM] * len(stats),
        out_specs=VMEM,
        compiler_params=params(1),
    )(*stats)


def scale_kernel(local_ref, *refs):
    *ins, out_ref = refs
    peak = ins[0][0:1]
    for ref in ins[1:]:
        peak = jnp.maximum(peak, ref[0:1])
    total = jnp.zeros_like(peak)
    moment = jnp.zeros_like(peak)
    for ref in ins:
        drop = ref[0:1] - peak
        factor = jnp.exp(drop)
        total += factor * ref[1:2]
        moment += factor * (ref[2:3] + drop * ref[1:2])
    out_ref[0:1] = jnp.exp(local_ref[0:1] - peak) / total
    out_ref[1:2] = jnp.log(total) - moment / total
    out_ref[2:8] = jnp.zeros((6, peak.shape[1]), jnp.float32)


def local_scale(local, *stats):
    return pl.pallas_call(
        scale_kernel,
        out_shape=jax.ShapeDtypeStruct(local.shape, jnp.float32),
        in_specs=[VMEM] * (1 + len(stats)),
        out_specs=VMEM,
        compiler_params=params(1),
    )(local, *stats)


def grad_kernel(place_ref, own_ref, other_ref, own_stats, other_stats, ids_ref, mask_ref, grad_ref, turned_ref):
    teacher = place_ref[0] == 0
    mask = mask_ref[...].astype(jnp.float32)
    entropy = jnp.where(teacher, own_stats[1:2], other_stats[1:2])
    by_own = jnp.where(teacher, -entropy, entropy + 1.0) * own_stats[0:1] * mask
    by_other = jnp.where(teacher, entropy + 1.0, -entropy) * other_stats[0:1] * mask
    width = own_ref.shape[0]
    first = ((place_ref[1] * 4 + place_ref[2]) * 8 + place_ref[3] * 2 + place_ref[4]) * width
    entries = lax.broadcasted_iota(jnp.int32, own_ref.shape, 0) + first
    onehot = jnp.where(entries == ids_ref[...], mask, 0.0)
    grad = by_own * own_ref[...] + by_other * other_ref[...].astype(jnp.float32) - onehot
    grad_ref[...] = grad.astype(jnp.bfloat16)
    turned_ref[...] = grad.T.astype(jnp.bfloat16)


def logits_grad(place, own, other, own_stats, other_stats, ids, mask):
    width, toks = own.shape
    return pl.pallas_call(
        grad_kernel,
        out_shape=[
            jax.ShapeDtypeStruct((width, toks), jnp.bfloat16),
            jax.ShapeDtypeStruct((toks, width), jnp.bfloat16),
        ],
        in_specs=[pl.BlockSpec(memory_space=pltpu.SMEM)] + [VMEM] * 6,
        out_specs=[VMEM, VMEM],
        compiler_params=params(5),
    )(place, own, other, own_stats, other_stats, ids, mask)


def products_kernel(place_ref, turned_ref, *refs):
    *ins, out_ref = refs
    for e in range(4):
        part = jnp.dot(turned_ref[...], ins[e][...], preferred_element_type=jnp.float32)
        if len(ins) > 4:
            part += ins[4][e].astype(jnp.float32)
        out_ref[e] = part.astype(jnp.bfloat16)


def products(place, turned, head_t, d, received=None):
    toks, width = turned.shape
    share = jax.ShapeDtypeStruct((4, toks, 256), jnp.bfloat16)

    def piece(e):
        def index(step, place):
            c = 1 - place[4] if received is None else place[4]
            at_x = (place[2] + jnp.where(c == 0, d, e)) % 4
            at_y = (place[3] + jnp.where(c == 0, e, d)) % 4
            return (0, c * 16 + at_x * 4 + at_y)

        return pl.BlockSpec((width, 256), index)

    whole = pl.BlockSpec(share.shape, lambda step, place: (0, 0, 0))
    extra = [] if received is None else [received]
    return pl.pallas_call(
        products_kernel,
        grid_spec=pltpu.PrefetchScalarGridSpec(
            num_scalar_prefetch=1,
            grid=(1,),
            in_specs=[pl.BlockSpec(turned.shape, lambda step, place: (0, 0))]
            + [piece(e) for e in range(4)]
            + [whole] * len(extra),
            out_specs=whole,
        ),
        out_shape=share,
        compiler_params=params(7),
    )(place, turned, *[head_t] * 4, *extra)


def add_split_kernel(*refs):
    ins, outs = refs[:4], refs[4:]
    for d, out_ref in enumerate(outs):
        total = ins[0][d].astype(jnp.float32)
        for ref in ins[1:]:
            total += ref[d].astype(jnp.float32)
        out_ref[...] = total.astype(out_ref.dtype)


def add_split(*blocks):
    return pl.pallas_call(
        add_split_kernel,
        out_shape=[jax.ShapeDtypeStruct(blocks[0].shape[1:], blocks[0].dtype)] * 4,
        in_specs=[VMEM] * 4,
        out_specs=[VMEM] * 4,
        compiler_params=params(6),
    )(*blocks)


def add_rows_kernel(place_ref, *refs):
    ins, outs, sum_ref = refs[:4], refs[4:8], refs[8]
    tok = place_ref[1]
    total = ins[0][...].astype(jnp.float32)
    for ref in ins[1:]:
        total += ref[...].astype(jnp.float32)
    sum_ref[...] = total.astype(sum_ref.dtype)
    block = outs[0].shape[0]
    for d, out_ref in enumerate(outs):
        out_ref[...] = sum_ref[pl.ds(pl.multiple_of((tok + d) % 4 * block, block), block), :]


def add_rows(place, blocks):
    toks, wide = blocks[0].shape
    return pl.pallas_call(
        add_rows_kernel,
        out_shape=[jax.ShapeDtypeStruct((toks // 4, wide), jnp.bfloat16)] * 4,
        in_specs=[pl.BlockSpec(memory_space=pltpu.SMEM)] + [VMEM] * 4,
        out_specs=[VMEM] * 4,
        scratch_shapes=[pltpu.VMEM((toks, wide), jnp.bfloat16)],
        compiler_params=params(2),
    )(place, *blocks)


def add_halves_kernel(*refs):
    ins, outs = refs[:4], refs[4:]
    total = ins[0][...].astype(jnp.float32)
    for ref in ins[1:]:
        total += ref[...].astype(jnp.float32)
    for half, out_ref in enumerate(outs):
        out_ref[...] = total[:, 128 * half : 128 * half + 128].astype(out_ref.dtype)


def add_halves(*blocks):
    rows, wide = blocks[0].shape
    return pl.pallas_call(
        add_halves_kernel,
        out_shape=[jax.ShapeDtypeStruct((rows, wide // 2), jnp.bfloat16)] * 2,
        in_specs=[VMEM] * 4,
        out_specs=[VMEM] * 2,
        compiler_params=params(1),
    )(*blocks)


def head_grad_kernel(place_ref, grad_ref, own_ref, sent_ref, twin_ref, out_ref):
    teacher = place_ref[0] == 0
    core = place_ref[4]

    def product(block):
        return jnp.dot(grad_ref[...], block, preferred_element_type=jnp.float32).astype(jnp.bfloat16)

    @pl.when(jnp.logical_not(teacher))
    def _():
        out_ref[...] = product(own_ref[0])

    @pl.when(teacher)
    def _():
        for y_at in range(2):
            for ref, part in ((sent_ref, core), (twin_ref, 1 - core)):
                columns = pl.ds(pl.multiple_of((y_at * 2 + part) * 256, 256), 256)
                out_ref[:, columns] = product(ref[0, :, 256 * y_at : 256 * y_at + 256])


def head_grad_half(place, grad, hidden, sent, twin):
    width, toks = grad.shape
    block = hidden.shape[2] // 2
    part = pl.BlockSpec((1, toks, block // 2), lambda step, place: (step // 2, 0, step % 2))
    return pl.pallas_call(
        head_grad_kernel,
        grid_spec=pltpu.PrefetchScalarGridSpec(
            num_scalar_prefetch=1,
            grid=(4,),
            in_specs=[
                pl.BlockSpec((width, toks), lambda step, place: (0, 0)),
                pl.BlockSpec((1, toks, block), lambda step, place: (2 + step // 2, 0, step % 2)),
            ]
            + [part] * 2,
            out_specs=pl.BlockSpec((width, block), lambda step, place: (0, step)),
        ),
        out_shape=jax.ShapeDtypeStruct((width, 4 * block), jnp.bfloat16),
        compiler_params=params(8),
    )(place, grad, hidden, sent, twin)


def spread(stats, name):
    far = send(stats, **{name: 2})
    near = send_by_core(stats, {name: 1}, {name: 3})
    return [stats, far, near, send(near, c=1)]


def on_device(hidden, head, token_ids, loss_mask):
    section, tok, vocab = (lax.axis_index(name) for name in AXES)
    place = jnp.stack([section, tok, vocab // 8, vocab // 2 % 4, vocab % 2]).astype(jnp.int32)
    core = vocab % 2
    states = hidden[0]

    with jax.named_scope("gather_tok"):
        blocks = [states] + [send(states, t=d) for d in (1, 2, 3)]
    with jax.named_scope("stage"):
        head_t = stage(head[0].T)
        head_t, *blocks = lax.optimization_barrier((head_t, *blocks))
    with jax.named_scope("gather_tok"):
        block = jnp.stack(blocks)
    with jax.named_scope("gather_first"):
        block = jnp.stack([block] + [send_by_core(block, {"x": d}, {"y": d}) for d in (1, 2, 3)])
    with jax.named_scope("gather_second"):
        own = [block] + [send_by_core(block, {"y": d}, {"x": d}) for d in (1, 2, 3)]
    with jax.named_scope("student_hidden"):
        sent = send_both_ways(first_half(place, own))
    with jax.named_scope("gather_cores"):
        other = [send(block, c=1) for block in own]
    with jax.named_scope("logits"):
        gathered, scaled, short, local = logits_parts(place, head_t, own, other)

    with jax.named_scope("stats"):
        stats = merge(local, send(local, c=1))
        stats, short = lax.optimization_barrier((stats, short))
    with jax.named_scope("exchange_scaled"):
        other_short = send(short, s=1)
    with jax.named_scope("stats"):
        stats = merge(*spread(stats, "x"))
        stats, sent = lax.optimization_barrier((stats, sent))
    with jax.named_scope("student_hidden"):
        twin = send(sent, c=1)
    with jax.named_scope("stats"):
        stats = merge(*spread(stats, "y"))
        own_stats = local_scale(local, *spread(stats, "t"))
        other_stats = send(own_stats, s=1)

    with jax.named_scope("logits_grad"):
        grad, turned = logits_grad(
            place, scaled, other_short, own_stats, other_stats, token_ids[None], loss_mask[None]
        )
    turned, twin = lax.optimization_barrier((turned, twin))
    received, sums, firsts = {}, {}, []
    with jax.named_scope("hidden_grad_give"):
        for d in (1, 2, 3, 0):
            give = products(place, turned, head_t, d)
            turned, give = lax.optimization_barrier((turned, give))
            received[d] = send(give, c=1)
    with jax.named_scope("hidden_grad_keep"):
        for d in (1, 2, 3, 0):
            sums[d] = products(place, turned, head_t, d, received[d])
            turned, sums[d] = lax.optimization_barrier((turned, sums[d]))
            if d > 0:
                firsts.append(send_by_core(sums[d], {"x": d}, {"y": d}))
    with jax.named_scope("head_grad"):
        head_out = head_grad_half(place, grad, gathered, sent, twin)
        firsts[0], head_out = lax.optimization_barrier((firsts[0], head_out))
    with jax.named_scope("reduce_second"):
        parts = add_split(sums[0], *firsts)
        seconds = [send_by_core(parts[d], {"y": d}, {"x": d}) for d in (1, 2, 3)]
    with jax.named_scope("reduce_tok"):
        rows = add_rows(place, [parts[0]] + seconds)
        left, right = add_halves(rows[0], *[send(rows[d], t=d) for d in (1, 2, 3)])
    with jax.named_scope("hidden_out"):
        straight = send_left(left)
        across = send(right, s=1, c=1)
        mine = jnp.where(section == 1, right, across)
        hidden_out = jnp.where(core == 1, mine, straight)
    return head_out.T, hidden_out


def solution(mesh):
    in_specs = (P("section", "tok", "vocab"), P("section", None, ("tok", "vocab")), P(), P())
    out_specs = (P("section", ("tok", "vocab")), P("tok", ("section", "vocab")))
    return jax.shard_map(
        on_device, mesh=mesh, in_specs=in_specs, out_specs=out_specs, check_vma=False
    )
```

```python
import functools
import jax
import jax.numpy as jnp
from jax import lax
from jax.experimental import pallas as pl
from jax.experimental.pallas import tpu as pltpu
from jax.sharding import PartitionSpec as P

AXES = ("section", "tok", "vocab")
SIZES = {"s": 2, "t": 4, "x": 4, "y": 4, "c": 2}
MIB = 1024 * 1024


def route(shift_of):
    names = list(SIZES)
    pairs = []
    for device in range(256):
        place, rest = {}, device
        for name in reversed(names):
            rest, place[name] = divmod(rest, SIZES[name])
        shift = shift_of(place)
        target = 0
        for name in names:
            target = target * SIZES[name] + (place[name] + shift.get(name, 0)) % SIZES[name]
        pairs.append((device, target))
    return pairs


def send(block, **shift):
    return lax.ppermute(block, AXES, route(lambda place: shift))


def send_by_core(block, even, odd):
    return lax.ppermute(block, AXES, route(lambda place: odd if place["c"] else even))


def send_both_ways(block):
    def shift_of(place):
        return {"s": 1, "t": (1 if place["s"] else 3) if place["c"] else 0}

    return lax.ppermute(block, AXES, route(shift_of))


def params(mib):
    return pltpu.CompilerParams(vmem_limit_bytes=mib * MIB)


VMEM = pl.BlockSpec(memory_space=pltpu.VMEM)
SMEM = pl.BlockSpec(memory_space=pltpu.SMEM)


def stage_kernel(head_ref, out_ref, arrived):
    copy = pltpu.make_async_copy(head_ref, out_ref, arrived)
    copy.start()
    copy.wait()


def stage(head_t):
    return pl.pallas_call(
        stage_kernel,
        out_shape=jax.ShapeDtypeStruct(head_t.shape, head_t.dtype),
        in_specs=[pl.BlockSpec(memory_space=pl.ANY)],
        out_specs=VMEM,
        scratch_shapes=[pltpu.SemaphoreType.DMA],
        compiler_params=params(10),
    )(head_t)


def first_half_kernel(place_ref, *refs):
    own, out_ref = refs[:4], refs[4]
    tok, x, y, c = place_ref[1], place_ref[2], place_ref[3], place_ref[4]
    _, _, rows, chunk = own[0].shape

    def lay(x_at, y_at, piece):
        columns = pl.ds(pl.multiple_of(y_at * chunk, chunk), chunk)
        for dt in range(4):
            at = pl.ds(pl.multiple_of((tok + 4 - dt) % 4 * rows, rows), rows)
            out_ref[x_at, at, columns] = piece(dt)

    for x_at in range(2):
        dx = (x + 4 - x_at) % 4

        @pl.when(c == 0)
        def _():
            for dy in range(4):
                lay(x_at, (y + 4 - dy) % 4, lambda dt: own[dy][dx, dt])

        for step in range(4):
            @pl.when(jnp.logical_and(c == 1, dx == step))
            def _():
                for dy in range(4):
                    lay(x_at, (y + 4 - dy) % 4, lambda dt: own[step][dy, dt])


def first_half(place, own):
    _, _, rows, chunk = own[0].shape
    return pl.pallas_call(
        first_half_kernel,
        out_shape=jax.ShapeDtypeStruct((2, 4 * rows, 4 * chunk), own[0].dtype),
        in_specs=[SMEM] + [VMEM] * 4,
        out_specs=VMEM,
        compiler_params=params(5),
    )(place, *own)


def logits_kernel(place_ref, head_ref, *refs):
    own, other = refs[:4], refs[4:8]
    hidden_ref, scaled_ref, short_ref, stats_ref, acc_ref = refs[8:]
    tok, x, y, c = place_ref[1], place_ref[2], place_ref[3], place_ref[4]
    _, _, rows, chunk = own[0].shape
    for core, blocks in ((c, own), (1 - c, other)):
        for late in range(4):
            for early in range(4):
                at_x = (x + 4 - jnp.where(core == 0, early, late)) % 4
                at_y = (y + 4 - jnp.where(core == 0, late, early)) % 4
                columns = pl.ds(pl.multiple_of(((at_x * 4 + at_y) * 2 + core) * chunk, chunk), chunk)
                for dt in range(4):
                    at = pl.ds(pl.multiple_of((tok + 4 - dt) % 4 * rows, rows), rows)
                    hidden_ref[at, columns] = blocks[late][early, dt]

    acc_ref[...] = jnp.zeros_like(acc_ref)
    step = head_ref.shape[1] // 8

    @pl.loop(0, 8)
    def _(k):
        columns = pl.ds(pl.multiple_of(k * step, step), step)
        acc_ref[...] += lax.dot_general(
            head_ref[:, columns],
            hidden_ref[:, columns],
            (((1,), (1,)), ((), ())),
            preferred_element_type=jnp.float32,
        )

    logits = acc_ref[...]
    peak = jnp.max(logits, axis=0, keepdims=True)
    shifted = logits - peak
    scaled = jnp.exp(shifted)
    scaled_ref[...] = scaled
    short_ref[...] = scaled.astype(jnp.bfloat16)
    stats_ref[0:1] = peak
    stats_ref[1:2] = jnp.sum(scaled, axis=0, keepdims=True)
    stats_ref[2:3] = jnp.sum(scaled * shifted, axis=0, keepdims=True)
    stats_ref[3:8] = jnp.zeros((5, peak.shape[1]), jnp.float32)


def logits_parts(place, head_t, own, other):
    width, features = head_t.shape
    toks = 4 * own[0].shape[2]
    return pl.pallas_call(
        logits_kernel,
        out_shape=[
            jax.ShapeDtypeStruct((toks, features), jnp.bfloat16),
            jax.ShapeDtypeStruct((width, toks), jnp.float32),
            jax.ShapeDtypeStruct((width, toks), jnp.bfloat16),
            jax.ShapeDtypeStruct((8, toks), jnp.float32),
        ],
        in_specs=[SMEM] + [VMEM] * 9,
        out_specs=[VMEM] * 4,
        scratch_shapes=[pltpu.VMEM((width, toks), jnp.float32)],
        compiler_params=params(26),
    )(place, head_t, *own, *other)


def merge_kernel(*refs):
    *ins, out_ref = refs
    peak = ins[0][0:1]
    for ref in ins[1:]:
        peak = jnp.maximum(peak, ref[0:1])
    total = jnp.zeros_like(peak)
    moment = jnp.zeros_like(peak)
    for ref in ins:
        drop = ref[0:1] - peak
        factor = jnp.exp(drop)
        total += factor * ref[1:2]
        moment += factor * (ref[2:3] + drop * ref[1:2])
    out_ref[0:1] = peak
    out_ref[1:2] = total
    out_ref[2:3] = moment
    out_ref[3:8] = jnp.zeros((5, peak.shape[1]), jnp.float32)


def merge(*stats):
    return pl.pallas_call(
        merge_kernel,
        out_shape=jax.ShapeDtypeStruct(stats[0].shape, jnp.float32),
        in_specs=[VMEM] * len(stats),
        out_specs=VMEM,
        compiler_params=params(1),
    )(*stats)


def scale_kernel(local_ref, *refs):
    *ins, out_ref = refs
    peak = ins[0][0:1]
    for ref in ins[1:]:
        peak = jnp.maximum(peak, ref[0:1])
    total = jnp.zeros_like(peak)
    moment = jnp.zeros_like(peak)
    for ref in ins:
        drop = ref[0:1] - peak
        factor = jnp.exp(drop)
        total += factor * ref[1:2]
        moment += factor * (ref[2:3] + drop * ref[1:2])
    out_ref[0:1] = jnp.exp(local_ref[0:1] - peak) / total
    out_ref[1:2] = jnp.log(total) - moment / total
    out_ref[2:8] = jnp.zeros((6, peak.shape[1]), jnp.float32)


def local_scale(local, *stats):
    return pl.pallas_call(
        scale_kernel,
        out_shape=jax.ShapeDtypeStruct(local.shape, jnp.float32),
        in_specs=[VMEM] * (1 + len(stats)),
        out_specs=VMEM,
        compiler_params=params(1),
    )(local, *stats)


def grad_kernel(place_ref, own_ref, other_ref, own_stats, other_stats, ids_ref, mask_ref, grad_ref, turned_ref):
    teacher = place_ref[0] == 0
    mask = mask_ref[...].astype(jnp.float32)
    entropy = jnp.where(teacher, own_stats[1:2], other_stats[1:2])
    by_own = jnp.where(teacher, -entropy, entropy + 1.0) * own_stats[0:1] * mask
    by_other = jnp.where(teacher, entropy + 1.0, -entropy) * other_stats[0:1] * mask
    width = own_ref.shape[0]
    first = ((place_ref[1] * 4 + place_ref[2]) * 8 + place_ref[3] * 2 + place_ref[4]) * width
    entries = lax.broadcasted_iota(jnp.int32, own_ref.shape, 0) + first
    onehot = jnp.where(entries == ids_ref[...], mask, 0.0)
    grad = by_own * own_ref[...] + by_other * other_ref[...].astype(jnp.float32) - onehot
    grad_ref[...] = grad.astype(jnp.bfloat16)
    turned_ref[...] = grad.T.astype(jnp.bfloat16)


def logits_grad(place, own, other, own_stats, other_stats, ids, mask):
    width, toks = own.shape
    return pl.pallas_call(
        grad_kernel,
        out_shape=[
            jax.ShapeDtypeStruct((width, toks), jnp.bfloat16),
            jax.ShapeDtypeStruct((toks, width), jnp.bfloat16),
        ],
        in_specs=[SMEM] + [VMEM] * 6,
        out_specs=[VMEM, VMEM],
        compiler_params=params(5),
    )(place, own, other, own_stats, other_stats, ids, mask)


def products_kernel(d, twin, place_ref, turned_ref, head_ref, *refs):
    *ins, out_ref = refs
    c = 1 - place_ref[4] if twin else place_ref[4]
    for e in range(4):
        at_x = (place_ref[2] + jnp.where(c == 0, d, e)) % 4
        at_y = (place_ref[3] + jnp.where(c == 0, e, d)) % 4
        columns = pl.ds(pl.multiple_of((c * 16 + at_x * 4 + at_y) * 256, 256), 256)
        part = jnp.dot(turned_ref[...], head_ref[:, columns], preferred_element_type=jnp.float32)
        if not twin:
            part += ins[0][e].astype(jnp.float32)
        out_ref[e] = part.astype(jnp.bfloat16)


def products(place, turned, head_t, d, received=None):
    toks = turned.shape[0]
    extra = [] if received is None else [received]
    return pl.pallas_call(
        functools.partial(products_kernel, d, received is None),
        out_shape=jax.ShapeDtypeStruct((4, toks, 256), jnp.bfloat16),
        in_specs=[SMEM] + [VMEM] * (2 + len(extra)),
        out_specs=VMEM,
        compiler_params=params(11),
    )(place, turned, head_t, *extra)


def add_split_kernel(*refs):
    ins, outs = refs[:4], refs[4:]
    for d, out_ref in enumerate(outs):
        total = ins[0][d].astype(jnp.float32)
        for ref in ins[1:]:
            total += ref[d].astype(jnp.float32)
        out_ref[...] = total.astype(out_ref.dtype)


def add_split(*blocks):
    return pl.pallas_call(
        add_split_kernel,
        out_shape=[jax.ShapeDtypeStruct(blocks[0].shape[1:], blocks[0].dtype)] * 4,
        in_specs=[VMEM] * 4,
        out_specs=[VMEM] * 4,
        compiler_params=params(6),
    )(*blocks)


def add_rows_kernel(place_ref, *refs):
    ins, outs, sum_ref = refs[:4], refs[4:8], refs[8]
    tok = place_ref[1]
    total = ins[0][...].astype(jnp.float32)
    for ref in ins[1:]:
        total += ref[...].astype(jnp.float32)
    sum_ref[...] = total.astype(sum_ref.dtype)
    block = outs[0].shape[0]
    for d, out_ref in enumerate(outs):
        out_ref[...] = sum_ref[pl.ds(pl.multiple_of((tok + d) % 4 * block, block), block), :]


def add_rows(place, blocks):
    toks, wide = blocks[0].shape
    return pl.pallas_call(
        add_rows_kernel,
        out_shape=[jax.ShapeDtypeStruct((toks // 4, wide), jnp.bfloat16)] * 4,
        in_specs=[SMEM] + [VMEM] * 4,
        out_specs=[VMEM] * 4,
        scratch_shapes=[pltpu.VMEM((toks, wide), jnp.bfloat16)],
        compiler_params=params(2),
    )(place, *blocks)


def add_toks_kernel(place_ref, own_ref, *refs):
    ins, (keep_ref, give_ref) = refs[:4], refs[4:]
    even = place_ref[4] == 0
    first = jnp.where(even, ins[0][...].astype(jnp.float32), own_ref[...].astype(jnp.float32))
    total = first
    for ref in ins[1:]:
        total += ref[...].astype(jnp.float32)
    left, right = total[:, :128], total[:, 128:]
    keep_ref[...] = jnp.where(even, left, right).astype(keep_ref.dtype)
    give_ref[...] = jnp.where(even, right, left).astype(give_ref.dtype)


def add_toks(place, own, *received):
    rows, wide = own.shape
    return pl.pallas_call(
        add_toks_kernel,
        out_shape=[jax.ShapeDtypeStruct((rows, wide // 2), jnp.bfloat16)] * 2,
        in_specs=[SMEM] + [VMEM] * 5,
        out_specs=[VMEM] * 2,
        compiler_params=params(1),
    )(place, own, *received)


def choose_kernel(place_ref, keep_ref, got_ref, out_ref):
    mine = place_ref[0] == place_ref[4]
    keep, got = keep_ref[...].astype(jnp.float32), got_ref[...].astype(jnp.float32)
    out_ref[...] = jnp.where(mine, keep, got).astype(out_ref.dtype)


def choose(place, keep, got):
    return pl.pallas_call(
        choose_kernel,
        out_shape=jax.ShapeDtypeStruct(keep.shape, keep.dtype),
        in_specs=[SMEM, VMEM, VMEM],
        out_specs=VMEM,
        compiler_params=params(1),
    )(place, keep, got)


def head_grad_kernel(place_ref, grad_ref, own_ref, sent_ref, twin_ref, out_ref):
    teacher = place_ref[0] == 0
    core = place_ref[4]

    def product(block):
        return jnp.dot(grad_ref[...], block, preferred_element_type=jnp.float32).astype(jnp.bfloat16)

    @pl.when(jnp.logical_not(teacher))
    def _():
        out_ref[...] = product(own_ref[...])

    @pl.when(teacher)
    def _():
        for y_at in range(2):
            for ref, part in ((sent_ref, core), (twin_ref, 1 - core)):
                columns = pl.ds(pl.multiple_of((y_at * 2 + part) * 256, 256), 256)
                out_ref[:, columns] = product(ref[0, :, 256 * y_at : 256 * y_at + 256])


def head_grad_half(place, grad, hidden, sent, twin):
    width, toks = grad.shape
    block = hidden.shape[1] // 8
    part = pl.BlockSpec((1, toks, block // 2), lambda step, place: (step // 2, 0, step % 2))
    return pl.pallas_call(
        head_grad_kernel,
        grid_spec=pltpu.PrefetchScalarGridSpec(
            num_scalar_prefetch=1,
            grid=(4,),
            in_specs=[
                pl.BlockSpec((width, toks), lambda step, place: (0, 0)),
                pl.BlockSpec((toks, block), lambda step, place: (0, 4 + step)),
            ]
            + [part] * 2,
            out_specs=pl.BlockSpec((width, block), lambda step, place: (0, step)),
        ),
        out_shape=jax.ShapeDtypeStruct((width, 4 * block), jnp.bfloat16),
        compiler_params=params(8),
    )(place, grad, hidden, sent, twin)


def spread(stats, name):
    far = send(stats, **{name: 2})
    near = send_by_core(stats, {name: 1}, {name: 3})
    return [stats, far, near, send(near, c=1)]


def on_device(hidden, head, token_ids, loss_mask):
    section, tok, vocab = (lax.axis_index(name) for name in AXES)
    place = jnp.stack([section, tok, vocab >> 3, (vocab >> 1) & 3, vocab & 1]).astype(jnp.int32)
    states = hidden[0]

    with jax.named_scope("gather_tok"):
        blocks = [states] + [send(states, t=d) for d in (1, 2, 3)]
        place, *blocks = lax.optimization_barrier((place, *blocks))
        block = jnp.stack(blocks)
    with jax.named_scope("gather_first"):
        block = jnp.stack([block] + [send_by_core(block, {"x": d}, {"y": d}) for d in (1, 2, 3)])
    with jax.named_scope("gather_second"):
        own = [block] + [send_by_core(block, {"y": d}, {"x": d}) for d in (1, 2, 3)]
    with jax.named_scope("stage"):
        head_t, own[1] = lax.optimization_barrier((stage(head[0].T), own[1]))
    with jax.named_scope("student_hidden"):
        sent = send_both_ways(first_half(place, own))
    with jax.named_scope("gather_cores"):
        other = [send(block, c=1) for block in own]
    with jax.named_scope("logits"):
        gathered, scaled, short, local = logits_parts(place, head_t, own, other)

    with jax.named_scope("stats"):
        stats = merge(local, send(local, c=1))
        stats, short = lax.optimization_barrier((stats, short))
    with jax.named_scope("exchange_scaled"):
        other_short = send(short, s=1)
    with jax.named_scope("stats"):
        stats = merge(*spread(stats, "x"))
        stats, sent = lax.optimization_barrier((stats, sent))
    with jax.named_scope("student_hidden"):
        twin = send(sent, c=1)
    with jax.named_scope("stats"):
        stats = merge(*spread(stats, "y"))
        own_stats = local_scale(local, *spread(stats, "t"))
        other_stats = send(own_stats, s=1)

    with jax.named_scope("logits_grad"):
        grad, turned = logits_grad(
            place, scaled, other_short, own_stats, other_stats, token_ids[None], loss_mask[None]
        )
    turned, twin = lax.optimization_barrier((turned, twin))
    received, sums, firsts = {}, {}, []
    with jax.named_scope("hidden_grad_give"):
        for d in (1, 2, 3, 0):
            give = products(place, turned, head_t, d)
            turned, give = lax.optimization_barrier((turned, give))
            received[d] = send(give, c=1)
    with jax.named_scope("hidden_grad_keep"):
        for d in (1, 2, 3, 0):
            sums[d] = products(place, turned, head_t, d, received[d])
            turned, sums[d] = lax.optimization_barrier((turned, sums[d]))
            if d > 0:
                firsts.append(send_by_core(sums[d], {"x": d}, {"y": d}))
    with jax.named_scope("head_grad"):
        head_out = head_grad_half(place, grad, gathered, sent, twin)
        firsts[0], head_out = lax.optimization_barrier((firsts[0], head_out))
    with jax.named_scope("reduce_second"):
        parts = add_split(sums[0], *firsts)
        seconds = [send_by_core(parts[d], {"y": d}, {"x": d}) for d in (1, 2, 3)]
    with jax.named_scope("reduce_tok"):
        rows = add_rows(place, [parts[0]] + seconds)
        received = [send(rows[0], s=1)]
        received += [send_by_core(rows[d], {"s": 1, "t": d}, {"t": d}) for d in (1, 2, 3)]
        keep, give = add_toks(place, rows[0], *received)
    with jax.named_scope("hidden_out"):
        hidden_out = choose(place, keep, send(give, c=1))
    return head_out.T, hidden_out


def solution(mesh):
    in_specs = (P("section", "tok", "vocab"), P("section", None, ("tok", "vocab")), P(), P())
    out_specs = (P("section", ("tok", "vocab")), P("tok", ("section", "vocab")))
    return jax.shard_map(
        on_device, mesh=mesh, in_specs=in_specs, out_specs=out_specs, check_vma=False
    )
```

```python
import functools
import jax
import jax.numpy as jnp
from jax import lax
from jax.experimental import pallas as pl
from jax.experimental.pallas import tpu as pltpu
from jax.sharding import PartitionSpec as P

AXES = ("section", "tok", "vocab")
SIZES = {"s": 2, "t": 4, "x": 4, "y": 4, "c": 2}
MIB = 1024 * 1024


def route(shift_of):
    names = list(SIZES)
    pairs = []
    for device in range(256):
        place, rest = {}, device
        for name in reversed(names):
            rest, place[name] = divmod(rest, SIZES[name])
        shift = shift_of(place)
        target = 0
        for name in names:
            target = target * SIZES[name] + (place[name] + shift.get(name, 0)) % SIZES[name]
        pairs.append((device, target))
    return pairs


def send(block, **shift):
    return lax.ppermute(block, AXES, route(lambda place: shift))


def send_by_core(block, even, odd):
    return lax.ppermute(block, AXES, route(lambda place: odd if place["c"] else even))


def send_both_ways(block):
    def shift_of(place):
        return {"s": 1, "t": (1 if place["s"] else 3) if place["c"] else 0}

    return lax.ppermute(block, AXES, route(shift_of))


def params(mib):
    return pltpu.CompilerParams(vmem_limit_bytes=mib * MIB)


BRIEF = pl.CostEstimate(flops=0, bytes_accessed=0, transcendentals=0)
VMEM = pl.BlockSpec(memory_space=pltpu.VMEM)
SMEM = pl.BlockSpec(memory_space=pltpu.SMEM)


def stage_kernel(head_ref, out_ref, arrived):
    copy = pltpu.make_async_copy(head_ref, out_ref, arrived)
    copy.start()
    copy.wait()


def stage(head_t):
    return pl.pallas_call(
        stage_kernel,
        out_shape=jax.ShapeDtypeStruct(head_t.shape, head_t.dtype),
        in_specs=[pl.BlockSpec(memory_space=pl.ANY)],
        out_specs=VMEM,
        scratch_shapes=[pltpu.SemaphoreType.DMA],
        compiler_params=params(10),
    )(head_t)


def first_half_kernel(place_ref, *refs):
    own, out_ref = refs[:4], refs[4]
    tok, x, y, c = place_ref[1], place_ref[2], place_ref[3], place_ref[4]
    _, _, rows, chunk = own[0].shape

    def lay(x_at, y_at, piece):
        columns = pl.ds(pl.multiple_of(y_at * chunk, chunk), chunk)
        for dt in range(4):
            at = pl.ds(pl.multiple_of((tok + 4 - dt) % 4 * rows, rows), rows)
            out_ref[x_at, at, columns] = piece(dt)

    for x_at in range(2):
        dx = (x + 4 - x_at) % 4

        @pl.when(c == 0)
        def _():
            for dy in range(4):
                lay(x_at, (y + 4 - dy) % 4, lambda dt: own[dy][dx, dt])

        for step in range(4):
            @pl.when(jnp.logical_and(c == 1, dx == step))
            def _():
                for dy in range(4):
                    lay(x_at, (y + 4 - dy) % 4, lambda dt: own[step][dy, dt])


def first_half(place, own):
    _, _, rows, chunk = own[0].shape
    return pl.pallas_call(
        first_half_kernel,
        out_shape=jax.ShapeDtypeStruct((2, 4 * rows, 4 * chunk), own[0].dtype),
        in_specs=[SMEM] + [VMEM] * 4,
        out_specs=VMEM,
        compiler_params=params(5),
        cost_estimate=BRIEF,
    )(place, *own)


def lay_out(place_ref, core, blocks, hidden_ref):
    tok, x, y = place_ref[1], place_ref[2], place_ref[3]
    _, _, rows, chunk = blocks[0].shape
    for late in range(4):
        for early in range(4):
            at_x = (x + 4 - jnp.where(core == 0, early, late)) % 4
            at_y = (y + 4 - jnp.where(core == 0, late, early)) % 4
            columns = pl.ds(pl.multiple_of(at_y * chunk, chunk), chunk)
            for dt in range(4):
                at = pl.ds(pl.multiple_of((tok + 4 - dt) % 4 * rows, rows), rows)
                hidden_ref[at_x, at, columns] = blocks[late][early, dt]


def add_products(core, head_ref, hidden_ref, acc_ref):
    chunk = hidden_ref.shape[2] // 4

    @pl.loop(0, 4)
    def _(x):
        total = acc_ref[...]
        for y in range(4):
            columns = pl.ds(pl.multiple_of(((x * 4 + y) * 2 + core) * chunk, chunk), chunk)
            total += lax.dot_general(
                head_ref[:, columns],
                hidden_ref[x, :, y * chunk : y * chunk + chunk],
                (((1,), (1,)), ((), ())),
                preferred_element_type=jnp.float32,
            )
        acc_ref[...] = total


def own_logits_kernel(place_ref, head_ref, *refs):
    own, (hidden_ref, acc_ref) = refs[:4], refs[4:]
    lay_out(place_ref, place_ref[4], own, hidden_ref)
    acc_ref[...] = jnp.zeros_like(acc_ref)
    add_products(place_ref[4], head_ref, hidden_ref, acc_ref)


def own_logits(place, head_t, own):
    width, _ = head_t.shape
    _, _, rows, chunk = own[0].shape
    toks = 4 * rows
    return pl.pallas_call(
        own_logits_kernel,
        out_shape=[
            jax.ShapeDtypeStruct((4, toks, 4 * chunk), jnp.bfloat16),
            jax.ShapeDtypeStruct((width, toks), jnp.float32),
        ],
        in_specs=[SMEM] + [VMEM] * 5,
        out_specs=[VMEM] * 2,
        compiler_params=params(16),
    )(place, head_t, *own)


def logits_kernel(place_ref, head_ref, *refs):
    other, part_ref = refs[:4], refs[4]
    hidden_ref, scaled_ref, short_ref, stats_ref, acc_ref = refs[5:]
    lay_out(place_ref, 1 - place_ref[4], other, hidden_ref)
    acc_ref[...] = part_ref[...]
    add_products(1 - place_ref[4], head_ref, hidden_ref, acc_ref)
    logits = acc_ref[...]
    peak = jnp.max(logits, axis=0, keepdims=True)
    shifted = logits - peak
    scaled = jnp.exp(shifted)
    scaled_ref[...] = scaled
    short_ref[...] = scaled.astype(jnp.bfloat16)
    stats_ref[0:1] = peak
    stats_ref[1:2] = jnp.sum(scaled, axis=0, keepdims=True)
    stats_ref[2:3] = jnp.sum(scaled * shifted, axis=0, keepdims=True)
    stats_ref[3:8] = jnp.zeros((5, peak.shape[1]), jnp.float32)


def logits_parts(place, head_t, other, part):
    width, toks = part.shape
    _, _, rows, chunk = other[0].shape
    return pl.pallas_call(
        logits_kernel,
        out_shape=[
            jax.ShapeDtypeStruct((4, toks, 4 * chunk), jnp.bfloat16),
            jax.ShapeDtypeStruct((width, toks), jnp.float32),
            jax.ShapeDtypeStruct((width, toks), jnp.bfloat16),
            jax.ShapeDtypeStruct((8, toks), jnp.float32),
        ],
        in_specs=[SMEM] + [VMEM] * 6,
        out_specs=[VMEM] * 4,
        scratch_shapes=[pltpu.VMEM((width, toks), jnp.float32)],
        compiler_params=params(17),
        cost_estimate=BRIEF,
    )(place, head_t, *other, part)


def merge_kernel(*refs):
    *ins, out_ref = refs
    peak = ins[0][0:1]
    for ref in ins[1:]:
        peak = jnp.maximum(peak, ref[0:1])
    total = jnp.zeros_like(peak)
    moment = jnp.zeros_like(peak)
    for ref in ins:
        drop = ref[0:1] - peak
        factor = jnp.exp(drop)
        total += factor * ref[1:2]
        moment += factor * (ref[2:3] + drop * ref[1:2])
    out_ref[0:1] = peak
    out_ref[1:2] = total
    out_ref[2:3] = moment
    out_ref[3:8] = jnp.zeros((5, peak.shape[1]), jnp.float32)


def merge(*stats):
    return pl.pallas_call(
        merge_kernel,
        out_shape=jax.ShapeDtypeStruct(stats[0].shape, jnp.float32),
        in_specs=[VMEM] * len(stats),
        out_specs=VMEM,
        compiler_params=params(1),
        cost_estimate=BRIEF,
    )(*stats)


def scale_kernel(local_ref, *refs):
    *ins, out_ref = refs
    peak = ins[0][0:1]
    for ref in ins[1:]:
        peak = jnp.maximum(peak, ref[0:1])
    total = jnp.zeros_like(peak)
    moment = jnp.zeros_like(peak)
    for ref in ins:
        drop = ref[0:1] - peak
        factor = jnp.exp(drop)
        total += factor * ref[1:2]
        moment += factor * (ref[2:3] + drop * ref[1:2])
    out_ref[0:1] = jnp.exp(local_ref[0:1] - peak) / total
    out_ref[1:2] = jnp.log(total) - moment / total
    out_ref[2:8] = jnp.zeros((6, peak.shape[1]), jnp.float32)


def local_scale(local, *stats):
    return pl.pallas_call(
        scale_kernel,
        out_shape=jax.ShapeDtypeStruct(local.shape, jnp.float32),
        in_specs=[VMEM] * (1 + len(stats)),
        out_specs=VMEM,
        compiler_params=params(1),
        cost_estimate=BRIEF,
    )(local, *stats)


def grad_kernel(place_ref, own_ref, other_ref, own_stats, other_stats, ids_ref, mask_ref, grad_ref, turned_ref):
    teacher = place_ref[0] == 0
    mask = mask_ref[...].astype(jnp.float32)
    entropy = jnp.where(teacher, own_stats[1:2], other_stats[1:2])
    by_own = jnp.where(teacher, -entropy, entropy + 1.0) * own_stats[0:1] * mask
    by_other = jnp.where(teacher, entropy + 1.0, -entropy) * other_stats[0:1] * mask
    width = own_ref.shape[0]
    first = ((place_ref[1] * 4 + place_ref[2]) * 8 + place_ref[3] * 2 + place_ref[4]) * width
    entries = lax.broadcasted_iota(jnp.int32, own_ref.shape, 0) + first
    onehot = jnp.where(entries == ids_ref[...], mask, 0.0)
    grad = by_own * own_ref[...] + by_other * other_ref[...].astype(jnp.float32) - onehot
    grad_ref[...] = grad.astype(jnp.bfloat16)
    turned_ref[...] = grad.T.astype(jnp.bfloat16)


def logits_grad(place, own, other, own_stats, other_stats, ids, mask):
    width, toks = own.shape
    return pl.pallas_call(
        grad_kernel,
        out_shape=[
            jax.ShapeDtypeStruct((width, toks), jnp.bfloat16),
            jax.ShapeDtypeStruct((toks, width), jnp.bfloat16),
        ],
        in_specs=[SMEM] + [VMEM] * 6,
        out_specs=[VMEM, VMEM],
        compiler_params=params(5),
        cost_estimate=BRIEF,
    )(place, own, other, own_stats, other_stats, ids, mask)


def products_kernel(d, twin, place_ref, turned_ref, head_ref, *refs):
    *ins, out_ref = refs
    c = 1 - place_ref[4] if twin else place_ref[4]
    for e in range(4):
        at_x = (place_ref[2] + jnp.where(c == 0, d, e)) % 4
        at_y = (place_ref[3] + jnp.where(c == 0, e, d)) % 4
        columns = pl.ds(pl.multiple_of((c * 16 + at_x * 4 + at_y) * 256, 256), 256)
        part = jnp.dot(turned_ref[...], head_ref[:, columns], preferred_element_type=jnp.float32)
        if not twin:
            part += ins[0][e].astype(jnp.float32)
        out_ref[e] = part.astype(jnp.bfloat16)


def products(place, turned, head_t, d, received=None):
    toks = turned.shape[0]
    extra = [] if received is None else [received]
    return pl.pallas_call(
        functools.partial(products_kernel, d, received is None),
        out_shape=jax.ShapeDtypeStruct((4, toks, 256), jnp.bfloat16),
        in_specs=[SMEM] + [VMEM] * (2 + len(extra)),
        out_specs=VMEM,
        compiler_params=params(11),
        cost_estimate=BRIEF,
    )(place, turned, head_t, *extra)


def add_split_kernel(*refs):
    ins, outs = refs[:4], refs[4:]
    for d, out_ref in enumerate(outs):
        total = ins[0][d].astype(jnp.float32)
        for ref in ins[1:]:
            total += ref[d].astype(jnp.float32)
        out_ref[...] = total.astype(out_ref.dtype)


def add_split(*blocks):
    return pl.pallas_call(
        add_split_kernel,
        out_shape=[jax.ShapeDtypeStruct(blocks[0].shape[1:], blocks[0].dtype)] * 4,
        in_specs=[VMEM] * 4,
        out_specs=[VMEM] * 4,
        compiler_params=params(6),
        cost_estimate=BRIEF,
    )(*blocks)


def add_rows_kernel(place_ref, *refs):
    ins, outs, sum_ref = refs[:4], refs[4:8], refs[8]
    tok = place_ref[1]
    total = ins[0][...].astype(jnp.float32)
    for ref in ins[1:]:
        total += ref[...].astype(jnp.float32)
    sum_ref[...] = total.astype(sum_ref.dtype)
    block = outs[0].shape[0]
    for d, out_ref in enumerate(outs):
        out_ref[...] = sum_ref[pl.ds(pl.multiple_of((tok + d) % 4 * block, block), block), :]


def add_rows(place, blocks):
    toks, wide = blocks[0].shape
    return pl.pallas_call(
        add_rows_kernel,
        out_shape=[jax.ShapeDtypeStruct((toks // 4, wide), jnp.bfloat16)] * 4,
        in_specs=[SMEM] + [VMEM] * 4,
        out_specs=[VMEM] * 4,
        scratch_shapes=[pltpu.VMEM((toks, wide), jnp.bfloat16)],
        compiler_params=params(2),
        cost_estimate=BRIEF,
    )(place, *blocks)


def add_toks_kernel(place_ref, own_ref, *refs):
    ins, (keep_ref, give_ref) = refs[:4], refs[4:]
    even = place_ref[4] == 0
    first = jnp.where(even, ins[0][...].astype(jnp.float32), own_ref[...].astype(jnp.float32))
    total = first
    for ref in ins[1:]:
        total += ref[...].astype(jnp.float32)
    left, right = total[:, :128], total[:, 128:]
    keep_ref[...] = jnp.where(even, left, right).astype(keep_ref.dtype)
    give_ref[...] = jnp.where(even, right, left).astype(give_ref.dtype)


def add_toks(place, own, *received):
    rows, wide = own.shape
    return pl.pallas_call(
        add_toks_kernel,
        out_shape=[jax.ShapeDtypeStruct((rows, wide // 2), jnp.bfloat16)] * 2,
        in_specs=[SMEM] + [VMEM] * 5,
        out_specs=[VMEM] * 2,
        compiler_params=params(1),
        cost_estimate=BRIEF,
    )(place, own, *received)


def choose_kernel(place_ref, keep_ref, got_ref, out_ref):
    mine = place_ref[0] == place_ref[4]
    keep, got = keep_ref[...].astype(jnp.float32), got_ref[...].astype(jnp.float32)
    out_ref[...] = jnp.where(mine, keep, got).astype(out_ref.dtype)


def choose(place, keep, got):
    return pl.pallas_call(
        choose_kernel,
        out_shape=jax.ShapeDtypeStruct(keep.shape, keep.dtype),
        in_specs=[SMEM, VMEM, VMEM],
        out_specs=VMEM,
        compiler_params=params(1),
        cost_estimate=BRIEF,
    )(place, keep, got)


def head_grad_kernel(place_ref, grad_ref, own_ref, other_ref, sent_ref, twin_ref, out_ref):
    teacher = place_ref[0] == 0
    core = place_ref[4]

    def write(mine, others):
        for y in range(2):
            for ref, part in ((mine, core), (others, 1 - core)):
                columns = pl.ds(pl.multiple_of((y * 2 + part) * 256, 256), 256)
                out_ref[:, columns] = jnp.dot(
                    grad_ref[...], ref[0, :, 256 * y : 256 * y + 256], preferred_element_type=jnp.float32
                ).astype(jnp.bfloat16)

    @pl.when(teacher)
    def _():
        write(sent_ref, twin_ref)

    @pl.when(jnp.logical_not(teacher))
    def _():
        write(own_ref, other_ref)


def head_grad_half(place, grad, own, other, sent, twin):
    width, toks = grad.shape
    block = own.shape[2]
    second = pl.BlockSpec((1, toks, block // 2), lambda step, place: (2 + step // 2, 0, step % 2))
    first = pl.BlockSpec((1, toks, block // 2), lambda step, place: (step // 2, 0, step % 2))
    return pl.pallas_call(
        head_grad_kernel,
        grid_spec=pltpu.PrefetchScalarGridSpec(
            num_scalar_prefetch=1,
            grid=(4,),
            in_specs=[
                pl.BlockSpec((width, toks), lambda step, place: (0, 0)),
                second,
                second,
                first,
                first,
            ],
            out_specs=pl.BlockSpec((width, block), lambda step, place: (0, step)),
        ),
        out_shape=jax.ShapeDtypeStruct((width, 4 * block), jnp.bfloat16),
        compiler_params=params(8),
        cost_estimate=BRIEF,
    )(place, grad, own, other, sent, twin)


def spread(stats, name):
    far = send(stats, **{name: 2})
    near = send_by_core(stats, {name: 1}, {name: 3})
    return [stats, far, near, send(near, c=1)]


def on_device(hidden, head, token_ids, loss_mask):
    section, tok, vocab = (lax.axis_index(name) for name in AXES)
    place = jnp.stack([section, tok, vocab >> 3, (vocab >> 1) & 3, vocab & 1]).astype(jnp.int32)
    states = hidden[0]

    with jax.named_scope("gather_tok"):
        blocks = [states] + [send(states, t=d) for d in (1, 2, 3)]
        place, *blocks = lax.optimization_barrier((place, *blocks))
        block = jnp.stack(blocks)
    with jax.named_scope("gather_first"):
        blocks = [block] + [send_by_core(block, {"x": d}, {"y": d}) for d in (1, 2, 3)]
    with jax.named_scope("stage"):
        head_t, *blocks = lax.optimization_barrier((stage(head[0].T), *blocks))
    with jax.named_scope("gather_first"):
        block = jnp.stack(blocks)
    with jax.named_scope("gather_second"):
        own = [block] + [send_by_core(block, {"y": d}, {"x": d}) for d in (1, 2, 3)]
    with jax.named_scope("gather_cores"):
        other = [send(block, c=1) for block in own[:3]]
        own[3], *other = lax.optimization_barrier((own[3], *other))
        other.append(send(own[3], c=1))
    with jax.named_scope("student_hidden"):
        sent = send_both_ways(first_half(place, own))
    with jax.named_scope("own_logits"):
        hidden_own, part = own_logits(place, head_t, own)
    with jax.named_scope("logits"):
        hidden_other, scaled, short, local = logits_parts(place, head_t, other, part)

    with jax.named_scope("stats"):
        stats = merge(local, send(local, c=1))
        stats, short = lax.optimization_barrier((stats, short))
    with jax.named_scope("exchange_scaled"):
        other_short = send(short, s=1)
    with jax.named_scope("stats"):
        stats = merge(*spread(stats, "x"))
        stats, sent = lax.optimization_barrier((stats, sent))
    with jax.named_scope("student_hidden"):
        twin = send(sent, c=1)
    with jax.named_scope("stats"):
        stats = merge(*spread(stats, "y"))
        own_stats = local_scale(local, *spread(stats, "t"))
        other_stats = send(own_stats, s=1)

    with jax.named_scope("logits_grad"):
        grad, turned = logits_grad(
            place, scaled, other_short, own_stats, other_stats, token_ids[None], loss_mask[None]
        )
    turned, twin = lax.optimization_barrier((turned, twin))
    received, sums, firsts = {}, {}, []
    order = (("give", 1), ("give", 2), ("keep", 1), ("give", 3), ("keep", 2), ("give", 0), ("keep", 3), ("keep", 0))
    for part, d in order:
        with jax.named_scope("hidden_grad_" + part):
            if part == "give":
                give = products(place, turned, head_t, d)
                turned, give = lax.optimization_barrier((turned, give))
                received[d] = send(give, c=1)
            else:
                sums[d] = products(place, turned, head_t, d, received[d])
                turned, sums[d] = lax.optimization_barrier((turned, sums[d]))
                if d > 0:
                    firsts.append(send_by_core(sums[d], {"x": d}, {"y": d}))
    with jax.named_scope("head_grad"):
        head_out = head_grad_half(place, grad, hidden_own, hidden_other, sent, twin)
        firsts[0], head_out = lax.optimization_barrier((firsts[0], head_out))
    with jax.named_scope("reduce_second"):
        parts = add_split(sums[0], *firsts)
        seconds = [send_by_core(parts[d], {"y": d}, {"x": d}) for d in (1, 2, 3)]
    with jax.named_scope("reduce_tok"):
        rows = add_rows(place, [parts[0]] + seconds)
        received = [send(rows[0], s=1)]
        received += [send_by_core(rows[d], {"s": 1, "t": d}, {"t": d}) for d in (1, 2, 3)]
        keep, give = add_toks(place, rows[0], *received)
    with jax.named_scope("hidden_out"):
        hidden_out = choose(place, keep, send(give, c=1))
    return head_out.T, hidden_out


def solution(mesh):
    in_specs = (P("section", "tok", "vocab"), P("section", None, ("tok", "vocab")), P(), P())
    out_specs = (P("section", ("tok", "vocab")), P("tok", ("section", "vocab")))
    return jax.shard_map(
        on_device, mesh=mesh, in_specs=in_specs, out_specs=out_specs, check_vma=False
    )
```

```python
import functools
import jax
import jax.numpy as jnp
from jax import lax
from jax.experimental import pallas as pl
from jax.experimental.pallas import tpu as pltpu
from jax.sharding import PartitionSpec as P

AXES = ("section", "tok", "vocab")
SIZES = {"s": 2, "t": 4, "x": 4, "y": 4, "c": 2}
MIB = 1024 * 1024


def route(shift_of):
    names = list(SIZES)
    pairs = []
    for device in range(256):
        place, rest = {}, device
        for name in reversed(names):
            rest, place[name] = divmod(rest, SIZES[name])
        shift = shift_of(place)
        target = 0
        for name in names:
            target = target * SIZES[name] + (place[name] + shift.get(name, 0)) % SIZES[name]
        pairs.append((device, target))
    return pairs


def send(block, **shift):
    return lax.ppermute(block, AXES, route(lambda place: shift))


def send_by_core(block, even, odd):
    return lax.ppermute(block, AXES, route(lambda place: odd if place["c"] else even))


def send_both_ways(block):
    def shift_of(place):
        return {"s": 1, "t": (1 if place["s"] else 3) if place["c"] else 0}

    return lax.ppermute(block, AXES, route(shift_of))


def params(mib):
    return pltpu.CompilerParams(vmem_limit_bytes=mib * MIB)


BRIEF = pl.CostEstimate(flops=0, bytes_accessed=0, transcendentals=0)
VMEM = pl.BlockSpec(memory_space=pltpu.VMEM)
SMEM = pl.BlockSpec(memory_space=pltpu.SMEM)


def piece_columns(place_ref, core, d, e):
    at_x = (place_ref[2] + jnp.where(core == 0, d, e)) % 4
    at_y = (place_ref[3] + jnp.where(core == 0, e, d)) % 4
    return pl.ds(pl.multiple_of((core * 16 + at_x * 4 + at_y) * 256, 256), 256)


def stage_kernel(place_ref, head_ref, out_ref, *refs):
    gives, arrived = refs[:8], refs[8]
    copy = pltpu.make_async_copy(head_ref, out_ref, arrived)
    copy.start()
    for d in range(4):
        for e in range(4):
            columns = piece_columns(place_ref, 1 - place_ref[4], d, e)
            gives[2 * d + e // 2][:, e % 2 * 256 : e % 2 * 256 + 256] = head_ref[:, columns]
    copy.wait()


def stage(place, head_t):
    width, _ = head_t.shape
    return pl.pallas_call(
        stage_kernel,
        out_shape=[jax.ShapeDtypeStruct(head_t.shape, head_t.dtype)]
        + [jax.ShapeDtypeStruct((width, 512), head_t.dtype)] * 8,
        in_specs=[SMEM, VMEM],
        out_specs=[VMEM] * 9,
        scratch_shapes=[pltpu.SemaphoreType.DMA],
        compiler_params=params(22),
    )(place, head_t)


def first_half_kernel(place_ref, *refs):
    own, out_ref = refs[:4], refs[4]
    tok, x, y, c = place_ref[1], place_ref[2], place_ref[3], place_ref[4]
    _, _, rows, chunk = own[0].shape

    def lay(x_at, y_at, piece):
        columns = pl.ds(pl.multiple_of(y_at * chunk, chunk), chunk)
        for dt in range(4):
            at = pl.ds(pl.multiple_of((tok + 4 - dt) % 4 * rows, rows), rows)
            out_ref[x_at, at, columns] = piece(dt)

    for x_at in range(2):
        dx = (x + 4 - x_at) % 4

        @pl.when(c == 0)
        def _():
            for dy in range(4):
                lay(x_at, (y + 4 - dy) % 4, lambda dt: own[dy][dx, dt])

        for step in range(4):
            @pl.when(jnp.logical_and(c == 1, dx == step))
            def _():
                for dy in range(4):
                    lay(x_at, (y + 4 - dy) % 4, lambda dt: own[step][dy, dt])


def first_half(place, own):
    _, _, rows, chunk = own[0].shape
    return pl.pallas_call(
        first_half_kernel,
        out_shape=jax.ShapeDtypeStruct((2, 4 * rows, 4 * chunk), own[0].dtype),
        in_specs=[SMEM] + [VMEM] * 4,
        out_specs=VMEM,
        compiler_params=params(5),
        cost_estimate=BRIEF,
    )(place, *own)


def lay_out(place_ref, core, blocks, hidden_ref):
    tok, x, y = place_ref[1], place_ref[2], place_ref[3]
    _, _, rows, chunk = blocks[0].shape
    for late in range(4):
        for early in range(4):
            at_x = (x + 4 - jnp.where(core == 0, early, late)) % 4
            at_y = (y + 4 - jnp.where(core == 0, late, early)) % 4
            columns = pl.ds(pl.multiple_of(at_y * chunk, chunk), chunk)
            for dt in range(4):
                at = pl.ds(pl.multiple_of((tok + 4 - dt) % 4 * rows, rows), rows)
                hidden_ref[at_x, at, columns] = blocks[late][early, dt]


def add_products(core, head_ref, hidden_ref, acc_ref):
    chunk = hidden_ref.shape[2] // 4

    @pl.loop(0, 4)
    def _(x):
        total = acc_ref[...]
        for y in range(4):
            columns = pl.ds(pl.multiple_of(((x * 4 + y) * 2 + core) * chunk, chunk), chunk)
            total += lax.dot_general(
                head_ref[:, columns],
                hidden_ref[x, :, y * chunk : y * chunk + chunk],
                (((1,), (1,)), ((), ())),
                preferred_element_type=jnp.float32,
            )
        acc_ref[...] = total


def own_logits_kernel(place_ref, head_ref, *refs):
    own, (hidden_ref, acc_ref) = refs[:4], refs[4:]
    lay_out(place_ref, place_ref[4], own, hidden_ref)
    acc_ref[...] = jnp.zeros_like(acc_ref)
    add_products(place_ref[4], head_ref, hidden_ref, acc_ref)


def own_logits(place, head_t, own):
    width, _ = head_t.shape
    _, _, rows, chunk = own[0].shape
    toks = 4 * rows
    return pl.pallas_call(
        own_logits_kernel,
        out_shape=[
            jax.ShapeDtypeStruct((4, toks, 4 * chunk), jnp.bfloat16),
            jax.ShapeDtypeStruct((width, toks), jnp.float32),
        ],
        in_specs=[SMEM] + [VMEM] * 5,
        out_specs=[VMEM] * 2,
        compiler_params=params(16),
    )(place, head_t, *own)


def logits_kernel(place_ref, head_ref, *refs):
    other, part_ref = refs[:4], refs[4]
    hidden_ref, scaled_ref, short_ref, stats_ref, acc_ref = refs[5:]
    lay_out(place_ref, 1 - place_ref[4], other, hidden_ref)
    acc_ref[...] = part_ref[...]
    add_products(1 - place_ref[4], head_ref, hidden_ref, acc_ref)
    logits = acc_ref[...]
    peak = jnp.max(logits, axis=0, keepdims=True)
    shifted = logits - peak
    scaled = jnp.exp(shifted)
    scaled_ref[...] = scaled
    short_ref[...] = scaled.astype(jnp.bfloat16)
    stats_ref[0:1] = peak
    stats_ref[1:2] = jnp.sum(scaled, axis=0, keepdims=True)
    stats_ref[2:3] = jnp.sum(scaled * shifted, axis=0, keepdims=True)
    stats_ref[3:8] = jnp.zeros((5, peak.shape[1]), jnp.float32)


def logits_parts(place, head_t, other, part):
    width, toks = part.shape
    _, _, rows, chunk = other[0].shape
    return pl.pallas_call(
        logits_kernel,
        out_shape=[
            jax.ShapeDtypeStruct((4, toks, 4 * chunk), jnp.bfloat16),
            jax.ShapeDtypeStruct((width, toks), jnp.float32),
            jax.ShapeDtypeStruct((width, toks), jnp.bfloat16),
            jax.ShapeDtypeStruct((8, toks), jnp.float32),
        ],
        in_specs=[SMEM] + [VMEM] * 6,
        out_specs=[VMEM] * 4,
        scratch_shapes=[pltpu.VMEM((width, toks), jnp.float32)],
        compiler_params=params(17),
        cost_estimate=BRIEF,
    )(place, head_t, *other, part)


def merge_kernel(*refs):
    *ins, out_ref = refs
    peak = ins[0][0:1]
    for ref in ins[1:]:
        peak = jnp.maximum(peak, ref[0:1])
    total = jnp.zeros_like(peak)
    moment = jnp.zeros_like(peak)
    for ref in ins:
        drop = ref[0:1] - peak
        factor = jnp.exp(drop)
        total += factor * ref[1:2]
        moment += factor * (ref[2:3] + drop * ref[1:2])
    out_ref[0:1] = peak
    out_ref[1:2] = total
    out_ref[2:3] = moment
    out_ref[3:8] = jnp.zeros((5, peak.shape[1]), jnp.float32)


def merge(*stats):
    return pl.pallas_call(
        merge_kernel,
        out_shape=jax.ShapeDtypeStruct(stats[0].shape, jnp.float32),
        in_specs=[VMEM] * len(stats),
        out_specs=VMEM,
        compiler_params=params(1),
        cost_estimate=BRIEF,
    )(*stats)


def scale_kernel(local_ref, *refs):
    *ins, out_ref = refs
    peak = ins[0][0:1]
    for ref in ins[1:]:
        peak = jnp.maximum(peak, ref[0:1])
    total = jnp.zeros_like(peak)
    moment = jnp.zeros_like(peak)
    for ref in ins:
        drop = ref[0:1] - peak
        factor = jnp.exp(drop)
        total += factor * ref[1:2]
        moment += factor * (ref[2:3] + drop * ref[1:2])
    out_ref[0:1] = jnp.exp(local_ref[0:1] - peak) / total
    out_ref[1:2] = jnp.log(total) - moment / total
    out_ref[2:8] = jnp.zeros((6, peak.shape[1]), jnp.float32)


def local_scale(local, *stats):
    return pl.pallas_call(
        scale_kernel,
        out_shape=jax.ShapeDtypeStruct(local.shape, jnp.float32),
        in_specs=[VMEM] * (1 + len(stats)),
        out_specs=VMEM,
        compiler_params=params(1),
        cost_estimate=BRIEF,
    )(local, *stats)


def grad_kernel(place_ref, own_ref, other_ref, own_stats, other_stats, ids_ref, mask_ref, grad_ref, turned_ref):
    teacher = place_ref[0] == 0
    mask = mask_ref[...].astype(jnp.float32)
    entropy = jnp.where(teacher, own_stats[1:2], other_stats[1:2])
    by_own = jnp.where(teacher, -entropy, entropy + 1.0) * own_stats[0:1] * mask
    by_other = jnp.where(teacher, entropy + 1.0, -entropy) * other_stats[0:1] * mask
    width = own_ref.shape[0]
    first = ((place_ref[1] * 4 + place_ref[2]) * 8 + place_ref[3] * 2 + place_ref[4]) * width
    entries = lax.broadcasted_iota(jnp.int32, own_ref.shape, 0) + first
    onehot = jnp.where(entries == ids_ref[...], mask, 0.0)
    grad = by_own * own_ref[...] + by_other * other_ref[...].astype(jnp.float32) - onehot
    grad_ref[...] = grad.astype(jnp.bfloat16)
    turned_ref[...] = grad.T.astype(jnp.bfloat16)


def logits_grad(place, own, other, own_stats, other_stats, ids, mask):
    width, toks = own.shape
    return pl.pallas_call(
        grad_kernel,
        out_shape=[
            jax.ShapeDtypeStruct((width, toks), jnp.bfloat16),
            jax.ShapeDtypeStruct((toks, width), jnp.bfloat16),
        ],
        in_specs=[SMEM] + [VMEM] * 6,
        out_specs=[VMEM, VMEM],
        compiler_params=params(5),
        cost_estimate=BRIEF,
    )(place, own, other, own_stats, other_stats, ids, mask)


def own_products_kernel(d, place_ref, turned_ref, head_ref, out_ref):
    for e in range(4):
        out_ref[e] = jnp.dot(
            turned_ref[...],
            head_ref[:, piece_columns(place_ref, place_ref[4], d, e)],
            preferred_element_type=jnp.float32,
        )


def own_products(place, turned, head_t, d):
    return pl.pallas_call(
        functools.partial(own_products_kernel, d),
        out_shape=jax.ShapeDtypeStruct((4, turned.shape[0], 256), jnp.float32),
        in_specs=[SMEM, VMEM, VMEM],
        out_specs=VMEM,
        compiler_params=params(11),
        cost_estimate=BRIEF,
    )(place, turned, head_t)


def products_kernel(d, place_ref, turned_ref, head_ref, twin_ref, *refs):
    halves, parts, out_ref = refs[:2], refs[2:-1], refs[-1]
    for e in range(4):
        total = jnp.dot(
            twin_ref[...],
            halves[e // 2][:, e % 2 * 256 : e % 2 * 256 + 256],
            preferred_element_type=jnp.float32,
        )
        if parts:
            total += parts[0][e]
        else:
            total += jnp.dot(
                turned_ref[...],
                head_ref[:, piece_columns(place_ref, place_ref[4], d, e)],
                preferred_element_type=jnp.float32,
            )
        out_ref[e] = total.astype(jnp.bfloat16)


def products(place, turned, head_t, twin, halves, d, *parts):
    toks = turned.shape[0]
    return pl.pallas_call(
        functools.partial(products_kernel, d),
        out_shape=jax.ShapeDtypeStruct((4, toks, 256), jnp.bfloat16),
        in_specs=[SMEM] + [VMEM] * (5 + len(parts)),
        out_specs=VMEM,
        compiler_params=params(13),
        cost_estimate=BRIEF,
    )(place, turned, head_t, twin, *halves, *parts)


def add_split_kernel(*refs):
    ins, outs = refs[:4], refs[4:]
    for d, out_ref in enumerate(outs):
        total = ins[0][d].astype(jnp.float32)
        for ref in ins[1:]:
            total += ref[d].astype(jnp.float32)
        out_ref[...] = total.astype(out_ref.dtype)


def add_split(*blocks):
    return pl.pallas_call(
        add_split_kernel,
        out_shape=[jax.ShapeDtypeStruct(blocks[0].shape[1:], blocks[0].dtype)] * 4,
        in_specs=[VMEM] * 4,
        out_specs=[VMEM] * 4,
        compiler_params=params(6),
        cost_estimate=BRIEF,
    )(*blocks)


def add_rows_kernel(place_ref, *refs):
    ins, outs, sum_ref = refs[:4], refs[4:8], refs[8]
    tok = place_ref[1]
    total = ins[0][...].astype(jnp.float32)
    for ref in ins[1:]:
        total += ref[...].astype(jnp.float32)
    sum_ref[...] = total.astype(sum_ref.dtype)
    block = outs[0].shape[0]
    for d, out_ref in enumerate(outs):
        out_ref[...] = sum_ref[pl.ds(pl.multiple_of((tok + d) % 4 * block, block), block), :]


def add_rows(place, blocks):
    toks, wide = blocks[0].shape
    return pl.pallas_call(
        add_rows_kernel,
        out_shape=[jax.ShapeDtypeStruct((toks // 4, wide), jnp.bfloat16)] * 4,
        in_specs=[SMEM] + [VMEM] * 4,
        out_specs=[VMEM] * 4,
        scratch_shapes=[pltpu.VMEM((toks, wide), jnp.bfloat16)],
        compiler_params=params(2),
        cost_estimate=BRIEF,
    )(place, *blocks)


def add_toks_kernel(place_ref, own_ref, *refs):
    ins, (keep_ref, give_ref) = refs[:4], refs[4:]
    even = place_ref[4] == 0
    first = jnp.where(even, ins[0][...].astype(jnp.float32), own_ref[...].astype(jnp.float32))
    total = first
    for ref in ins[1:]:
        total += ref[...].astype(jnp.float32)
    left, right = total[:, :128], total[:, 128:]
    keep_ref[...] = jnp.where(even, left, right).astype(keep_ref.dtype)
    give_ref[...] = jnp.where(even, right, left).astype(give_ref.dtype)


def add_toks(place, own, *received):
    rows, wide = own.shape
    return pl.pallas_call(
        add_toks_kernel,
        out_shape=[jax.ShapeDtypeStruct((rows, wide // 2), jnp.bfloat16)] * 2,
        in_specs=[SMEM] + [VMEM] * 5,
        out_specs=[VMEM] * 2,
        compiler_params=params(1),
        cost_estimate=BRIEF,
    )(place, own, *received)


def choose_kernel(place_ref, keep_ref, got_ref, out_ref):
    mine = place_ref[0] == place_ref[4]
    keep, got = keep_ref[...].astype(jnp.float32), got_ref[...].astype(jnp.float32)
    out_ref[...] = jnp.where(mine, keep, got).astype(out_ref.dtype)


def choose(place, keep, got):
    return pl.pallas_call(
        choose_kernel,
        out_shape=jax.ShapeDtypeStruct(keep.shape, keep.dtype),
        in_specs=[SMEM, VMEM, VMEM],
        out_specs=VMEM,
        compiler_params=params(1),
        cost_estimate=BRIEF,
    )(place, keep, got)


def head_grad_kernel(place_ref, grad_ref, own_ref, other_ref, sent_ref, twin_ref, out_ref):
    teacher = place_ref[0] == 0
    core = place_ref[4]

    def write(mine, others):
        for y in range(2):
            for ref, part in ((mine, core), (others, 1 - core)):
                columns = pl.ds(pl.multiple_of((y * 2 + part) * 256, 256), 256)
                out_ref[:, columns] = jnp.dot(
                    grad_ref[...], ref[0, :, 256 * y : 256 * y + 256], preferred_element_type=jnp.float32
                ).astype(jnp.bfloat16)

    @pl.when(teacher)
    def _():
        write(sent_ref, twin_ref)

    @pl.when(jnp.logical_not(teacher))
    def _():
        write(own_ref, other_ref)


def head_grad_half(place, grad, own, other, sent, twin):
    width, toks = grad.shape
    block = own.shape[2]
    second = pl.BlockSpec((1, toks, block // 2), lambda step, place: (2 + step // 2, 0, step % 2))
    first = pl.BlockSpec((1, toks, block // 2), lambda step, place: (step // 2, 0, step % 2))
    return pl.pallas_call(
        head_grad_kernel,
        grid_spec=pltpu.PrefetchScalarGridSpec(
            num_scalar_prefetch=1,
            grid=(4,),
            in_specs=[
                pl.BlockSpec((width, toks), lambda step, place: (0, 0)),
                second,
                second,
                first,
                first,
            ],
            out_specs=pl.BlockSpec((width, block), lambda step, place: (0, step)),
        ),
        out_shape=jax.ShapeDtypeStruct((width, 4 * block), jnp.bfloat16),
        compiler_params=params(8),
        cost_estimate=BRIEF,
    )(place, grad, own, other, sent, twin)


def spread(stats, name):
    far = send(stats, **{name: 2})
    near = send_by_core(stats, {name: 1}, {name: 3})
    return [stats, far, near, send(near, c=1)]


def on_device(hidden, head, token_ids, loss_mask):
    section, tok, vocab = (lax.axis_index(name) for name in AXES)
    place = jnp.stack([section, tok, vocab >> 3, (vocab >> 1) & 3, vocab & 1]).astype(jnp.int32)
    states = hidden[0]

    with jax.named_scope("gather_tok"):
        blocks = [states] + [send(states, t=d) for d in (1, 2, 3)]
    with jax.named_scope("stage"):
        head_t, *halves = stage(place, head[0].T)
        head_t, *blocks = lax.optimization_barrier((head_t, *blocks))
        halves = [send(half, c=1) for half in halves]
    with jax.named_scope("gather_tok"):
        block = jnp.stack(blocks)
    with jax.named_scope("gather_first"):
        blocks = [block] + [send_by_core(block, {"x": d}, {"y": d}) for d in (1, 2, 3)]
    with jax.named_scope("gather_first"):
        block = jnp.stack(blocks)
    with jax.named_scope("gather_second"):
        own = [block] + [send_by_core(block, {"y": d}, {"x": d}) for d in (1, 2, 3)]
    own[1], halves = lax.optimization_barrier((own[1], halves))
    with jax.named_scope("gather_cores"):
        other = [send(block, c=1) for block in own[:3]]
        own[3], *other = lax.optimization_barrier((own[3], *other))
        other.append(send(own[3], c=1))
    with jax.named_scope("student_hidden"):
        sent = send_both_ways(first_half(place, own))
    with jax.named_scope("own_logits"):
        hidden_own, part = own_logits(place, head_t, own)
    with jax.named_scope("logits"):
        hidden_other, scaled, short, local = logits_parts(place, head_t, other, part)

    with jax.named_scope("stats"):
        stats = merge(local, send(local, c=1))
        stats, short = lax.optimization_barrier((stats, short))
    with jax.named_scope("exchange_scaled"):
        other_short = send(short, s=1)
    with jax.named_scope("stats"):
        stats = merge(*spread(stats, "x"))
        stats, sent = lax.optimization_barrier((stats, sent))
    with jax.named_scope("student_hidden"):
        twin = send(sent, c=1)
    with jax.named_scope("stats"):
        stats = merge(*spread(stats, "y"))
        own_stats = local_scale(local, *spread(stats, "t"))
        other_stats = send(own_stats, s=1)

    with jax.named_scope("logits_grad"):
        grad, turned = logits_grad(
            place, scaled, other_short, own_stats, other_stats, token_ids[None], loss_mask[None]
        )
    turned, twin = lax.optimization_barrier((turned, twin))
    sums, firsts = [], []
    with jax.named_scope("hidden_grad"):
        turned_twin = send(turned, c=1)
        part = own_products(place, turned, head_t, 1)
        part, turned_twin = lax.optimization_barrier((part, turned_twin))
        for d in (1, 2, 3, 0):
            parts = (part,) if d == 1 else ()
            if d == 0:
                turned, firsts[0] = lax.optimization_barrier((turned, firsts[0]))
            sums.append(products(place, turned, head_t, turned_twin, halves[2 * d : 2 * d + 2], d, *parts))
            turned, sums[-1] = lax.optimization_barrier((turned, sums[-1]))
            if d > 0:
                firsts.append(send_by_core(sums[-1], {"x": d}, {"y": d}))
    with jax.named_scope("head_grad"):
        head_out = head_grad_half(place, grad, hidden_own, hidden_other, sent, twin)
        firsts[1], head_out = lax.optimization_barrier((firsts[1], head_out))
    with jax.named_scope("reduce_second"):
        parts = add_split(sums[3], *firsts)
        seconds = [send_by_core(parts[d], {"y": d}, {"x": d}) for d in (1, 2, 3)]
    with jax.named_scope("reduce_tok"):
        rows = add_rows(place, [parts[0]] + seconds)
        received = [send(rows[0], s=1)]
        received += [send_by_core(rows[d], {"s": 1, "t": d}, {"t": d}) for d in (1, 2, 3)]
        keep, give = add_toks(place, rows[0], *received)
    with jax.named_scope("hidden_out"):
        hidden_out = choose(place, keep, send(give, c=1))
    return head_out.T, hidden_out


def solution(mesh):
    in_specs = (P("section", "tok", "vocab"), P("section", None, ("tok", "vocab")), P(), P())
    out_specs = (P("section", ("tok", "vocab")), P("tok", ("section", "vocab")))
    return jax.shard_map(
        on_device, mesh=mesh, in_specs=in_specs, out_specs=out_specs, check_vma=False
    )
```

```python
import functools
import jax
import jax.numpy as jnp
from jax import lax
from jax.experimental import pallas as pl
from jax.experimental.pallas import tpu as pltpu
from jax.sharding import PartitionSpec as P

AXES = ("section", "tok", "vocab")
SIZES = {"s": 2, "t": 4, "x": 4, "y": 4, "c": 2}
MIB = 1024 * 1024
SLOTS = (0, 1, 3, 2)


def route(shift_of):
    names = list(SIZES)
    pairs = []
    for device in range(256):
        place, rest = {}, device
        for name in reversed(names):
            rest, place[name] = divmod(rest, SIZES[name])
        shift = shift_of(place)
        target = 0
        for name in names:
            target = target * SIZES[name] + (place[name] + shift.get(name, 0)) % SIZES[name]
        pairs.append((device, target))
    return pairs


def send(block, **shift):
    return lax.ppermute(block, AXES, route(lambda place: shift))


def send_by_core(block, even, odd):
    return lax.ppermute(block, AXES, route(lambda place: odd if place["c"] else even))


def swap(block, name, bits, section_of=None):
    def shift_of(place):
        shift = {name: (place[name] ^ bits) - place[name]}
        if section_of is not None and place["c"] == section_of:
            shift["s"] = 1
        return shift

    return lax.ppermute(block, AXES, route(shift_of))


def send_both_ways(block):
    def shift_of(place):
        return {"s": 1, "t": (1 if place["s"] else 3) if place["c"] else 0}

    return lax.ppermute(block, AXES, route(shift_of))


def params(mib):
    return pltpu.CompilerParams(vmem_limit_bytes=mib * MIB)


BRIEF = pl.CostEstimate(flops=0, bytes_accessed=0, transcendentals=0)
VMEM = pl.BlockSpec(memory_space=pltpu.VMEM)
SMEM = pl.BlockSpec(memory_space=pltpu.SMEM)


def piece_columns(place_ref, core, d, e):
    at_x = (place_ref[2] + jnp.where(core == 0, d, e)) % 4
    at_y = (place_ref[3] + jnp.where(core == 0, e, d)) % 4
    return pl.ds(pl.multiple_of((core * 16 + at_x * 4 + at_y) * 256, 256), 256)


def stage_kernel(place_ref, head_ref, out_ref, *refs):
    gives, arrived = refs[:8], refs[8]
    copy = pltpu.make_async_copy(head_ref, out_ref, arrived)
    copy.start()
    for d in range(4):
        for e in range(4):
            columns = piece_columns(place_ref, 1 - place_ref[4], d, e)
            gives[2 * d + e // 2][:, e % 2 * 256 : e % 2 * 256 + 256] = head_ref[:, columns]
    copy.wait()


def stage(place, head_t):
    width, _ = head_t.shape
    return pl.pallas_call(
        stage_kernel,
        out_shape=[jax.ShapeDtypeStruct(head_t.shape, head_t.dtype)]
        + [jax.ShapeDtypeStruct((width, 512), head_t.dtype)] * 8,
        in_specs=[SMEM, VMEM],
        out_specs=[VMEM] * 9,
        scratch_shapes=[pltpu.SemaphoreType.DMA],
        compiler_params=params(22),
    )(place, head_t)


def first_half_kernel(place_ref, *refs):
    own, out_ref = refs[:4], refs[4]
    tok, x, y, c = place_ref[1], place_ref[2], place_ref[3], place_ref[4]
    _, _, rows, chunk = own[0].shape

    def lay(x_at, y_at, piece):
        columns = pl.ds(pl.multiple_of(y_at * chunk, chunk), chunk)
        for dt in range(4):
            at = pl.ds(pl.multiple_of((tok ^ SLOTS[dt]) * rows, rows), rows)
            out_ref[x_at, at, columns] = piece(dt)

    for x_at in range(2):
        dx = (x + 4 - x_at) % 4

        @pl.when(c == 0)
        def _():
            for dy in range(4):
                lay(x_at, (y + 4 - dy) % 4, lambda dt: own[dy][dx, dt])

        for step in range(4):
            @pl.when(jnp.logical_and(c == 1, dx == step))
            def _():
                for dy in range(4):
                    lay(x_at, (y + 4 - dy) % 4, lambda dt: own[step][dy, dt])


def first_half(place, own):
    _, _, rows, chunk = own[0].shape
    return pl.pallas_call(
        first_half_kernel,
        out_shape=jax.ShapeDtypeStruct((2, 4 * rows, 4 * chunk), own[0].dtype),
        in_specs=[SMEM] + [VMEM] * 4,
        out_specs=VMEM,
        compiler_params=params(5),
        cost_estimate=BRIEF,
    )(place, *own)


def lay_out(place_ref, core, blocks, hidden_ref):
    tok, x, y = place_ref[1], place_ref[2], place_ref[3]
    _, _, rows, chunk = blocks[0].shape
    for late in range(4):
        for early in range(4):
            at_x = (x + 4 - jnp.where(core == 0, early, late)) % 4
            at_y = (y + 4 - jnp.where(core == 0, late, early)) % 4
            columns = pl.ds(pl.multiple_of(at_y * chunk, chunk), chunk)
            for dt in range(4):
                at = pl.ds(pl.multiple_of((tok ^ SLOTS[dt]) * rows, rows), rows)
                hidden_ref[at_x, at, columns] = blocks[late][early, dt]


def add_products(core, head_ref, hidden_ref, acc_ref):
    chunk = hidden_ref.shape[2] // 4

    @pl.loop(0, 4)
    def _(x):
        total = acc_ref[...]
        for y in range(4):
            columns = pl.ds(pl.multiple_of(((x * 4 + y) * 2 + core) * chunk, chunk), chunk)
            total += lax.dot_general(
                head_ref[:, columns],
                hidden_ref[x, :, y * chunk : y * chunk + chunk],
                (((1,), (1,)), ((), ())),
                preferred_element_type=jnp.float32,
            )
        acc_ref[...] = total


def own_logits_kernel(place_ref, head_ref, *refs):
    own, (hidden_ref, acc_ref) = refs[:4], refs[4:]
    lay_out(place_ref, place_ref[4], own, hidden_ref)
    acc_ref[...] = jnp.zeros_like(acc_ref)
    add_products(place_ref[4], head_ref, hidden_ref, acc_ref)


def own_logits(place, head_t, own):
    width, _ = head_t.shape
    _, _, rows, chunk = own[0].shape
    toks = 4 * rows
    return pl.pallas_call(
        own_logits_kernel,
        out_shape=[
            jax.ShapeDtypeStruct((4, toks, 4 * chunk), jnp.bfloat16),
            jax.ShapeDtypeStruct((width, toks), jnp.float32),
        ],
        in_specs=[SMEM] + [VMEM] * 5,
        out_specs=[VMEM] * 2,
        compiler_params=params(16),
    )(place, head_t, *own)


def logits_kernel(place_ref, head_ref, *refs):
    other, part_ref = refs[:4], refs[4]
    hidden_ref, scaled_ref, short_ref, stats_ref, acc_ref = refs[5:]
    lay_out(place_ref, 1 - place_ref[4], other, hidden_ref)
    acc_ref[...] = part_ref[...]
    add_products(1 - place_ref[4], head_ref, hidden_ref, acc_ref)
    logits = acc_ref[...]
    peak = jnp.max(logits, axis=0, keepdims=True)
    shifted = logits - peak
    scaled = jnp.exp(shifted)
    scaled_ref[...] = scaled
    short_ref[...] = scaled.astype(jnp.bfloat16)
    stats_ref[0:1] = peak
    stats_ref[1:2] = jnp.sum(scaled, axis=0, keepdims=True)
    stats_ref[2:3] = jnp.sum(scaled * shifted, axis=0, keepdims=True)
    stats_ref[3:8] = jnp.zeros((5, peak.shape[1]), jnp.float32)


def logits_parts(place, head_t, other, part):
    width, toks = part.shape
    _, _, rows, chunk = other[0].shape
    return pl.pallas_call(
        logits_kernel,
        out_shape=[
            jax.ShapeDtypeStruct((4, toks, 4 * chunk), jnp.bfloat16),
            jax.ShapeDtypeStruct((width, toks), jnp.float32),
            jax.ShapeDtypeStruct((width, toks), jnp.bfloat16),
            jax.ShapeDtypeStruct((8, toks), jnp.float32),
        ],
        in_specs=[SMEM] + [VMEM] * 6,
        out_specs=[VMEM] * 4,
        scratch_shapes=[pltpu.VMEM((width, toks), jnp.float32)],
        compiler_params=params(17),
        cost_estimate=BRIEF,
    )(place, head_t, *other, part)


def merge_kernel(*refs):
    *ins, out_ref = refs
    peak = ins[0][0:1]
    for ref in ins[1:]:
        peak = jnp.maximum(peak, ref[0:1])
    total = jnp.zeros_like(peak)
    moment = jnp.zeros_like(peak)
    for ref in ins:
        drop = ref[0:1] - peak
        factor = jnp.exp(drop)
        total += factor * ref[1:2]
        moment += factor * (ref[2:3] + drop * ref[1:2])
    out_ref[0:1] = peak
    out_ref[1:2] = total
    out_ref[2:3] = moment
    out_ref[3:8] = jnp.zeros((5, peak.shape[1]), jnp.float32)


def merge(*stats):
    return pl.pallas_call(
        merge_kernel,
        out_shape=jax.ShapeDtypeStruct(stats[0].shape, jnp.float32),
        in_specs=[VMEM] * len(stats),
        out_specs=VMEM,
        compiler_params=params(1),
        cost_estimate=BRIEF,
    )(*stats)


def scale_kernel(local_ref, *refs):
    *ins, out_ref = refs
    peak = ins[0][0:1]
    for ref in ins[1:]:
        peak = jnp.maximum(peak, ref[0:1])
    total = jnp.zeros_like(peak)
    moment = jnp.zeros_like(peak)
    for ref in ins:
        drop = ref[0:1] - peak
        factor = jnp.exp(drop)
        total += factor * ref[1:2]
        moment += factor * (ref[2:3] + drop * ref[1:2])
    out_ref[0:1] = jnp.exp(local_ref[0:1] - peak) / total
    out_ref[1:2] = jnp.log(total) - moment / total
    out_ref[2:8] = jnp.zeros((6, peak.shape[1]), jnp.float32)


def local_scale(local, *stats):
    return pl.pallas_call(
        scale_kernel,
        out_shape=jax.ShapeDtypeStruct(local.shape, jnp.float32),
        in_specs=[VMEM] * (1 + len(stats)),
        out_specs=VMEM,
        compiler_params=params(1),
        cost_estimate=BRIEF,
    )(local, *stats)


def grad_kernel(place_ref, own_ref, other_ref, own_stats, other_stats, ids_ref, mask_ref, grad_ref, turned_ref):
    teacher = place_ref[0] == 0
    mask = mask_ref[...].astype(jnp.float32)
    entropy = jnp.where(teacher, own_stats[1:2], other_stats[1:2])
    by_own = jnp.where(teacher, -entropy, entropy + 1.0) * own_stats[0:1] * mask
    by_other = jnp.where(teacher, entropy + 1.0, -entropy) * other_stats[0:1] * mask
    width = own_ref.shape[0]
    first = ((place_ref[1] * 4 + place_ref[2]) * 8 + place_ref[3] * 2 + place_ref[4]) * width
    entries = lax.broadcasted_iota(jnp.int32, own_ref.shape, 0) + first
    onehot = jnp.where(entries == ids_ref[...], mask, 0.0)
    grad = by_own * own_ref[...] + by_other * other_ref[...].astype(jnp.float32) - onehot
    grad_ref[...] = grad.astype(jnp.bfloat16)
    turned_ref[...] = grad.T.astype(jnp.bfloat16)


def logits_grad(place, own, other, own_stats, other_stats, ids, mask):
    width, toks = own.shape
    return pl.pallas_call(
        grad_kernel,
        out_shape=[
            jax.ShapeDtypeStruct((width, toks), jnp.bfloat16),
            jax.ShapeDtypeStruct((toks, width), jnp.bfloat16),
        ],
        in_specs=[SMEM] + [VMEM] * 6,
        out_specs=[VMEM, VMEM],
        compiler_params=params(5),
        cost_estimate=BRIEF,
    )(place, own, other, own_stats, other_stats, ids, mask)


def own_products_kernel(d, place_ref, turned_ref, head_ref, out_ref):
    for e in range(4):
        out_ref[e] = jnp.dot(
            turned_ref[...],
            head_ref[:, piece_columns(place_ref, place_ref[4], d, e)],
            preferred_element_type=jnp.float32,
        )


def own_products(place, turned, head_t, d):
    return pl.pallas_call(
        functools.partial(own_products_kernel, d),
        out_shape=jax.ShapeDtypeStruct((4, turned.shape[0], 256), jnp.float32),
        in_specs=[SMEM, VMEM, VMEM],
        out_specs=VMEM,
        compiler_params=params(11),
        cost_estimate=BRIEF,
    )(place, turned, head_t)


def products_kernel(d, place_ref, turned_ref, head_ref, twin_ref, *refs):
    halves, parts, out_ref = refs[:2], refs[2:-1], refs[-1]
    for e in range(4):
        total = jnp.dot(
            twin_ref[...],
            halves[e // 2][:, e % 2 * 256 : e % 2 * 256 + 256],
            preferred_element_type=jnp.float32,
        )
        if parts:
            total += parts[0][e]
        else:
            total += jnp.dot(
                turned_ref[...],
                head_ref[:, piece_columns(place_ref, place_ref[4], d, e)],
                preferred_element_type=jnp.float32,
            )
        out_ref[e] = total.astype(jnp.bfloat16)


def products(place, turned, head_t, twin, halves, d, *parts):
    toks = turned.shape[0]
    return pl.pallas_call(
        functools.partial(products_kernel, d),
        out_shape=jax.ShapeDtypeStruct((4, toks, 256), jnp.bfloat16),
        in_specs=[SMEM] + [VMEM] * (5 + len(parts)),
        out_specs=VMEM,
        compiler_params=params(13),
        cost_estimate=BRIEF,
    )(place, turned, head_t, twin, *halves, *parts)


def add_split_kernel(*refs):
    ins, outs = refs[:4], refs[4:]
    for d, out_ref in enumerate(outs):
        total = ins[0][d].astype(jnp.float32)
        for ref in ins[1:]:
            total += ref[d].astype(jnp.float32)
        out_ref[...] = total.astype(out_ref.dtype)


def add_split(*blocks):
    return pl.pallas_call(
        add_split_kernel,
        out_shape=[jax.ShapeDtypeStruct(blocks[0].shape[1:], blocks[0].dtype)] * 4,
        in_specs=[VMEM] * 4,
        out_specs=[VMEM] * 4,
        compiler_params=params(6),
        cost_estimate=BRIEF,
    )(*blocks)


def add_rows_kernel(place_ref, *refs):
    ins, (keep_ref, give_ref, sum_ref) = refs[:4], refs[4:]
    upper = place_ref[1] // 2
    total = ins[0][...].astype(jnp.float32)
    for ref in ins[1:]:
        total += ref[...].astype(jnp.float32)
    sum_ref[...] = total.astype(sum_ref.dtype)
    half = keep_ref.shape[0]
    keep_ref[...] = sum_ref[pl.ds(pl.multiple_of(upper * half, half), half), :]
    give_ref[...] = sum_ref[pl.ds(pl.multiple_of((1 - upper) * half, half), half), :]


def add_rows(place, blocks):
    toks, wide = blocks[0].shape
    return pl.pallas_call(
        add_rows_kernel,
        out_shape=[jax.ShapeDtypeStruct((toks // 2, wide), jnp.bfloat16)] * 2,
        in_specs=[SMEM] + [VMEM] * 4,
        out_specs=[VMEM] * 2,
        scratch_shapes=[pltpu.VMEM((toks, wide), jnp.bfloat16)],
        compiler_params=params(2),
        cost_estimate=BRIEF,
    )(place, *blocks)


def add_pair_kernel(place_ref, own_ref, got_ref, keep_ref, give_ref, sum_ref):
    odd = place_ref[1] % 2
    sum_ref[...] = own_ref[...].astype(jnp.float32) + got_ref[...].astype(jnp.float32)
    block = keep_ref.shape[0]
    keep_ref[...] = sum_ref[pl.ds(pl.multiple_of(odd * block, block), block), :].astype(keep_ref.dtype)
    give_ref[...] = sum_ref[pl.ds(pl.multiple_of((1 - odd) * block, block), block), :].astype(give_ref.dtype)


def add_pair(place, own, got):
    rows, wide = own.shape
    return pl.pallas_call(
        add_pair_kernel,
        out_shape=[jax.ShapeDtypeStruct((rows // 2, wide), jnp.bfloat16)] * 2,
        in_specs=[SMEM] + [VMEM] * 2,
        out_specs=[VMEM] * 2,
        scratch_shapes=[pltpu.VMEM((rows, wide), jnp.float32)],
        compiler_params=params(2),
        cost_estimate=BRIEF,
    )(place, own, got)


def add_toks_kernel(place_ref, own_ref, straight_ref, crossed_ref, keep_ref, give_ref):
    even = place_ref[4] == 0
    first = jnp.where(even, straight_ref[...].astype(jnp.float32), own_ref[...].astype(jnp.float32))
    total = first + crossed_ref[...].astype(jnp.float32)
    left, right = total[:, :128], total[:, 128:]
    keep_ref[...] = jnp.where(even, left, right).astype(keep_ref.dtype)
    give_ref[...] = jnp.where(even, right, left).astype(give_ref.dtype)


def add_toks(place, own, straight, crossed):
    rows, wide = own.shape
    return pl.pallas_call(
        add_toks_kernel,
        out_shape=[jax.ShapeDtypeStruct((rows, wide // 2), jnp.bfloat16)] * 2,
        in_specs=[SMEM] + [VMEM] * 3,
        out_specs=[VMEM] * 2,
        compiler_params=params(1),
        cost_estimate=BRIEF,
    )(place, own, straight, crossed)


def choose_kernel(place_ref, keep_ref, got_ref, out_ref):
    mine = place_ref[0] == place_ref[4]
    keep, got = keep_ref[...].astype(jnp.float32), got_ref[...].astype(jnp.float32)
    out_ref[...] = jnp.where(mine, keep, got).astype(out_ref.dtype)


def choose(place, keep, got):
    return pl.pallas_call(
        choose_kernel,
        out_shape=jax.ShapeDtypeStruct(keep.shape, keep.dtype),
        in_specs=[SMEM, VMEM, VMEM],
        out_specs=VMEM,
        compiler_params=params(1),
        cost_estimate=BRIEF,
    )(place, keep, got)


def head_grad_kernel(place_ref, grad_ref, own_ref, other_ref, sent_ref, twin_ref, out_ref):
    teacher = place_ref[0] == 0
    core = place_ref[4]

    def write(mine, others):
        for y in range(2):
            for ref, part in ((mine, core), (others, 1 - core)):
                columns = pl.ds(pl.multiple_of((y * 2 + part) * 256, 256), 256)
                out_ref[:, columns] = jnp.dot(
                    grad_ref[...], ref[0, :, 256 * y : 256 * y + 256], preferred_element_type=jnp.float32
                ).astype(jnp.bfloat16)

    @pl.when(teacher)
    def _():
        write(sent_ref, twin_ref)

    @pl.when(jnp.logical_not(teacher))
    def _():
        write(own_ref, other_ref)


def head_grad_half(place, grad, own, other, sent, twin):
    width, toks = grad.shape
    block = own.shape[2]
    second = pl.BlockSpec((1, toks, block // 2), lambda step, place: (2 + step // 2, 0, step % 2))
    first = pl.BlockSpec((1, toks, block // 2), lambda step, place: (step // 2, 0, step % 2))
    return pl.pallas_call(
        head_grad_kernel,
        grid_spec=pltpu.PrefetchScalarGridSpec(
            num_scalar_prefetch=1,
            grid=(4,),
            in_specs=[
                pl.BlockSpec((width, toks), lambda step, place: (0, 0)),
                second,
                second,
                first,
                first,
            ],
            out_specs=pl.BlockSpec((width, block), lambda step, place: (0, step)),
        ),
        out_shape=jax.ShapeDtypeStruct((width, 4 * block), jnp.bfloat16),
        compiler_params=params(8),
        cost_estimate=BRIEF,
    )(place, grad, own, other, sent, twin)


def on_device(hidden, head, token_ids, loss_mask):
    section, tok, vocab = (lax.axis_index(name) for name in AXES)
    place = jnp.stack([section, tok, vocab >> 3, (vocab >> 1) & 3, vocab & 1]).astype(jnp.int32)
    states = hidden[0]

    with jax.named_scope("gather_tok"):
        pair = jnp.stack([states, swap(states, "t", 1)])
        pair, place = lax.optimization_barrier((pair, place))
        blocks = [pair, swap(pair, "t", 3)]
    with jax.named_scope("stage"):
        head_t, *halves = stage(place, head[0].T)
        head_t, *blocks = lax.optimization_barrier((head_t, *blocks))
        halves = [send(half, c=1) for half in halves]
    with jax.named_scope("gather_tok"):
        block = jnp.concatenate(blocks)
    with jax.named_scope("gather_first"):
        blocks = [block] + [send_by_core(block, {"x": d}, {"y": d}) for d in (1, 2, 3)]
    with jax.named_scope("gather_first"):
        block = jnp.stack(blocks)
    with jax.named_scope("gather_second"):
        own = [block] + [send_by_core(block, {"y": d}, {"x": d}) for d in (1, 2, 3)]
    own[1], halves = lax.optimization_barrier((own[1], halves))
    with jax.named_scope("gather_cores"):
        other = [send(block, c=1) for block in own[:3]]
        own[3], *other = lax.optimization_barrier((own[3], *other))
        other.append(send(own[3], c=1))
    with jax.named_scope("student_hidden"):
        sent = send_both_ways(first_half(place, own))
    with jax.named_scope("own_logits"):
        hidden_own, part = own_logits(place, head_t, own)
    with jax.named_scope("logits"):
        hidden_other, scaled, short, local = logits_parts(place, head_t, other, part)

    with jax.named_scope("stats"):
        stats = merge(local, send(local, c=1))
        stats, short = lax.optimization_barrier((stats, short))
    with jax.named_scope("exchange_scaled"):
        other_short = send(short, s=1)
    with jax.named_scope("stats"):
        stats = merge(stats, swap(stats, "x", 1))
        stats = merge(stats, swap(stats, "x", 3))
        stats, sent = lax.optimization_barrier((stats, sent))
    with jax.named_scope("student_hidden"):
        twin = send(sent, c=1)
    with jax.named_scope("stats"):
        stats = merge(stats, swap(stats, "y", 1))
        stats = merge(stats, swap(stats, "y", 3))
        stats = merge(stats, swap(stats, "t", 3))
        own_stats = local_scale(local, stats, swap(stats, "t", 1))
        other_stats = send(own_stats, s=1)

    with jax.named_scope("logits_grad"):
        grad, turned = logits_grad(
            place, scaled, other_short, own_stats, other_stats, token_ids[None], loss_mask[None]
        )
    turned, twin = lax.optimization_barrier((turned, twin))
    sums, firsts = [], []
    with jax.named_scope("hidden_grad"):
        turned_twin = send(turned, c=1)
        part = own_products(place, turned, head_t, 1)
        part, turned_twin = lax.optimization_barrier((part, turned_twin))
        for d in (1, 2, 3, 0):
            parts = (part,) if d == 1 else ()
            if d == 0:
                turned, *firsts[:2] = lax.optimization_barrier((turned, *firsts[:2]))
            sums.append(products(place, turned, head_t, turned_twin, halves[2 * d : 2 * d + 2], d, *parts))
            turned, sums[-1] = lax.optimization_barrier((turned, sums[-1]))
            if d > 0:
                firsts.append(send_by_core(sums[-1], {"x": d}, {"y": d}))
    with jax.named_scope("head_grad"):
        head_out = head_grad_half(place, grad, hidden_own, hidden_other, sent, twin)
        firsts[2], head_out = lax.optimization_barrier((firsts[2], head_out))
    with jax.named_scope("reduce_second"):
        parts = add_split(sums[3], *firsts)
        seconds = [send_by_core(parts[d], {"y": d}, {"x": d}) for d in (1, 2, 3)]
    with jax.named_scope("reduce_tok"):
        keep, give = add_rows(place, [parts[0]] + seconds)
        keep, give = add_pair(place, keep, swap(give, "t", 3))
        keep, give = add_toks(place, keep, send(keep, s=1), swap(give, "t", 1, section_of=0))
    with jax.named_scope("hidden_out"):
        hidden_out = choose(place, keep, send(give, c=1))
    return head_out.T, hidden_out


def solution(mesh):
    in_specs = (P("section", "tok", "vocab"), P("section", None, ("tok", "vocab")), P(), P())
    out_specs = (P("section", ("tok", "vocab")), P("tok", ("section", "vocab")))
    return jax.shard_map(
        on_device, mesh=mesh, in_specs=in_specs, out_specs=out_specs, check_vma=False
    )
```

```python
import functools
import jax
import jax.numpy as jnp
from jax import lax
from jax.experimental import pallas as pl
from jax.experimental.pallas import tpu as pltpu
from jax.sharding import PartitionSpec as P

AXES = ("section", "tok", "vocab")
SIZES = {"s": 2, "t": 4, "x": 4, "y": 4, "c": 2}
MIB = 1024 * 1024


def route(shift_of):
    names = list(SIZES)
    pairs = []
    for device in range(256):
        place, rest = {}, device
        for name in reversed(names):
            rest, place[name] = divmod(rest, SIZES[name])
        shift = shift_of(place)
        target = 0
        for name in names:
            target = target * SIZES[name] + (place[name] + shift.get(name, 0)) % SIZES[name]
        pairs.append((device, target))
    return pairs


def send(block, **shift):
    return lax.ppermute(block, AXES, route(lambda place: shift))


def send_by_core(block, even, odd):
    return lax.ppermute(block, AXES, route(lambda place: odd if place["c"] else even))


def send_both_ways(block):
    def shift_of(place):
        return {"s": 1, "t": (1 if place["s"] else 3) if place["c"] else 0}

    return lax.ppermute(block, AXES, route(shift_of))


def params(mib):
    return pltpu.CompilerParams(vmem_limit_bytes=mib * MIB)


BRIEF = pl.CostEstimate(flops=0, bytes_accessed=0, transcendentals=0)
VMEM = pl.BlockSpec(memory_space=pltpu.VMEM)
SMEM = pl.BlockSpec(memory_space=pltpu.SMEM)


def piece_columns(place_ref, core, d, e):
    at_x = (place_ref[2] + jnp.where(core == 0, d, e)) % 4
    at_y = (place_ref[3] + jnp.where(core == 0, e, d)) % 4
    return pl.ds(pl.multiple_of((core * 16 + at_x * 4 + at_y) * 256, 256), 256)


def stage_kernel(place_ref, head_ref, out_ref, *refs):
    gives, arrived = refs[:8], refs[8]
    copy = pltpu.make_async_copy(head_ref, out_ref, arrived)
    copy.start()
    for d in range(4):
        for e in range(4):
            columns = piece_columns(place_ref, 1 - place_ref[4], d, e)
            gives[2 * d + e // 2][:, e % 2 * 256 : e % 2 * 256 + 256] = head_ref[:, columns]
    copy.wait()


def stage(place, head_t):
    width, _ = head_t.shape
    return pl.pallas_call(
        stage_kernel,
        out_shape=[jax.ShapeDtypeStruct(head_t.shape, head_t.dtype)]
        + [jax.ShapeDtypeStruct((width, 512), head_t.dtype)] * 8,
        in_specs=[SMEM, VMEM],
        out_specs=[VMEM] * 9,
        scratch_shapes=[pltpu.SemaphoreType.DMA],
        compiler_params=params(22),
    )(place, head_t)


def first_half_kernel(place_ref, *refs):
    own, out_ref = refs[:4], refs[4]
    tok, x, y, c = place_ref[1], place_ref[2], place_ref[3], place_ref[4]
    _, _, rows, chunk = own[0].shape

    def lay(x_at, y_at, piece):
        columns = pl.ds(pl.multiple_of(y_at * chunk, chunk), chunk)
        for dt in range(4):
            at = pl.ds(pl.multiple_of((tok + 4 - dt) % 4 * rows, rows), rows)
            out_ref[x_at, at, columns] = piece(dt)

    for x_at in range(2):
        dx = (x + 4 - x_at) % 4

        @pl.when(c == 0)
        def _():
            for dy in range(4):
                lay(x_at, (y + 4 - dy) % 4, lambda dt: own[dy][dx, dt])

        for step in range(4):
            @pl.when(jnp.logical_and(c == 1, dx == step))
            def _():
                for dy in range(4):
                    lay(x_at, (y + 4 - dy) % 4, lambda dt: own[step][dy, dt])


def first_half(place, own):
    _, _, rows, chunk = own[0].shape
    return pl.pallas_call(
        first_half_kernel,
        out_shape=jax.ShapeDtypeStruct((2, 4 * rows, 4 * chunk), own[0].dtype),
        in_specs=[SMEM] + [VMEM] * 4,
        out_specs=VMEM,
        compiler_params=params(5),
        cost_estimate=BRIEF,
    )(place, *own)


def lay_out(place_ref, core, blocks, hidden_ref):
    tok, x, y = place_ref[1], place_ref[2], place_ref[3]
    _, _, rows, chunk = blocks[0].shape
    for late in range(4):
        for early in range(4):
            at_x = (x + 4 - jnp.where(core == 0, early, late)) % 4
            at_y = (y + 4 - jnp.where(core == 0, late, early)) % 4
            columns = pl.ds(pl.multiple_of(at_y * chunk, chunk), chunk)
            for dt in range(4):
                at = pl.ds(pl.multiple_of((tok + 4 - dt) % 4 * rows, rows), rows)
                hidden_ref[at_x, at, columns] = blocks[late][early, dt]


def add_products(core, head_ref, hidden_ref, acc_ref):
    chunk = hidden_ref.shape[2] // 4

    @pl.loop(0, 4)
    def _(x):
        total = acc_ref[...]
        for y in range(4):
            columns = pl.ds(pl.multiple_of(((x * 4 + y) * 2 + core) * chunk, chunk), chunk)
            total += lax.dot_general(
                head_ref[:, columns],
                hidden_ref[x, :, y * chunk : y * chunk + chunk],
                (((1,), (1,)), ((), ())),
                preferred_element_type=jnp.float32,
            )
        acc_ref[...] = total


def own_logits_kernel(place_ref, head_ref, *refs):
    own, (hidden_ref, acc_ref) = refs[:4], refs[4:]
    lay_out(place_ref, place_ref[4], own, hidden_ref)
    acc_ref[...] = jnp.zeros_like(acc_ref)
    add_products(place_ref[4], head_ref, hidden_ref, acc_ref)


def own_logits(place, head_t, own):
    width, _ = head_t.shape
    _, _, rows, chunk = own[0].shape
    toks = 4 * rows
    return pl.pallas_call(
        own_logits_kernel,
        out_shape=[
            jax.ShapeDtypeStruct((4, toks, 4 * chunk), jnp.bfloat16),
            jax.ShapeDtypeStruct((width, toks), jnp.float32),
        ],
        in_specs=[SMEM] + [VMEM] * 5,
        out_specs=[VMEM] * 2,
        compiler_params=params(16),
    )(place, head_t, *own)


def logits_kernel(place_ref, head_ref, *refs):
    other, part_ref = refs[:4], refs[4]
    hidden_ref, scaled_ref, short_ref, stats_ref, acc_ref = refs[5:]
    lay_out(place_ref, 1 - place_ref[4], other, hidden_ref)
    acc_ref[...] = part_ref[...]
    add_products(1 - place_ref[4], head_ref, hidden_ref, acc_ref)
    logits = acc_ref[...]
    peak = jnp.max(logits, axis=0, keepdims=True)
    shifted = logits - peak
    scaled = jnp.exp(shifted)
    scaled_ref[...] = scaled
    short_ref[...] = scaled.astype(jnp.bfloat16)
    stats_ref[0:1] = peak
    stats_ref[1:2] = jnp.sum(scaled, axis=0, keepdims=True)
    stats_ref[2:3] = jnp.sum(scaled * shifted, axis=0, keepdims=True)
    stats_ref[3:8] = jnp.zeros((5, peak.shape[1]), jnp.float32)


def logits_parts(place, head_t, other, part):
    width, toks = part.shape
    _, _, rows, chunk = other[0].shape
    return pl.pallas_call(
        logits_kernel,
        out_shape=[
            jax.ShapeDtypeStruct((4, toks, 4 * chunk), jnp.bfloat16),
            jax.ShapeDtypeStruct((width, toks), jnp.float32),
            jax.ShapeDtypeStruct((width, toks), jnp.bfloat16),
            jax.ShapeDtypeStruct((8, toks), jnp.float32),
        ],
        in_specs=[SMEM] + [VMEM] * 6,
        out_specs=[VMEM] * 4,
        scratch_shapes=[pltpu.VMEM((width, toks), jnp.float32)],
        compiler_params=params(17),
        cost_estimate=BRIEF,
    )(place, head_t, *other, part)


def merge_kernel(*refs):
    *ins, out_ref = refs
    peak = ins[0][0:1]
    for ref in ins[1:]:
        peak = jnp.maximum(peak, ref[0:1])
    total = jnp.zeros_like(peak)
    moment = jnp.zeros_like(peak)
    for ref in ins:
        drop = ref[0:1] - peak
        factor = jnp.exp(drop)
        total += factor * ref[1:2]
        moment += factor * (ref[2:3] + drop * ref[1:2])
    out_ref[0:1] = peak
    out_ref[1:2] = total
    out_ref[2:3] = moment
    out_ref[3:8] = jnp.zeros((5, peak.shape[1]), jnp.float32)


def merge(*stats):
    return pl.pallas_call(
        merge_kernel,
        out_shape=jax.ShapeDtypeStruct(stats[0].shape, jnp.float32),
        in_specs=[VMEM] * len(stats),
        out_specs=VMEM,
        compiler_params=params(1),
        cost_estimate=BRIEF,
    )(*stats)


def scale_kernel(local_ref, *refs):
    *ins, out_ref = refs
    peak = ins[0][0:1]
    for ref in ins[1:]:
        peak = jnp.maximum(peak, ref[0:1])
    total = jnp.zeros_like(peak)
    moment = jnp.zeros_like(peak)
    for ref in ins:
        drop = ref[0:1] - peak
        factor = jnp.exp(drop)
        total += factor * ref[1:2]
        moment += factor * (ref[2:3] + drop * ref[1:2])
    out_ref[0:1] = jnp.exp(local_ref[0:1] - peak) / total
    out_ref[1:2] = jnp.log(total) - moment / total
    out_ref[2:8] = jnp.zeros((6, peak.shape[1]), jnp.float32)


def local_scale(local, *stats):
    return pl.pallas_call(
        scale_kernel,
        out_shape=jax.ShapeDtypeStruct(local.shape, jnp.float32),
        in_specs=[VMEM] * (1 + len(stats)),
        out_specs=VMEM,
        compiler_params=params(1),
        cost_estimate=BRIEF,
    )(local, *stats)


def grad_kernel(place_ref, own_ref, other_ref, own_stats, other_stats, ids_ref, mask_ref, grad_ref, turned_ref):
    teacher = place_ref[0] == 0
    mask = mask_ref[...].astype(jnp.float32)
    entropy = jnp.where(teacher, own_stats[1:2], other_stats[1:2])
    by_own = jnp.where(teacher, -entropy, entropy + 1.0) * own_stats[0:1] * mask
    by_other = jnp.where(teacher, entropy + 1.0, -entropy) * other_stats[0:1] * mask
    width = own_ref.shape[0]
    first = ((place_ref[1] * 4 + place_ref[2]) * 8 + place_ref[3] * 2 + place_ref[4]) * width
    entries = lax.broadcasted_iota(jnp.int32, own_ref.shape, 0) + first
    onehot = jnp.where(entries == ids_ref[...], mask, 0.0)
    grad = by_own * own_ref[...] + by_other * other_ref[...].astype(jnp.float32) - onehot
    grad_ref[...] = grad.astype(jnp.bfloat16)
    turned_ref[...] = grad.T.astype(jnp.bfloat16)


def logits_grad(place, own, other, own_stats, other_stats, ids, mask):
    width, toks = own.shape
    return pl.pallas_call(
        grad_kernel,
        out_shape=[
            jax.ShapeDtypeStruct((width, toks), jnp.bfloat16),
            jax.ShapeDtypeStruct((toks, width), jnp.bfloat16),
        ],
        in_specs=[SMEM] + [VMEM] * 6,
        out_specs=[VMEM, VMEM],
        compiler_params=params(5),
        cost_estimate=BRIEF,
    )(place, own, other, own_stats, other_stats, ids, mask)


def own_products_kernel(d, place_ref, turned_ref, head_ref, out_ref):
    for e in range(4):
        out_ref[e] = jnp.dot(
            turned_ref[...],
            head_ref[:, piece_columns(place_ref, place_ref[4], d, e)],
            preferred_element_type=jnp.float32,
        )


def own_products(place, turned, head_t, d):
    return pl.pallas_call(
        functools.partial(own_products_kernel, d),
        out_shape=jax.ShapeDtypeStruct((4, turned.shape[0], 256), jnp.float32),
        in_specs=[SMEM, VMEM, VMEM],
        out_specs=VMEM,
        compiler_params=params(11),
        cost_estimate=BRIEF,
    )(place, turned, head_t)


def products_kernel(d, place_ref, turned_ref, head_ref, twin_ref, *refs):
    halves, parts, out_ref = refs[:2], refs[2:-1], refs[-1]
    for e in range(4):
        total = jnp.dot(
            twin_ref[...],
            halves[e // 2][:, e % 2 * 256 : e % 2 * 256 + 256],
            preferred_element_type=jnp.float32,
        )
        if parts:
            total += parts[0][e]
        else:
            total += jnp.dot(
                turned_ref[...],
                head_ref[:, piece_columns(place_ref, place_ref[4], d, e)],
                preferred_element_type=jnp.float32,
            )
        out_ref[e] = total.astype(jnp.bfloat16)


def products(place, turned, head_t, twin, halves, d, *parts):
    toks = turned.shape[0]
    return pl.pallas_call(
        functools.partial(products_kernel, d),
        out_shape=jax.ShapeDtypeStruct((4, toks, 256), jnp.bfloat16),
        in_specs=[SMEM] + [VMEM] * (5 + len(parts)),
        out_specs=VMEM,
        compiler_params=params(13),
        cost_estimate=BRIEF,
    )(place, turned, head_t, twin, *halves, *parts)


def add_split_kernel(*refs):
    ins, outs = refs[:4], refs[4:]
    for d, out_ref in enumerate(outs):
        total = ins[0][d].astype(jnp.float32)
        for ref in ins[1:]:
            total += ref[d].astype(jnp.float32)
        out_ref[...] = total.astype(out_ref.dtype)


def add_split(*blocks):
    return pl.pallas_call(
        add_split_kernel,
        out_shape=[jax.ShapeDtypeStruct(blocks[0].shape[1:], blocks[0].dtype)] * 4,
        in_specs=[VMEM] * 4,
        out_specs=[VMEM] * 4,
        compiler_params=params(6),
        cost_estimate=BRIEF,
    )(*blocks)


def add_rows_kernel(place_ref, *refs):
    ins, outs, sum_ref = refs[:4], refs[4:8], refs[8]
    tok = place_ref[1]
    total = ins[0][...].astype(jnp.float32)
    for ref in ins[1:]:
        total += ref[...].astype(jnp.float32)
    sum_ref[...] = total.astype(sum_ref.dtype)
    block = outs[0].shape[0]
    for d, out_ref in enumerate(outs):
        out_ref[...] = sum_ref[pl.ds(pl.multiple_of((tok + d) % 4 * block, block), block), :]


def add_rows(place, blocks):
    toks, wide = blocks[0].shape
    return pl.pallas_call(
        add_rows_kernel,
        out_shape=[jax.ShapeDtypeStruct((toks // 4, wide), jnp.bfloat16)] * 4,
        in_specs=[SMEM] + [VMEM] * 4,
        out_specs=[VMEM] * 4,
        scratch_shapes=[pltpu.VMEM((toks, wide), jnp.bfloat16)],
        compiler_params=params(2),
        cost_estimate=BRIEF,
    )(place, *blocks)


def add_toks_kernel(place_ref, own_ref, *refs):
    ins, (keep_ref, give_ref) = refs[:4], refs[4:]
    even = place_ref[4] == 0
    first = jnp.where(even, ins[0][...].astype(jnp.float32), own_ref[...].astype(jnp.float32))
    total = first
    for ref in ins[1:]:
        total += ref[...].astype(jnp.float32)
    left, right = total[:, :128], total[:, 128:]
    keep_ref[...] = jnp.where(even, left, right).astype(keep_ref.dtype)
    give_ref[...] = jnp.where(even, right, left).astype(give_ref.dtype)


def add_toks(place, own, *received):
    rows, wide = own.shape
    return pl.pallas_call(
        add_toks_kernel,
        out_shape=[jax.ShapeDtypeStruct((rows, wide // 2), jnp.bfloat16)] * 2,
        in_specs=[SMEM] + [VMEM] * 5,
        out_specs=[VMEM] * 2,
        compiler_params=params(1),
        cost_estimate=BRIEF,
    )(place, own, *received)


def choose_kernel(place_ref, keep_ref, got_ref, out_ref):
    mine = place_ref[0] == place_ref[4]
    keep, got = keep_ref[...].astype(jnp.float32), got_ref[...].astype(jnp.float32)
    out_ref[...] = jnp.where(mine, keep, got).astype(out_ref.dtype)


def choose(place, keep, got):
    return pl.pallas_call(
        choose_kernel,
        out_shape=jax.ShapeDtypeStruct(keep.shape, keep.dtype),
        in_specs=[SMEM, VMEM, VMEM],
        out_specs=VMEM,
        compiler_params=params(1),
        cost_estimate=BRIEF,
    )(place, keep, got)


def head_grad_kernel(place_ref, grad_ref, own_ref, other_ref, sent_ref, twin_ref, out_ref):
    teacher = place_ref[0] == 0
    core = place_ref[4]

    def write(mine, others):
        for y in range(2):
            for ref, part in ((mine, core), (others, 1 - core)):
                columns = pl.ds(pl.multiple_of((y * 2 + part) * 256, 256), 256)
                out_ref[:, columns] = jnp.dot(
                    grad_ref[...], ref[0, :, 256 * y : 256 * y + 256], preferred_element_type=jnp.float32
                ).astype(jnp.bfloat16)

    @pl.when(teacher)
    def _():
        write(sent_ref, twin_ref)

    @pl.when(jnp.logical_not(teacher))
    def _():
        write(own_ref, other_ref)


def head_grad_half(place, grad, own, other, sent, twin):
    width, toks = grad.shape
    block = own.shape[2]
    second = pl.BlockSpec((1, toks, block // 2), lambda step, place: (2 + step // 2, 0, step % 2))
    first = pl.BlockSpec((1, toks, block // 2), lambda step, place: (step // 2, 0, step % 2))
    return pl.pallas_call(
        head_grad_kernel,
        grid_spec=pltpu.PrefetchScalarGridSpec(
            num_scalar_prefetch=1,
            grid=(4,),
            in_specs=[
                pl.BlockSpec((width, toks), lambda step, place: (0, 0)),
                second,
                second,
                first,
                first,
            ],
            out_specs=pl.BlockSpec((width, block), lambda step, place: (0, step)),
        ),
        out_shape=jax.ShapeDtypeStruct((width, 4 * block), jnp.bfloat16),
        compiler_params=params(8),
        cost_estimate=BRIEF,
    )(place, grad, own, other, sent, twin)


def spread(stats, name):
    far = send(stats, **{name: 2})
    near = send_by_core(stats, {name: 1}, {name: 3})
    return [stats, far, near, send(near, c=1)]


def on_device(hidden, head, token_ids, loss_mask):
    section, tok, vocab = (lax.axis_index(name) for name in AXES)
    place = jnp.stack([section, tok, vocab >> 3, (vocab >> 1) & 3, vocab & 1]).astype(jnp.int32)
    states = hidden[0]

    with jax.named_scope("gather_tok"):
        blocks = [states] + [send(states, t=d) for d in (1, 2, 3)]
    with jax.named_scope("stage"):
        head_t, *halves = stage(place, head[0].T)
        head_t, *blocks = lax.optimization_barrier((head_t, *blocks))
        halves = [send(half, c=1) for half in halves]
    with jax.named_scope("gather_tok"):
        block = jnp.stack(blocks)
    with jax.named_scope("gather_first"):
        blocks = [block] + [send_by_core(block, {"x": d}, {"y": d}) for d in (1, 2, 3)]
    with jax.named_scope("gather_first"):
        block = jnp.stack(blocks)
    with jax.named_scope("gather_second"):
        own = [block] + [send_by_core(block, {"y": d}, {"x": d}) for d in (1, 2, 3)]
    own[1], halves = lax.optimization_barrier((own[1], halves))
    with jax.named_scope("gather_cores"):
        other = [send(block, c=1) for block in own[:3]]
        own[3], *other = lax.optimization_barrier((own[3], *other))
        other.append(send(own[3], c=1))
    with jax.named_scope("student_hidden"):
        sent = send_both_ways(first_half(place, own))
    with jax.named_scope("own_logits"):
        hidden_own, part = own_logits(place, head_t, own)
    with jax.named_scope("logits"):
        hidden_other, scaled, short, local = logits_parts(place, head_t, other, part)

    with jax.named_scope("stats"):
        stats = merge(local, send(local, c=1))
        stats, short = lax.optimization_barrier((stats, short))
    with jax.named_scope("exchange_scaled"):
        other_short = send(short, s=1)
    with jax.named_scope("stats"):
        stats = merge(*spread(stats, "x"))
        stats, sent = lax.optimization_barrier((stats, sent))
    with jax.named_scope("student_hidden"):
        twin = send(sent, c=1)
    with jax.named_scope("stats"):
        stats = merge(*spread(stats, "y"))
        own_stats = local_scale(local, *spread(stats, "t"))
        other_stats = send(own_stats, s=1)

    with jax.named_scope("logits_grad"):
        grad, turned = logits_grad(
            place, scaled, other_short, own_stats, other_stats, token_ids[None], loss_mask[None]
        )
    turned, twin = lax.optimization_barrier((turned, twin))
    sums, firsts = [], []
    with jax.named_scope("hidden_grad"):
        turned_twin = send(turned, c=1)
        part = own_products(place, turned, head_t, 1)
        part, turned_twin = lax.optimization_barrier((part, turned_twin))
        for d in (1, 2, 3, 0):
            parts = (part,) if d == 1 else ()
            if d == 0:
                grad, firsts[0] = lax.optimization_barrier((grad, firsts[0]))
                head_out = head_grad_half(place, grad, hidden_own, hidden_other, sent, twin)
                turned, firsts[1], head_out = lax.optimization_barrier((turned, firsts[1], head_out))
            sums.append(products(place, turned, head_t, turned_twin, halves[2 * d : 2 * d + 2], d, *parts))
            turned, sums[-1] = lax.optimization_barrier((turned, sums[-1]))
            if d > 0:
                firsts.append(send_by_core(sums[-1], {"x": d}, {"y": d}))
    with jax.named_scope("reduce_second"):
        parts = add_split(sums[3], *firsts)
        seconds = [send_by_core(parts[d], {"y": d}, {"x": d}) for d in (1, 2, 3)]
    with jax.named_scope("reduce_tok"):
        rows = add_rows(place, [parts[0]] + seconds)
        received = [send(rows[0], s=1)]
        received += [send_by_core(rows[d], {"s": 1, "t": d}, {"t": d}) for d in (1, 2, 3)]
        keep, give = add_toks(place, rows[0], *received)
    with jax.named_scope("hidden_out"):
        hidden_out = choose(place, keep, send(give, c=1))
    return head_out.T, hidden_out


def solution(mesh):
    in_specs = (P("section", "tok", "vocab"), P("section", None, ("tok", "vocab")), P(), P())
    out_specs = (P("section", ("tok", "vocab")), P("tok", ("section", "vocab")))
    return jax.shard_map(
        on_device, mesh=mesh, in_specs=in_specs, out_specs=out_specs, check_vma=False
    )
```

```python
import functools
import jax
import jax.numpy as jnp
from jax import lax
from jax.experimental import pallas as pl
from jax.experimental.pallas import tpu as pltpu
from jax.sharding import PartitionSpec as P

AXES = ("section", "tok", "vocab")
SIZES = {"s": 2, "t": 4, "x": 4, "y": 4, "c": 2}
MIB = 1024 * 1024


def route(shift_of):
    names = list(SIZES)
    pairs = []
    for device in range(256):
        place, rest = {}, device
        for name in reversed(names):
            rest, place[name] = divmod(rest, SIZES[name])
        shift = shift_of(place)
        target = 0
        for name in names:
            target = target * SIZES[name] + (place[name] + shift.get(name, 0)) % SIZES[name]
        pairs.append((device, target))
    return pairs


def send(block, **shift):
    return lax.ppermute(block, AXES, route(lambda place: shift))


def send_by_core(block, even, odd):
    return lax.ppermute(block, AXES, route(lambda place: odd if place["c"] else even))


def send_both_ways(block):
    def shift_of(place):
        return {"s": 1, "t": (1 if place["s"] else 3) if place["c"] else 0}

    return lax.ppermute(block, AXES, route(shift_of))


def params(mib):
    return pltpu.CompilerParams(vmem_limit_bytes=mib * MIB)


BRIEF = pl.CostEstimate(flops=0, bytes_accessed=0, transcendentals=0)
VMEM = pl.BlockSpec(memory_space=pltpu.VMEM)
SMEM = pl.BlockSpec(memory_space=pltpu.SMEM)


def piece_columns(place_ref, core, d, e):
    at_x = (place_ref[2] + jnp.where(core == 0, d, e)) % 4
    at_y = (place_ref[3] + jnp.where(core == 0, e, d)) % 4
    return pl.ds(pl.multiple_of((core * 16 + at_x * 4 + at_y) * 256, 256), 256)


def stage_kernel(place_ref, head_ref, out_ref, *refs):
    gives, arrived = refs[:8], refs[8]
    copy = pltpu.make_async_copy(head_ref, out_ref, arrived)
    copy.start()
    for d in range(4):
        for e in range(4):
            columns = piece_columns(place_ref, 1 - place_ref[4], d, e)
            gives[2 * d + e // 2][:, e % 2 * 256 : e % 2 * 256 + 256] = head_ref[:, columns]
    copy.wait()


def stage(place, head_t):
    width, _ = head_t.shape
    return pl.pallas_call(
        stage_kernel,
        out_shape=[jax.ShapeDtypeStruct(head_t.shape, head_t.dtype)]
        + [jax.ShapeDtypeStruct((width, 512), head_t.dtype)] * 8,
        in_specs=[SMEM, VMEM],
        out_specs=[VMEM] * 9,
        scratch_shapes=[pltpu.SemaphoreType.DMA],
        compiler_params=params(22),
    )(place, head_t)


def first_half_kernel(place_ref, *refs):
    own, out_ref = refs[:4], refs[4]
    tok, x, y, c = place_ref[1], place_ref[2], place_ref[3], place_ref[4]
    _, _, rows, chunk = own[0].shape

    def lay(x_at, y_at, piece):
        columns = pl.ds(pl.multiple_of(y_at * chunk, chunk), chunk)
        for dt in range(4):
            at = pl.ds(pl.multiple_of((tok + 4 - dt) % 4 * rows, rows), rows)
            out_ref[x_at, at, columns] = piece(dt)

    for x_at in range(2):
        dx = (x + 4 - x_at) % 4

        @pl.when(c == 0)
        def _():
            for dy in range(4):
                lay(x_at, (y + 4 - dy) % 4, lambda dt: own[dy][dx, dt])

        for step in range(4):
            @pl.when(jnp.logical_and(c == 1, dx == step))
            def _():
                for dy in range(4):
                    lay(x_at, (y + 4 - dy) % 4, lambda dt: own[step][dy, dt])


def first_half(place, own):
    _, _, rows, chunk = own[0].shape
    return pl.pallas_call(
        first_half_kernel,
        out_shape=jax.ShapeDtypeStruct((2, 4 * rows, 4 * chunk), own[0].dtype),
        in_specs=[SMEM] + [VMEM] * 4,
        out_specs=VMEM,
        compiler_params=params(5),
        cost_estimate=BRIEF,
    )(place, *own)


def lay_out(place_ref, core, blocks, hidden_ref):
    tok, x, y = place_ref[1], place_ref[2], place_ref[3]
    _, _, rows, chunk = blocks[0].shape
    for late in range(4):
        for early in range(4):
            at_x = (x + 4 - jnp.where(core == 0, early, late)) % 4
            at_y = (y + 4 - jnp.where(core == 0, late, early)) % 4
            columns = pl.ds(pl.multiple_of(at_y * chunk, chunk), chunk)
            for dt in range(4):
                at = pl.ds(pl.multiple_of((tok + 4 - dt) % 4 * rows, rows), rows)
                hidden_ref[at_x, at, columns] = blocks[late][early, dt]


def add_products(core, head_ref, hidden_ref, acc_ref):
    chunk = hidden_ref.shape[2] // 4

    @pl.loop(0, 4)
    def _(x):
        total = acc_ref[...]
        for y in range(4):
            columns = pl.ds(pl.multiple_of(((x * 4 + y) * 2 + core) * chunk, chunk), chunk)
            total += lax.dot_general(
                head_ref[:, columns],
                hidden_ref[x, :, y * chunk : y * chunk + chunk],
                (((1,), (1,)), ((), ())),
                preferred_element_type=jnp.float32,
            )
        acc_ref[...] = total


def own_logits_kernel(place_ref, head_ref, *refs):
    own, (hidden_ref, acc_ref) = refs[:4], refs[4:]
    lay_out(place_ref, place_ref[4], own, hidden_ref)
    acc_ref[...] = jnp.zeros_like(acc_ref)
    add_products(place_ref[4], head_ref, hidden_ref, acc_ref)


def own_logits(place, head_t, own):
    width, _ = head_t.shape
    _, _, rows, chunk = own[0].shape
    toks = 4 * rows
    return pl.pallas_call(
        own_logits_kernel,
        out_shape=[
            jax.ShapeDtypeStruct((4, toks, 4 * chunk), jnp.bfloat16),
            jax.ShapeDtypeStruct((width, toks), jnp.float32),
        ],
        in_specs=[SMEM] + [VMEM] * 5,
        out_specs=[VMEM] * 2,
        compiler_params=params(16),
    )(place, head_t, *own)


def logits_kernel(place_ref, head_ref, *refs):
    other, part_ref = refs[:4], refs[4]
    hidden_ref, scaled_ref, short_ref, stats_ref, acc_ref = refs[5:]
    lay_out(place_ref, 1 - place_ref[4], other, hidden_ref)
    acc_ref[...] = part_ref[...]
    add_products(1 - place_ref[4], head_ref, hidden_ref, acc_ref)
    logits = acc_ref[...]
    peak = jnp.max(logits, axis=0, keepdims=True)
    shifted = logits - peak
    scaled = jnp.exp(shifted)
    scaled_ref[...] = scaled
    short_ref[...] = scaled.astype(jnp.bfloat16)
    stats_ref[0:1] = peak
    stats_ref[1:2] = jnp.sum(scaled, axis=0, keepdims=True)
    stats_ref[2:3] = jnp.sum(scaled * shifted, axis=0, keepdims=True)
    stats_ref[3:8] = jnp.zeros((5, peak.shape[1]), jnp.float32)


def logits_parts(place, head_t, other, part):
    width, toks = part.shape
    _, _, rows, chunk = other[0].shape
    return pl.pallas_call(
        logits_kernel,
        out_shape=[
            jax.ShapeDtypeStruct((4, toks, 4 * chunk), jnp.bfloat16),
            jax.ShapeDtypeStruct((width, toks), jnp.float32),
            jax.ShapeDtypeStruct((width, toks), jnp.bfloat16),
            jax.ShapeDtypeStruct((8, toks), jnp.float32),
        ],
        in_specs=[SMEM] + [VMEM] * 6,
        out_specs=[VMEM] * 4,
        scratch_shapes=[pltpu.VMEM((width, toks), jnp.float32)],
        compiler_params=params(17),
        cost_estimate=BRIEF,
    )(place, head_t, *other, part)


def merge_kernel(*refs):
    *ins, out_ref = refs
    peak = ins[0][0:1]
    for ref in ins[1:]:
        peak = jnp.maximum(peak, ref[0:1])
    total = jnp.zeros_like(peak)
    moment = jnp.zeros_like(peak)
    for ref in ins:
        drop = ref[0:1] - peak
        factor = jnp.exp(drop)
        total += factor * ref[1:2]
        moment += factor * (ref[2:3] + drop * ref[1:2])
    out_ref[0:1] = peak
    out_ref[1:2] = total
    out_ref[2:3] = moment
    out_ref[3:8] = jnp.zeros((5, peak.shape[1]), jnp.float32)


def merge(*stats):
    return pl.pallas_call(
        merge_kernel,
        out_shape=jax.ShapeDtypeStruct(stats[0].shape, jnp.float32),
        in_specs=[VMEM] * len(stats),
        out_specs=VMEM,
        compiler_params=params(1),
        cost_estimate=BRIEF,
    )(*stats)


def scale_kernel(local_ref, *refs):
    *ins, out_ref = refs
    peak = ins[0][0:1]
    for ref in ins[1:]:
        peak = jnp.maximum(peak, ref[0:1])
    total = jnp.zeros_like(peak)
    moment = jnp.zeros_like(peak)
    for ref in ins:
        drop = ref[0:1] - peak
        factor = jnp.exp(drop)
        total += factor * ref[1:2]
        moment += factor * (ref[2:3] + drop * ref[1:2])
    out_ref[0:1] = jnp.exp(local_ref[0:1] - peak) / total
    out_ref[1:2] = jnp.log(total) - moment / total
    out_ref[2:8] = jnp.zeros((6, peak.shape[1]), jnp.float32)


def local_scale(local, *stats):
    return pl.pallas_call(
        scale_kernel,
        out_shape=jax.ShapeDtypeStruct(local.shape, jnp.float32),
        in_specs=[VMEM] * (1 + len(stats)),
        out_specs=VMEM,
        compiler_params=params(1),
        cost_estimate=BRIEF,
    )(local, *stats)


def grad_kernel(place_ref, own_ref, other_ref, own_stats, other_stats, ids_ref, mask_ref, grad_ref, turned_ref):
    teacher = place_ref[0] == 0
    mask = mask_ref[...].astype(jnp.float32)
    entropy = jnp.where(teacher, own_stats[1:2], other_stats[1:2])
    by_own = jnp.where(teacher, -entropy, entropy + 1.0) * own_stats[0:1] * mask
    by_other = jnp.where(teacher, entropy + 1.0, -entropy) * other_stats[0:1] * mask
    width = own_ref.shape[0]
    first = ((place_ref[1] * 4 + place_ref[2]) * 8 + place_ref[3] * 2 + place_ref[4]) * width
    entries = lax.broadcasted_iota(jnp.int32, own_ref.shape, 0) + first
    onehot = jnp.where(entries == ids_ref[...], mask, 0.0)
    grad = by_own * own_ref[...] + by_other * other_ref[...].astype(jnp.float32) - onehot
    grad_ref[...] = grad.astype(jnp.bfloat16)
    turned_ref[...] = grad.T.astype(jnp.bfloat16)


def logits_grad(place, own, other, own_stats, other_stats, ids, mask):
    width, toks = own.shape
    return pl.pallas_call(
        grad_kernel,
        out_shape=[
            jax.ShapeDtypeStruct((width, toks), jnp.bfloat16),
            jax.ShapeDtypeStruct((toks, width), jnp.bfloat16),
        ],
        in_specs=[SMEM] + [VMEM] * 6,
        out_specs=[VMEM, VMEM],
        compiler_params=params(5),
        cost_estimate=BRIEF,
    )(place, own, other, own_stats, other_stats, ids, mask)


def own_products_kernel(d, place_ref, turned_ref, head_ref, out_ref):
    for e in range(4):
        out_ref[e] = jnp.dot(
            turned_ref[...],
            head_ref[:, piece_columns(place_ref, place_ref[4], d, e)],
            preferred_element_type=jnp.float32,
        )


def own_products(place, turned, head_t, d):
    return pl.pallas_call(
        functools.partial(own_products_kernel, d),
        out_shape=jax.ShapeDtypeStruct((4, turned.shape[0], 256), jnp.float32),
        in_specs=[SMEM, VMEM, VMEM],
        out_specs=VMEM,
        compiler_params=params(11),
        cost_estimate=BRIEF,
    )(place, turned, head_t)


def products_kernel(d, place_ref, turned_ref, head_ref, twin_ref, *refs):
    halves, parts, out_ref = refs[:2], refs[2:-1], refs[-1]
    for e in range(4):
        total = jnp.dot(
            twin_ref[...],
            halves[e // 2][:, e % 2 * 256 : e % 2 * 256 + 256],
            preferred_element_type=jnp.float32,
        )
        if parts:
            total += parts[0][e]
        else:
            total += jnp.dot(
                turned_ref[...],
                head_ref[:, piece_columns(place_ref, place_ref[4], d, e)],
                preferred_element_type=jnp.float32,
            )
        out_ref[e] = total.astype(jnp.bfloat16)


def products(place, turned, head_t, twin, halves, d, *parts):
    toks = turned.shape[0]
    return pl.pallas_call(
        functools.partial(products_kernel, d),
        out_shape=jax.ShapeDtypeStruct((4, toks, 256), jnp.bfloat16),
        in_specs=[SMEM] + [VMEM] * (5 + len(parts)),
        out_specs=VMEM,
        compiler_params=params(13),
        cost_estimate=BRIEF,
    )(place, turned, head_t, twin, *halves, *parts)


def add_split_kernel(*refs):
    ins, outs = refs[:4], refs[4:]
    for d, out_ref in enumerate(outs):
        total = ins[0][d].astype(jnp.float32)
        for ref in ins[1:]:
            total += ref[d].astype(jnp.float32)
        out_ref[...] = total.astype(out_ref.dtype)


def add_split(*blocks):
    return pl.pallas_call(
        add_split_kernel,
        out_shape=[jax.ShapeDtypeStruct(blocks[0].shape[1:], blocks[0].dtype)] * 4,
        in_specs=[VMEM] * 4,
        out_specs=[VMEM] * 4,
        compiler_params=params(6),
        cost_estimate=BRIEF,
    )(*blocks)


def add_rows_kernel(place_ref, *refs):
    ins, outs, sum_ref = refs[:4], refs[4:8], refs[8]
    tok = place_ref[1]
    total = ins[0][...].astype(jnp.float32)
    for ref in ins[1:]:
        total += ref[...].astype(jnp.float32)
    sum_ref[...] = total.astype(sum_ref.dtype)
    block = outs[0].shape[0]
    for d, out_ref in enumerate(outs):
        out_ref[...] = sum_ref[pl.ds(pl.multiple_of((tok + d) % 4 * block, block), block), :]


def add_rows(place, blocks):
    toks, wide = blocks[0].shape
    return pl.pallas_call(
        add_rows_kernel,
        out_shape=[jax.ShapeDtypeStruct((toks // 4, wide), jnp.bfloat16)] * 4,
        in_specs=[SMEM] + [VMEM] * 4,
        out_specs=[VMEM] * 4,
        scratch_shapes=[pltpu.VMEM((toks, wide), jnp.bfloat16)],
        compiler_params=params(2),
        cost_estimate=BRIEF,
    )(place, *blocks)


def add_toks_kernel(place_ref, own_ref, *refs):
    ins, (keep_ref, give_ref) = refs[:4], refs[4:]
    even = place_ref[4] == 0
    first = jnp.where(even, ins[0][...].astype(jnp.float32), own_ref[...].astype(jnp.float32))
    total = first
    for ref in ins[1:]:
        total += ref[...].astype(jnp.float32)
    left, right = total[:, :128], total[:, 128:]
    keep_ref[...] = jnp.where(even, left, right).astype(keep_ref.dtype)
    give_ref[...] = jnp.where(even, right, left).astype(give_ref.dtype)


def add_toks(place, own, *received):
    rows, wide = own.shape
    return pl.pallas_call(
        add_toks_kernel,
        out_shape=[jax.ShapeDtypeStruct((rows, wide // 2), jnp.bfloat16)] * 2,
        in_specs=[SMEM] + [VMEM] * 5,
        out_specs=[VMEM] * 2,
        compiler_params=params(1),
        cost_estimate=BRIEF,
    )(place, own, *received)


def choose_kernel(place_ref, keep_ref, got_ref, out_ref):
    mine = place_ref[0] == place_ref[4]
    keep, got = keep_ref[...].astype(jnp.float32), got_ref[...].astype(jnp.float32)
    out_ref[...] = jnp.where(mine, keep, got).astype(out_ref.dtype)


def choose(place, keep, got):
    return pl.pallas_call(
        choose_kernel,
        out_shape=jax.ShapeDtypeStruct(keep.shape, keep.dtype),
        in_specs=[SMEM, VMEM, VMEM],
        out_specs=VMEM,
        compiler_params=params(1),
        cost_estimate=BRIEF,
    )(place, keep, got)


def head_grad_kernel(place_ref, grad_ref, own_ref, other_ref, sent_ref, twin_ref, out_ref):
    teacher = place_ref[0] == 0
    core = place_ref[4]

    def write(mine, others):
        for y in range(2):
            for ref, part in ((mine, core), (others, 1 - core)):
                columns = pl.ds(pl.multiple_of((y * 2 + part) * 256, 256), 256)
                out_ref[:, columns] = jnp.dot(
                    grad_ref[...], ref[0, :, 256 * y : 256 * y + 256], preferred_element_type=jnp.float32
                ).astype(jnp.bfloat16)

    @pl.when(teacher)
    def _():
        write(sent_ref, twin_ref)

    @pl.when(jnp.logical_not(teacher))
    def _():
        write(own_ref, other_ref)


def head_grad_half(place, grad, own, other, sent, twin):
    width, toks = grad.shape
    block = own.shape[2]
    second = pl.BlockSpec((1, toks, block // 2), lambda step, place: (2 + step // 2, 0, step % 2))
    first = pl.BlockSpec((1, toks, block // 2), lambda step, place: (step // 2, 0, step % 2))
    return pl.pallas_call(
        head_grad_kernel,
        grid_spec=pltpu.PrefetchScalarGridSpec(
            num_scalar_prefetch=1,
            grid=(4,),
            in_specs=[
                pl.BlockSpec((width, toks), lambda step, place: (0, 0)),
                second,
                second,
                first,
                first,
            ],
            out_specs=pl.BlockSpec((width, block), lambda step, place: (0, step)),
        ),
        out_shape=jax.ShapeDtypeStruct((width, 4 * block), jnp.bfloat16),
        compiler_params=params(8),
        cost_estimate=BRIEF,
    )(place, grad, own, other, sent, twin)


def spread(stats, name):
    far = send(stats, **{name: 2})
    near = send_by_core(stats, {name: 1}, {name: 3})
    return [stats, far, near, send(near, c=1)]


def on_device(hidden, head, token_ids, loss_mask):
    section, tok, vocab = (lax.axis_index(name) for name in AXES)
    place = jnp.stack([section, tok, vocab >> 3, (vocab >> 1) & 3, vocab & 1]).astype(jnp.int32)
    states = hidden[0]

    with jax.named_scope("gather_tok"):
        blocks = [states] + [send(states, t=d) for d in (1, 2, 3)]
    with jax.named_scope("gather_tok"):
        place, *blocks = lax.optimization_barrier((place, *blocks))
        block = jnp.stack(blocks)
    with jax.named_scope("gather_first"):
        blocks = [block] + [send_by_core(block, {"x": d}, {"y": d}) for d in (1, 2, 3)]
    with jax.named_scope("stage"):
        head_t, *halves = stage(place, head[0].T)
        head_t, *blocks = lax.optimization_barrier((head_t, *blocks))
    with jax.named_scope("gather_first"):
        block = jnp.stack(blocks)
    with jax.named_scope("gather_second"):
        own = [block] + [send_by_core(block, {"y": d}, {"x": d}) for d in (1, 2, 3)]
    own[1], halves = lax.optimization_barrier((own[1], halves))
    with jax.named_scope("stage"):
        halves = [send(half, c=1) for half in halves]
    with jax.named_scope("gather_cores"):
        other = [send(block, c=1) for block in own[:3]]
        own[3], *other = lax.optimization_barrier((own[3], *other))
        other.append(send(own[3], c=1))
    with jax.named_scope("student_hidden"):
        sent = send_both_ways(first_half(place, own))
    with jax.named_scope("own_logits"):
        hidden_own, part = own_logits(place, head_t, own)
        part, halves = lax.optimization_barrier((part, halves))
    with jax.named_scope("logits"):
        hidden_other, scaled, short, local = logits_parts(place, head_t, other, part)

    with jax.named_scope("stats"):
        stats = merge(local, send(local, c=1))
        stats, short = lax.optimization_barrier((stats, short))
    with jax.named_scope("exchange_scaled"):
        other_short = send(short, s=1)
    with jax.named_scope("stats"):
        stats = merge(*spread(stats, "x"))
        stats, sent = lax.optimization_barrier((stats, sent))
    with jax.named_scope("student_hidden"):
        twin = send(sent, c=1)
    with jax.named_scope("stats"):
        stats = merge(*spread(stats, "y"))
        own_stats = local_scale(local, *spread(stats, "t"))
        other_stats = send(own_stats, s=1)

    with jax.named_scope("logits_grad"):
        grad, turned = logits_grad(
            place, scaled, other_short, own_stats, other_stats, token_ids[None], loss_mask[None]
        )
    turned, twin = lax.optimization_barrier((turned, twin))
    sums, firsts = [], []
    with jax.named_scope("hidden_grad"):
        turned_twin = send(turned, c=1)
        part = own_products(place, turned, head_t, 1)
        part, turned_twin = lax.optimization_barrier((part, turned_twin))
        for d in (1, 2, 3, 0):
            parts = (part,) if d == 1 else ()
            if d == 0:
                grad, firsts[0] = lax.optimization_barrier((grad, firsts[0]))
                head_out = head_grad_half(place, grad, hidden_own, hidden_other, sent, twin)
                turned, firsts[1], head_out = lax.optimization_barrier((turned, firsts[1], head_out))
            sums.append(products(place, turned, head_t, turned_twin, halves[2 * d : 2 * d + 2], d, *parts))
            turned, sums[-1] = lax.optimization_barrier((turned, sums[-1]))
            if d > 0:
                firsts.append(send_by_core(sums[-1], {"x": d}, {"y": d}))
    with jax.named_scope("reduce_second"):
        parts = add_split(sums[3], *firsts)
        seconds = [send_by_core(parts[d], {"y": d}, {"x": d}) for d in (1, 2, 3)]
    with jax.named_scope("reduce_tok"):
        rows = add_rows(place, [parts[0]] + seconds)
        received = [send(rows[0], s=1)]
        received += [send_by_core(rows[d], {"s": 1, "t": d}, {"t": d}) for d in (1, 2, 3)]
        keep, give = add_toks(place, rows[0], *received)
    with jax.named_scope("hidden_out"):
        hidden_out = choose(place, keep, send(give, c=1))
    return head_out.T, hidden_out


def solution(mesh):
    in_specs = (P("section", "tok", "vocab"), P("section", None, ("tok", "vocab")), P(), P())
    out_specs = (P("section", ("tok", "vocab")), P("tok", ("section", "vocab")))
    return jax.shard_map(
        on_device, mesh=mesh, in_specs=in_specs, out_specs=out_specs, check_vma=False
    )
```

```python
import functools
import jax
import jax.numpy as jnp
from jax import lax
from jax.experimental import pallas as pl
from jax.experimental.pallas import tpu as pltpu
from jax.sharding import PartitionSpec as P

AXES = ("section", "tok", "vocab")
SIZES = {"s": 2, "t": 4, "x": 4, "y": 4, "c": 2}
MIB = 1024 * 1024


def route(shift_of):
    names = list(SIZES)
    pairs = []
    for device in range(256):
        place, rest = {}, device
        for name in reversed(names):
            rest, place[name] = divmod(rest, SIZES[name])
        shift = shift_of(place)
        target = 0
        for name in names:
            target = target * SIZES[name] + (place[name] + shift.get(name, 0)) % SIZES[name]
        pairs.append((device, target))
    return pairs


def send(block, **shift):
    return lax.ppermute(block, AXES, route(lambda place: shift))


def send_by_core(block, even, odd):
    return lax.ppermute(block, AXES, route(lambda place: odd if place["c"] else even))


def send_both_ways(block):
    def shift_of(place):
        return {"s": 1, "t": (1 if place["s"] else 3) if place["c"] else 0}

    return lax.ppermute(block, AXES, route(shift_of))


def params(mib):
    return pltpu.CompilerParams(vmem_limit_bytes=mib * MIB)


BRIEF = pl.CostEstimate(flops=0, bytes_accessed=0, transcendentals=0)
VMEM = pl.BlockSpec(memory_space=pltpu.VMEM)
SMEM = pl.BlockSpec(memory_space=pltpu.SMEM)


def piece_columns(place_ref, core, d, e):
    at_x = (place_ref[2] + jnp.where(core == 0, d, e)) % 4
    at_y = (place_ref[3] + jnp.where(core == 0, e, d)) % 4
    return pl.ds(pl.multiple_of((core * 16 + at_x * 4 + at_y) * 256, 256), 256)


def stage_kernel(place_ref, head_ref, out_ref, *refs):
    gives, arrived = refs[:8], refs[8]
    copy = pltpu.make_async_copy(head_ref, out_ref, arrived)
    copy.start()
    for d in range(4):
        for e in range(4):
            columns = piece_columns(place_ref, 1 - place_ref[4], d, e)
            gives[2 * ((d + 3) % 4) + e // 2][:, e % 2 * 256 : e % 2 * 256 + 256] = head_ref[:, columns]
    copy.wait()


def stage(place, head_t):
    width, _ = head_t.shape
    return pl.pallas_call(
        stage_kernel,
        out_shape=[jax.ShapeDtypeStruct(head_t.shape, head_t.dtype)]
        + [jax.ShapeDtypeStruct((width, 512), head_t.dtype)] * 8,
        in_specs=[SMEM, VMEM],
        out_specs=[VMEM] * 9,
        scratch_shapes=[pltpu.SemaphoreType.DMA],
        compiler_params=params(22),
    )(place, head_t)


def first_half_kernel(place_ref, *refs):
    own, out_ref = refs[:4], refs[4]
    tok, x, y, c = place_ref[1], place_ref[2], place_ref[3], place_ref[4]
    _, _, rows, chunk = own[0].shape

    def lay(x_at, y_at, piece):
        columns = pl.ds(pl.multiple_of(y_at * chunk, chunk), chunk)
        for dt in range(4):
            at = pl.ds(pl.multiple_of((tok + 4 - dt) % 4 * rows, rows), rows)
            out_ref[x_at, at, columns] = piece(dt)

    for x_at in range(2):
        dx = (x + 4 - x_at) % 4

        @pl.when(c == 0)
        def _():
            for dy in range(4):
                lay(x_at, (y + 4 - dy) % 4, lambda dt: own[dy][dx, dt])

        for step in range(4):
            @pl.when(jnp.logical_and(c == 1, dx == step))
            def _():
                for dy in range(4):
                    lay(x_at, (y + 4 - dy) % 4, lambda dt: own[step][dy, dt])


def first_half(place, own):
    _, _, rows, chunk = own[0].shape
    return pl.pallas_call(
        first_half_kernel,
        out_shape=jax.ShapeDtypeStruct((2, 4 * rows, 4 * chunk), own[0].dtype),
        in_specs=[SMEM] + [VMEM] * 4,
        out_specs=VMEM,
        compiler_params=params(5),
        cost_estimate=BRIEF,
    )(place, *own)


def lay_out(place_ref, core, blocks, hidden_ref):
    tok, x, y = place_ref[1], place_ref[2], place_ref[3]
    _, _, rows, chunk = blocks[0].shape
    for late in range(4):
        for early in range(4):
            at_x = (x + 4 - jnp.where(core == 0, early, late)) % 4
            at_y = (y + 4 - jnp.where(core == 0, late, early)) % 4
            columns = pl.ds(pl.multiple_of(at_y * chunk, chunk), chunk)
            for dt in range(4):
                at = pl.ds(pl.multiple_of((tok + 4 - dt) % 4 * rows, rows), rows)
                hidden_ref[at_x, at, columns] = blocks[late][early, dt]


def add_products(core, head_ref, hidden_ref, acc_ref):
    chunk = hidden_ref.shape[2] // 4

    @pl.loop(0, 4)
    def _(x):
        total = acc_ref[...]
        for y in range(4):
            columns = pl.ds(pl.multiple_of(((x * 4 + y) * 2 + core) * chunk, chunk), chunk)
            total += lax.dot_general(
                head_ref[:, columns],
                hidden_ref[x, :, y * chunk : y * chunk + chunk],
                (((1,), (1,)), ((), ())),
                preferred_element_type=jnp.float32,
            )
        acc_ref[...] = total


def own_logits_kernel(place_ref, head_ref, *refs):
    own, (hidden_ref, acc_ref) = refs[:4], refs[4:]
    lay_out(place_ref, place_ref[4], own, hidden_ref)
    acc_ref[...] = jnp.zeros_like(acc_ref)
    add_products(place_ref[4], head_ref, hidden_ref, acc_ref)


def own_logits(place, head_t, own):
    width, _ = head_t.shape
    _, _, rows, chunk = own[0].shape
    toks = 4 * rows
    return pl.pallas_call(
        own_logits_kernel,
        out_shape=[
            jax.ShapeDtypeStruct((4, toks, 4 * chunk), jnp.bfloat16),
            jax.ShapeDtypeStruct((width, toks), jnp.float32),
        ],
        in_specs=[SMEM] + [VMEM] * 5,
        out_specs=[VMEM] * 2,
        compiler_params=params(16),
    )(place, head_t, *own)


def logits_kernel(place_ref, head_ref, *refs):
    other, part_ref = refs[:4], refs[4]
    hidden_ref, scaled_ref, short_ref, stats_ref, acc_ref = refs[5:]
    lay_out(place_ref, 1 - place_ref[4], other, hidden_ref)
    acc_ref[...] = part_ref[...]
    add_products(1 - place_ref[4], head_ref, hidden_ref, acc_ref)
    logits = acc_ref[...]
    peak = jnp.max(logits, axis=0, keepdims=True)
    shifted = logits - peak
    scaled = jnp.exp(shifted)
    scaled_ref[...] = scaled
    short_ref[...] = scaled.astype(jnp.bfloat16)
    stats_ref[0:1] = peak
    stats_ref[1:2] = jnp.sum(scaled, axis=0, keepdims=True)
    stats_ref[2:3] = jnp.sum(scaled * shifted, axis=0, keepdims=True)
    stats_ref[3:8] = jnp.zeros((5, peak.shape[1]), jnp.float32)


def logits_parts(place, head_t, other, part):
    width, toks = part.shape
    _, _, rows, chunk = other[0].shape
    return pl.pallas_call(
        logits_kernel,
        out_shape=[
            jax.ShapeDtypeStruct((4, toks, 4 * chunk), jnp.bfloat16),
            jax.ShapeDtypeStruct((width, toks), jnp.float32),
            jax.ShapeDtypeStruct((width, toks), jnp.bfloat16),
            jax.ShapeDtypeStruct((8, toks), jnp.float32),
        ],
        in_specs=[SMEM] + [VMEM] * 6,
        out_specs=[VMEM] * 4,
        scratch_shapes=[pltpu.VMEM((width, toks), jnp.float32)],
        compiler_params=params(17),
        cost_estimate=BRIEF,
    )(place, head_t, *other, part)


def merge_kernel(*refs):
    *ins, out_ref = refs
    peak = ins[0][0:1]
    for ref in ins[1:]:
        peak = jnp.maximum(peak, ref[0:1])
    total = jnp.zeros_like(peak)
    moment = jnp.zeros_like(peak)
    for ref in ins:
        drop = ref[0:1] - peak
        factor = jnp.exp(drop)
        total += factor * ref[1:2]
        moment += factor * (ref[2:3] + drop * ref[1:2])
    out_ref[0:1] = peak
    out_ref[1:2] = total
    out_ref[2:3] = moment
    out_ref[3:8] = jnp.zeros((5, peak.shape[1]), jnp.float32)


def merge(*stats):
    return pl.pallas_call(
        merge_kernel,
        out_shape=jax.ShapeDtypeStruct(stats[0].shape, jnp.float32),
        in_specs=[VMEM] * len(stats),
        out_specs=VMEM,
        compiler_params=params(1),
        cost_estimate=BRIEF,
    )(*stats)


def scale_kernel(local_ref, *refs):
    *ins, out_ref = refs
    peak = ins[0][0:1]
    for ref in ins[1:]:
        peak = jnp.maximum(peak, ref[0:1])
    total = jnp.zeros_like(peak)
    moment = jnp.zeros_like(peak)
    for ref in ins:
        drop = ref[0:1] - peak
        factor = jnp.exp(drop)
        total += factor * ref[1:2]
        moment += factor * (ref[2:3] + drop * ref[1:2])
    out_ref[0:1] = jnp.exp(local_ref[0:1] - peak) / total
    out_ref[1:2] = jnp.log(total) - moment / total
    out_ref[2:8] = jnp.zeros((6, peak.shape[1]), jnp.float32)


def local_scale(local, *stats):
    return pl.pallas_call(
        scale_kernel,
        out_shape=jax.ShapeDtypeStruct(local.shape, jnp.float32),
        in_specs=[VMEM] * (1 + len(stats)),
        out_specs=VMEM,
        compiler_params=params(1),
        cost_estimate=BRIEF,
    )(local, *stats)


def grad_kernel(place_ref, own_ref, other_ref, own_stats, other_stats, ids_ref, mask_ref, grad_ref, turned_ref):
    teacher = place_ref[0] == 0
    mask = mask_ref[...].astype(jnp.float32)
    entropy = jnp.where(teacher, own_stats[1:2], other_stats[1:2])
    by_own = jnp.where(teacher, -entropy, entropy + 1.0) * own_stats[0:1] * mask
    by_other = jnp.where(teacher, entropy + 1.0, -entropy) * other_stats[0:1] * mask
    width = own_ref.shape[0]
    first = ((place_ref[1] * 4 + place_ref[2]) * 8 + place_ref[3] * 2 + place_ref[4]) * width
    entries = lax.broadcasted_iota(jnp.int32, own_ref.shape, 0) + first
    onehot = jnp.where(entries == ids_ref[...], mask, 0.0)
    grad = by_own * own_ref[...] + by_other * other_ref[...].astype(jnp.float32) - onehot
    grad_ref[...] = grad.astype(jnp.bfloat16)
    turned_ref[...] = grad.T.astype(jnp.bfloat16)


def logits_grad(place, own, other, own_stats, other_stats, ids, mask):
    width, toks = own.shape
    return pl.pallas_call(
        grad_kernel,
        out_shape=[
            jax.ShapeDtypeStruct((width, toks), jnp.bfloat16),
            jax.ShapeDtypeStruct((toks, width), jnp.bfloat16),
        ],
        in_specs=[SMEM] + [VMEM] * 6,
        out_specs=[VMEM, VMEM],
        compiler_params=params(5),
        cost_estimate=BRIEF,
    )(place, own, other, own_stats, other_stats, ids, mask)


def own_products_kernel(d, place_ref, turned_ref, head_ref, out_ref):
    for e in range(4):
        out_ref[e] = jnp.dot(
            turned_ref[...],
            head_ref[:, piece_columns(place_ref, place_ref[4], d, e)],
            preferred_element_type=jnp.float32,
        )


def own_products(place, turned, head_t, d):
    return pl.pallas_call(
        functools.partial(own_products_kernel, d),
        out_shape=jax.ShapeDtypeStruct((4, turned.shape[0], 256), jnp.float32),
        in_specs=[SMEM, VMEM, VMEM],
        out_specs=VMEM,
        compiler_params=params(11),
        cost_estimate=BRIEF,
    )(place, turned, head_t)


def products_kernel(d, place_ref, turned_ref, head_ref, twin_ref, *refs):
    halves, parts, out_ref = refs[:2], refs[2:-1], refs[-1]
    for e in range(4):
        total = jnp.dot(
            twin_ref[...],
            halves[e // 2][:, e % 2 * 256 : e % 2 * 256 + 256],
            preferred_element_type=jnp.float32,
        )
        if parts:
            total += parts[0][e]
        else:
            total += jnp.dot(
                turned_ref[...],
                head_ref[:, piece_columns(place_ref, place_ref[4], d, e)],
                preferred_element_type=jnp.float32,
            )
        out_ref[e] = total.astype(jnp.bfloat16)


def products(place, turned, head_t, twin, halves, d, *parts):
    toks = turned.shape[0]
    return pl.pallas_call(
        functools.partial(products_kernel, d),
        out_shape=jax.ShapeDtypeStruct((4, toks, 256), jnp.bfloat16),
        in_specs=[SMEM] + [VMEM] * (5 + len(parts)),
        out_specs=VMEM,
        compiler_params=params(13),
        cost_estimate=BRIEF,
    )(place, turned, head_t, twin, *halves, *parts)


def add_split_kernel(*refs):
    ins, outs = refs[:4], refs[4:]
    for d, out_ref in enumerate(outs):
        total = ins[0][d].astype(jnp.float32)
        for ref in ins[1:]:
            total += ref[d].astype(jnp.float32)
        out_ref[...] = total.astype(out_ref.dtype)


def add_split(*blocks):
    return pl.pallas_call(
        add_split_kernel,
        out_shape=[jax.ShapeDtypeStruct(blocks[0].shape[1:], blocks[0].dtype)] * 4,
        in_specs=[VMEM] * 4,
        out_specs=[VMEM] * 4,
        compiler_params=params(6),
        cost_estimate=BRIEF,
    )(*blocks)


def add_rows_kernel(place_ref, *refs):
    ins, outs, sum_ref = refs[:4], refs[4:8], refs[8]
    tok = place_ref[1]
    total = ins[0][...].astype(jnp.float32)
    for ref in ins[1:]:
        total += ref[...].astype(jnp.float32)
    sum_ref[...] = total.astype(sum_ref.dtype)
    block = outs[0].shape[0]
    for d, out_ref in enumerate(outs):
        out_ref[...] = sum_ref[pl.ds(pl.multiple_of((tok + d) % 4 * block, block), block), :]


def add_rows(place, blocks):
    toks, wide = blocks[0].shape
    return pl.pallas_call(
        add_rows_kernel,
        out_shape=[jax.ShapeDtypeStruct((toks // 4, wide), jnp.bfloat16)] * 4,
        in_specs=[SMEM] + [VMEM] * 4,
        out_specs=[VMEM] * 4,
        scratch_shapes=[pltpu.VMEM((toks, wide), jnp.bfloat16)],
        compiler_params=params(2),
        cost_estimate=BRIEF,
    )(place, *blocks)


def add_toks_kernel(place_ref, own_ref, *refs):
    ins, (keep_ref, give_ref) = refs[:4], refs[4:]
    even = place_ref[4] == 0
    first = jnp.where(even, ins[0][...].astype(jnp.float32), own_ref[...].astype(jnp.float32))
    total = first
    for ref in ins[1:]:
        total += ref[...].astype(jnp.float32)
    left, right = total[:, :128], total[:, 128:]
    keep_ref[...] = jnp.where(even, left, right).astype(keep_ref.dtype)
    give_ref[...] = jnp.where(even, right, left).astype(give_ref.dtype)


def add_toks(place, own, *received):
    rows, wide = own.shape
    return pl.pallas_call(
        add_toks_kernel,
        out_shape=[jax.ShapeDtypeStruct((rows, wide // 2), jnp.bfloat16)] * 2,
        in_specs=[SMEM] + [VMEM] * 5,
        out_specs=[VMEM] * 2,
        compiler_params=params(1),
        cost_estimate=BRIEF,
    )(place, own, *received)


def choose_kernel(place_ref, keep_ref, got_ref, out_ref):
    mine = place_ref[0] == place_ref[4]
    keep, got = keep_ref[...].astype(jnp.float32), got_ref[...].astype(jnp.float32)
    out_ref[...] = jnp.where(mine, keep, got).astype(out_ref.dtype)


def choose(place, keep, got):
    return pl.pallas_call(
        choose_kernel,
        out_shape=jax.ShapeDtypeStruct(keep.shape, keep.dtype),
        in_specs=[SMEM, VMEM, VMEM],
        out_specs=VMEM,
        compiler_params=params(1),
        cost_estimate=BRIEF,
    )(place, keep, got)


def head_grad_kernel(place_ref, grad_ref, own_ref, other_ref, sent_ref, twin_ref, out_ref):
    teacher = place_ref[0] == 0
    core = place_ref[4]

    def write(mine, others):
        for y in range(2):
            for ref, part in ((mine, core), (others, 1 - core)):
                columns = pl.ds(pl.multiple_of((y * 2 + part) * 256, 256), 256)
                out_ref[:, columns] = jnp.dot(
                    grad_ref[...], ref[0, :, 256 * y : 256 * y + 256], preferred_element_type=jnp.float32
                ).astype(jnp.bfloat16)

    @pl.when(teacher)
    def _():
        write(sent_ref, twin_ref)

    @pl.when(jnp.logical_not(teacher))
    def _():
        write(own_ref, other_ref)


def head_grad_half(place, grad, own, other, sent, twin):
    width, toks = grad.shape
    block = own.shape[2]
    second = pl.BlockSpec((1, toks, block // 2), lambda step, place: (2 + step // 2, 0, step % 2))
    first = pl.BlockSpec((1, toks, block // 2), lambda step, place: (step // 2, 0, step % 2))
    return pl.pallas_call(
        head_grad_kernel,
        grid_spec=pltpu.PrefetchScalarGridSpec(
            num_scalar_prefetch=1,
            grid=(4,),
            in_specs=[
                pl.BlockSpec((width, toks), lambda step, place: (0, 0)),
                second,
                second,
                first,
                first,
            ],
            out_specs=pl.BlockSpec((width, block), lambda step, place: (0, step)),
        ),
        out_shape=jax.ShapeDtypeStruct((width, 4 * block), jnp.bfloat16),
        compiler_params=params(8),
        cost_estimate=BRIEF,
    )(place, grad, own, other, sent, twin)


def spread(stats, name):
    far = send(stats, **{name: 2})
    near = send_by_core(stats, {name: 1}, {name: 3})
    return [stats, far, near, send(near, c=1)]


def on_device(hidden, head, token_ids, loss_mask):
    section, tok, vocab = (lax.axis_index(name) for name in AXES)
    place = jnp.stack([section, tok, vocab >> 3, (vocab >> 1) & 3, vocab & 1]).astype(jnp.int32)
    states = hidden[0]

    with jax.named_scope("gather_tok"):
        blocks = [states] + [send(states, t=d) for d in (1, 2, 3)]
    with jax.named_scope("gather_tok"):
        place, *blocks = lax.optimization_barrier((place, *blocks))
        block = jnp.stack(blocks)
    with jax.named_scope("gather_first"):
        blocks = [block] + [send_by_core(block, {"x": d}, {"y": d}) for d in (1, 2, 3)]
    with jax.named_scope("stage"):
        head_t, *halves = stage(place, head[0].T)
        head_t, *blocks = lax.optimization_barrier((head_t, *blocks))
        early = [send(half, c=1) for half in halves[:4]]
    with jax.named_scope("gather_first"):
        block = jnp.stack(blocks)
    with jax.named_scope("gather_second"):
        own = [block] + [send_by_core(block, {"y": d}, {"x": d}) for d in (1, 2, 3)]
    own[1], early, late = lax.optimization_barrier((own[1], early, halves[4:]))
    with jax.named_scope("stage"):
        late = [send(half, c=1) for half in late]
    with jax.named_scope("gather_cores"):
        other = [send(block, c=1) for block in own[:3]]
        own[3], *other = lax.optimization_barrier((own[3], *other))
        other.append(send(own[3], c=1))
    with jax.named_scope("student_hidden"):
        sent = send_both_ways(first_half(place, own))
    with jax.named_scope("own_logits"):
        hidden_own, part = own_logits(place, head_t, own)
        part, late = lax.optimization_barrier((part, late))
    with jax.named_scope("logits"):
        hidden_other, scaled, short, local = logits_parts(place, head_t, other, part)

    with jax.named_scope("stats"):
        stats = merge(local, send(local, c=1))
        stats, short = lax.optimization_barrier((stats, short))
    with jax.named_scope("exchange_scaled"):
        other_short = send(short, s=1)
    with jax.named_scope("stats"):
        stats = merge(*spread(stats, "x"))
        stats, sent = lax.optimization_barrier((stats, sent))
    with jax.named_scope("student_hidden"):
        twin = send(sent, c=1)
    with jax.named_scope("stats"):
        stats = merge(*spread(stats, "y"))
        own_stats = local_scale(local, *spread(stats, "t"))
        other_stats = send(own_stats, s=1)

    with jax.named_scope("logits_grad"):
        grad, turned = logits_grad(
            place, scaled, other_short, own_stats, other_stats, token_ids[None], loss_mask[None]
        )
    turned, twin = lax.optimization_barrier((turned, twin))
    sums, firsts = [], []
    with jax.named_scope("hidden_grad"):
        turned_twin = send(turned, c=1)
        part = own_products(place, turned, head_t, 1)
        part, turned_twin = lax.optimization_barrier((part, turned_twin))
        for d in (1, 2, 3, 0):
            parts = (part,) if d == 1 else ()
            if d == 0:
                grad, firsts[0] = lax.optimization_barrier((grad, firsts[0]))
                head_out = head_grad_half(place, grad, hidden_own, hidden_other, sent, twin)
                turned, firsts[1], head_out = lax.optimization_barrier((turned, firsts[1], head_out))
            sums.append(products(place, turned, head_t, turned_twin, (early + late)[2 * ((d + 3) % 4) :][:2], d, *parts))
            turned, sums[-1] = lax.optimization_barrier((turned, sums[-1]))
            if d > 0:
                firsts.append(send_by_core(sums[-1], {"x": d}, {"y": d}))
    with jax.named_scope("reduce_second"):
        parts = add_split(sums[3], *firsts)
        seconds = [send_by_core(parts[d], {"y": d}, {"x": d}) for d in (1, 2, 3)]
    with jax.named_scope("reduce_tok"):
        rows = add_rows(place, [parts[0]] + seconds)
        received = [send(rows[0], s=1)]
        received += [send_by_core(rows[d], {"s": 1, "t": d}, {"t": d}) for d in (1, 2, 3)]
        keep, give = add_toks(place, rows[0], *received)
    with jax.named_scope("hidden_out"):
        hidden_out = choose(place, keep, send(give, c=1))
    return head_out.T, hidden_out


def solution(mesh):
    in_specs = (P("section", "tok", "vocab"), P("section", None, ("tok", "vocab")), P(), P())
    out_specs = (P("section", ("tok", "vocab")), P("tok", ("section", "vocab")))
    return jax.shard_map(
        on_device, mesh=mesh, in_specs=in_specs, out_specs=out_specs, check_vma=False
    )
```
